256 devices in a mesh: dom: 32 (over x_hi, z, core), face: 8 (over y, x_lo).
Axes of the slice: x: 4 (x_hi: 2, x_lo: 2; x = x_hi * 2 + x_lo), y: 4, z: 8, core: 2. Of those that a mesh axis runs over, the one named last changes fastest.
Arguments:
- positions: float32 [3, 65536], P(None, ('dom', 'face')), may hold values from 0 to 3
- species: int32 [65536], P(('dom', 'face')), may hold values from 0 to 6
- send_list: int32 [256, 8, 64], P(('dom', 'face')), may hold values from 0 to 255
- edge_src: int32 [256, 1024], P(('dom', 'face')), may hold values from 0 to 255
- edge_dst: int32 [256, 1024], P(('dom', 'face')), may hold values from 0 to 767
- edge_count: int32 [256], P(('dom', 'face')), may hold values from 256 to 1024, as said below
- w_in: float32 [22, 128], replicated, may hold values from -1.25 to 1.25
- w_mid: float32 [128, 128], replicated, may hold values from -0.5 to 0.5
- w_pair: float32 [128, 128], replicated, may hold values from -0.5 to 0.5
- w_mix: float32 [320, 128], replicated, may hold values from -0.3125 to 0.3125
- w_back: float32 [128, 128], replicated, may hold values from -0.5 to 0.5
- w_read: float32 [128], replicated, may hold values from -0.5 to 0.5
Outputs:
- forces: float32 [3, 65536], P(None, ('dom', 'face'))
- energies: float32 [65536], P(('dom', 'face'))
The draws below stay inside these ranges and needn't reach their ends.
Inputs may be any that keep to these rules, and one draw needn't show every extreme that they name: The first edge_count[g] pairs of domain g are live and the rest are padding; some domain is full in every draw.
All inputs are finite; a program needn't handle non-finite values.
Results may differ from the reference program's by a relative error of at most 0.0003.
Values sent between devices are 32-bit elements; how exact they have to be, the bound alone decides.
A program may use at most 128 MiB of HBM per device.

```python
import jax
import jax.numpy as jnp
from jax import lax

CHANNELS = 64
WIDTH = 128
BASIS = 8
SPECIES = 7
ATOM_DEV = 256
GHOST = 64
PAIR_DEV = 1024
ATOMS = 65536
N_DOM = 32
N_FACE = 8
DEVICES = 256


def draw_edge_count(key, part):
    key = jax.random.fold_in(key, 11)
    counts_key, full_key = jax.random.split(key)
    counts = jax.random.randint(counts_key, (DEVICES,), PAIR_DEV // 4, PAIR_DEV + 1)
    fullest = jax.random.randint(full_key, (), 0, DEVICES)
    return jnp.where(jnp.arange(DEVICES) == fullest, PAIR_DEV, counts).astype(jnp.int32)


def touch_ends(drawn, own_key, least, high):
    shape = drawn.shape
    place = [jax.random.randint(jax.random.fold_in(own_key, axis), (), 0, shape[axis]) for axis in range(len(shape))]
    drawn = drawn.at[tuple(place)].set(least)
    longest = shape.index(max(shape))
    place[longest] = (place[longest] + 1) % shape[longest]
    return drawn.at[tuple(place)].set(high)


def block_scale(own_key, dims, cuts, smallest, largest):
    def one(dim, parts):
        heights = jax.random.uniform(jax.random.fold_in(jax.random.fold_in(own_key, 6), dim), (parts,), jnp.float32, smallest / len(cuts), largest / len(cuts))
        return jnp.repeat(jnp.exp(heights), dims[dim] // parts).reshape((-1,) + (1,) * (len(dims) - dim - 1))

    loudness = one(*cuts[0])
    for cut in cuts[1:]:
        loudness = loudness * one(*cut)
    return loudness


def bell_draw(stream_key, shape, width, bound, kind=jnp.bfloat16):
    result = jax.random.normal(stream_key, shape, jnp.float32) * width
    return jnp.minimum(jnp.maximum(result, -bound), bound).astype(kind)


def setup_inputs(seed: int = 0) -> dict:
    arg_keys = jax.random.split(jax.random.key(seed), 13)
    positions = jnp.clip(3.0 * jax.random.uniform(arg_keys[0], (3, ATOMS), jnp.float32) ** block_scale(arg_keys[0], (3, ATOMS), ((1, 256),), -0.2, 0.2), 0.0, 3.0)
    species = touch_ends(jax.random.randint(arg_keys[1], (ATOMS,), 0, SPECIES), jax.random.fold_in(arg_keys[1], 1), 0, SPECIES - 1).astype(jnp.int32)
    send_list = touch_ends(jax.random.randint(arg_keys[2], (DEVICES, 8, GHOST), 0, ATOM_DEV), jax.random.fold_in(arg_keys[2], 1), 0, ATOM_DEV - 1).astype(jnp.int32)
    edge_src = touch_ends(jax.random.randint(arg_keys[3], (DEVICES, PAIR_DEV), 0, ATOM_DEV), jax.random.fold_in(arg_keys[3], 1), 0, ATOM_DEV - 1).astype(jnp.int32)
    edge_dst = touch_ends(jax.random.randint(arg_keys[4], (DEVICES, PAIR_DEV), 0, ATOM_DEV + 8 * GHOST), jax.random.fold_in(arg_keys[4], 1), 0, (ATOM_DEV + 8 * GHOST) - 1).astype(jnp.int32)
    edge_count = draw_edge_count(jax.random.fold_in(arg_keys[12], 71), 0)
    w_in = bell_draw(arg_keys[6], (2 * SPECIES + BASIS, WIDTH), (2 * SPECIES + BASIS) ** -0.5, 1.25, jnp.float32)
    w_mid = bell_draw(arg_keys[7], (WIDTH, WIDTH), WIDTH ** -0.5, 0.5, jnp.float32)
    w_pair = bell_draw(arg_keys[8], (WIDTH, 2 * CHANNELS), WIDTH ** -0.5, 0.5, jnp.float32)
    w_mix = bell_draw(arg_keys[9], (WIDTH + 3 * CHANNELS, WIDTH), (WIDTH + 3 * CHANNELS) ** -0.5, 0.3125, jnp.float32)
    w_back = bell_draw(arg_keys[10], (WIDTH, WIDTH), WIDTH ** -0.5, 0.5, jnp.float32)
    w_read = bell_draw(arg_keys[11], (WIDTH,), WIDTH ** -0.5, 0.5, jnp.float32)
    return {"positions": positions, "species": species, "send_list": send_list, "edge_src": edge_src, "edge_dst": edge_dst, "edge_count": edge_count, "w_in": w_in, "w_mid": w_mid, "w_pair": w_pair, "w_mix": w_mix, "w_back": w_back, "w_read": w_read}


ENV_SCALE = 0.2
CUTOFF = 6.0
DIRECTIONS = [(-1, -1), (-1, 0), (-1, 1), (0, -1), (0, 1), (1, -1), (1, 0), (1, 1)]

def product_of(left, right):
    return jnp.dot(left, right, precision=lax.Precision.HIGHEST, preferred_element_type=jnp.float32)

def harmonics(direction):
    comp_x = direction[:, 0]
    comp_y = direction[:, 1]
    comp_z = direction[:, 2]
    root3 = 3.0 ** 0.5
    root5 = 5.0 ** 0.5
    root15 = 15.0 ** 0.5
    return jnp.stack([jnp.ones_like(comp_x), root3 * comp_x, root3 * comp_y, root3 * comp_z, root15 * comp_x * comp_y, root15 * comp_y * comp_z, 0.5 * root5 * (2.0 * comp_z * comp_z - comp_x * comp_x - comp_y * comp_y), root15 * comp_x * comp_z, 0.5 * root15 * (comp_x * comp_x - comp_y * comp_y)], axis=1)

def pair_features(pos_centre, pos_partner, spec_centre, spec_partner, is_live, w_in, w_mid, w_pair):
    displace = pos_partner - pos_centre
    soft_len = jnp.sqrt(lax.optimization_barrier(jnp.sum(displace * displace, axis=1)) + 1.0)
    direction = displace / soft_len[:, None]
    orders = jnp.arange(1, BASIS + 1).astype(jnp.float32)
    radial = jnp.sin(jnp.pi * orders[None, :] * soft_len[:, None] / CUTOFF) / soft_len[:, None]
    scaled = soft_len / CUTOFF
    envelope = is_live * (1.0 - scaled * scaled) ** 2
    kinds = jnp.arange(SPECIES).astype(jnp.int32)
    hot_centre = (spec_centre[:, None] == kinds[None, :]).astype(jnp.float32)
    hot_partner = (spec_partner[:, None] == kinds[None, :]).astype(jnp.float32)
    inputs = jnp.concatenate([hot_centre, hot_partner, radial], axis=1)
    latent = product_of(jax.nn.silu(product_of(inputs, w_in)), w_mid)
    paired = product_of(latent, w_pair)
    return (latent, paired, harmonics(direction), envelope)

def env_terms(paired, angular, envelope):
    weights = paired[:, :CHANNELS] * envelope[:, None]
    return (weights[:, :, None] * angular[:, None, :]).reshape(-1, CHANNELS * 9) * ENV_SCALE

def edge_energy(latent, paired, angular, envelope, env_rows, w_mix, w_back, w_read):
    values = paired[:, CHANNELS:]
    env_blocks = env_rows.reshape(-1, CHANNELS, 9)
    product = env_blocks * angular[:, None, :]
    invariant = jnp.stack([product[:, :, 0], lax.optimization_barrier(jnp.sum(product[:, :, 1:4], axis=2)), lax.optimization_barrier(jnp.sum(product[:, :, 4:9], axis=2))], axis=2) * values[:, :, None]
    mixed_in = jnp.concatenate([latent, invariant.reshape(-1, 3 * CHANNELS)], axis=1)
    updated = latent + product_of(jax.nn.silu(product_of(mixed_in, w_mix)), w_back)
    return envelope * product_of(updated, w_read)

def reference(positions, species, send_list, edge_src, edge_dst, edge_count, w_in, w_mid, w_pair, w_mix, w_back, w_read):
    n_devices = N_DOM * N_FACE
    pos_all = positions.T
    device = jnp.arange(n_devices).astype(jnp.int32)
    dom_of = device // N_FACE
    face_of = device % N_FACE
    pieces = [device[:, None] * ATOM_DEV + jnp.arange(ATOM_DEV).astype(jnp.int32)[None, :]]
    for which in range(8):
        shift_a, shift_b = DIRECTIONS[which]
        neighbour = (dom_of + shift_a) % N_DOM * N_FACE + (face_of + shift_b) % N_FACE
        pieces.append(neighbour[:, None] * ATOM_DEV + send_list[neighbour, 7 - which])
    slot_table = jnp.concatenate(pieces, axis=1)
    first = jnp.take_along_axis(slot_table, edge_src, axis=1)
    second = jnp.take_along_axis(slot_table, edge_dst, axis=1)
    centre = jnp.concatenate([first, second], axis=1)
    partner = jnp.concatenate([second, first], axis=1)
    is_live = (jnp.arange(PAIR_DEV)[None, :] < edge_count[:, None]).astype(jnp.float32)
    alive_both = jnp.concatenate([is_live, is_live], axis=1)

    def features(pos_c, pos_p, cidx, pidx, alive):
        return pair_features(pos_c, pos_p, species[cidx], species[pidx], alive, w_in, w_mid, w_pair)

    def first_pass(environ, block):
        cidx, pidx, alive = block
        latent, paired, angular, envelope = features(pos_all[cidx], pos_all[pidx], cidx, pidx, alive)
        return (environ.at[cidx].add(env_terms(paired, angular, envelope)), None)
    environ, _ = lax.scan(first_pass, jnp.zeros((ATOMS, CHANNELS * 9), jnp.float32), (centre, partner, alive_both))

    def second_pass(carry, block):
        energies, g_environ, gradient = carry
        cidx, pidx, alive = block
        feats, pull = jax.vjp(lambda a, b: features(a, b, cidx, pidx, alive), pos_all[cidx], pos_all[pidx])
        latent, paired, angular, envelope = feats
        energy, energy_pull = jax.vjp(lambda l, p, y, e, r: edge_energy(l, p, y, e, r, w_mix, w_back, w_read), latent, paired, angular, envelope, environ[cidx])
        g_lat, g_pair, g_ang, g_env, g_rows = energy_pull(jnp.ones_like(energy))
        g_centre, g_partner = pull((g_lat, g_pair, g_ang, g_env))
        energies = energies.at[cidx].add(energy)
        g_environ = g_environ.at[cidx].add(g_rows)
        gradient = gradient.at[cidx].add(g_centre).at[pidx].add(g_partner)
        return ((energies, g_environ, gradient), None)
    start = (jnp.zeros((ATOMS,), jnp.float32), jnp.zeros((ATOMS, CHANNELS * 9), jnp.float32), jnp.zeros((ATOMS, 3), jnp.float32))
    (energies, g_environ, gradient), _ = lax.scan(second_pass, start, (centre, partner, alive_both))

    def third_pass(gradient, block):
        cidx, pidx, alive = block
        feats, pull = jax.vjp(lambda a, b: features(a, b, cidx, pidx, alive), pos_all[cidx], pos_all[pidx])
        latent, paired, angular, envelope = feats
        _, term_pull = jax.vjp(env_terms, paired, angular, envelope)
        g_pair, g_ang, g_env = term_pull(g_environ[cidx])
        g_centre, g_partner = pull((jnp.zeros_like(latent), g_pair, g_ang, g_env))
        return (gradient.at[cidx].add(g_centre).at[pidx].add(g_partner), None)
    gradient, _ = lax.scan(third_pass, gradient, (centre, partner, alive_both))
    return ((-gradient).T, energies)
```

```python
import functools

import jax
import jax.numpy as jnp
from jax import lax
from jax.experimental import pallas as pl
from jax.experimental.pallas import tpu as pltpu
from jax.sharding import PartitionSpec as P

CH = 64
WIDTH = 128
BASIS = 8
SPECIES = 7
ENV_SCALE = 0.2
CUTOFF = 6.0
PI = 3.141592653589793
DIRECTIONS = ((-1, -1), (-1, 0), (-1, 1), (0, -1), (0, 1), (1, -1), (1, 0), (1, 1))
NBR = 8
ATOM = 256
GHOST = 64
PAIR = 1024
SLOTS = NBR * GHOST
LIST = PAIR + 128
CAP = 10 * PAIR
EB = 512
F32 = jnp.float32
BF16 = jnp.bfloat16
I32 = jnp.int32
MESH = pl.DeviceIdType.MESH
VMEM = pl.BlockSpec(memory_space=pltpu.VMEM)
SMEM = pl.BlockSpec(memory_space=pltpu.SMEM)
ANY = pl.BlockSpec(memory_space=pl.ANY)

RAD, DRAD, ANG, ENVL, DENVL, RINV, DIR, ERAW, DANG, ROWS = 0, 8, 16, 25, 26, 27, 28, 31, 32, 40


def dot(a, b):
    return lax.dot_general(a, b, (((1,), (0,)), ((), ())), preferred_element_type=F32)


def dot_nt(a, b):
    return lax.dot_general(a, b, (((1,), (1,)), ((), ())), preferred_element_type=F32)


def exact(a, b):
    return jnp.dot(a, b, precision=lax.Precision.HIGHEST, preferred_element_type=F32)


def halves(x):
    high = x.astype(BF16)
    return high, (x - high.astype(F32)).astype(BF16)


def thirds(x):
    high = x.astype(BF16).astype(F32)
    rest = x - high
    mid = rest.astype(BF16).astype(F32)
    return high, mid, rest - mid


def one_hot(row, count):
    rows = lax.broadcasted_iota(I32, (count, row.shape[1]), 0)
    return jnp.where(rows == row, 1.0, 0.0).astype(BF16)


def atom_table(coords, kinds):
    parts = thirds(coords)
    pad = jnp.zeros((6, coords.shape[1]), F32)
    return jnp.concatenate([*parts, kinds, pad], axis=0)


def joined(rows):
    return rows[0:3] + rows[3:6] + rows[6:9]


def greet():
    here = [lax.axis_index("dom"), lax.axis_index("face")]
    sizes = [lax.axis_size("dom"), lax.axis_size("face")]
    peers = []
    for shift in DIRECTIONS:
        peers.append(
            tuple(lax.rem(at + by + size, size) for at, by, size in zip(here, shift, sizes))
        )
    barrier = pltpu.get_barrier_semaphore()
    for peer in peers:
        pl.semaphore_signal(barrier, inc=1, device_id=peer, device_id_type=MESH)
    return barrier, peers


def swap(peers, out_ref, in_ref, send_sem, recv_sem):
    copies = []
    for k, peer in enumerate(peers):
        copies.append(
            pltpu.make_async_remote_copy(
                src_ref=out_ref.at[k],
                dst_ref=in_ref.at[NBR - 1 - k],
                send_sem=send_sem.at[k],
                recv_sem=recv_sem.at[NBR - 1 - k],
                device_id=peer,
                device_id_type=MESH,
            )
        )
    for copy in copies:
        copy.start()
    return copies


def share_kernel(
    count_ref, pos_ref, spec_ref, send_ref, src_ref, dst_ref,
    w_in_ref, w_mid_ref, w_pair_ref, w_mix_ref, w_back_ref, w_read_ref,
    own_ref, table_ref, recv_ref, wx_ref, up_ref, upl_ref, dn_ref, dnl_ref,
    mt_ref, mtl_ref, mb_ref, mbl_ref, wr_ref, wrl_ref, ab_ref,
    out_buf, order_buf, send_sem, recv_sem,
):
    barrier, peers = greet()
    table = atom_table(pos_ref[...], spec_ref[...].astype(F32)).astype(BF16)
    table_ref[...] = table
    sends = jnp.concatenate([send_ref[k : k + 1, :] for k in range(NBR)], axis=1)
    ghosts = dot(table, one_hot(sends, ATOM))
    ghost_rows = jnp.concatenate([joined(ghosts), ghosts[9:10]], axis=0)
    src = src_ref[...]
    dst = dst_ref[...]
    lanes = lax.broadcasted_iota(I32, (1, PAIR), 1)
    live = lanes < count_ref[0]
    ghost = dst >= ATOM
    away = dst - ATOM
    bucket = jnp.where(ghost, (away >> 6) + 1, 0)
    bucket = jnp.where(live, bucket, 15)
    place = jnp.where(ghost, away & 63, dst)
    member = jnp.where(lax.broadcasted_iota(I32, (16, PAIR), 0) == bucket, 1.0, 0.0)
    before = lax.broadcasted_iota(I32, (ATOM, ATOM), 0) < lax.broadcasted_iota(I32, (ATOM, ATOM), 1)
    before = jnp.where(before, 1.0, 0.0).astype(BF16)
    pieces = [member[:, i * ATOM : (i + 1) * ATOM] for i in range(PAIR // ATOM)]
    ranks = dot(jnp.concatenate(pieces, axis=0).astype(BF16), before)
    sums = [jnp.sum(piece, axis=1, keepdims=True) for piece in pieces]
    total = sums[0] + sums[1] + sums[2] + sums[3]
    start = jnp.zeros((16, 1), F32)
    index = lax.broadcasted_iota(I32, (16, 1), 0)
    for b in range(NBR + 1):
        start = start + jnp.where(index > b, total[b : b + 1, :], 0.0)
    offset = start
    spots = []
    for i, piece in enumerate(pieces):
        where = ranks[16 * i : 16 * (i + 1)] + offset
        spots.append(jnp.sum(piece * where, axis=0, keepdims=True))
        offset = offset + sums[i]
    spot = jnp.concatenate(spots, axis=1)
    spot = jnp.where(live, spot, -1.0).astype(I32)
    picked = dot(table, one_hot(src, ATOM))
    data = jnp.concatenate(
        [picked[0:10], place.astype(F32), src.astype(F32), jnp.zeros((4, PAIR), F32)], axis=0
    ).astype(BF16)
    for i in range(PAIR // ATOM):
        rows = lax.broadcasted_iota(I32, (ATOM, PAIR), 0) + i * ATOM
        chosen = jnp.where(rows == spot, 1.0, 0.0).astype(BF16)
        order_buf[:, i * ATOM : (i + 1) * ATOM] = dot_nt(data, chosen)
    ordered = order_buf[...]
    entries = jnp.concatenate(
        [joined(ordered), ordered[9:12], jnp.zeros((2, PAIR), F32)], axis=0
    )
    none = jnp.zeros((8, GHOST), F32)
    for k in range(NBR):
        out_buf[k, :, 0:PAIR] = entries
        mine = jnp.concatenate([ghost_rows[:, k * GHOST : (k + 1) * GHOST], none[0:4]], axis=0)
        out_buf[k, :, PAIR:LIST] = jnp.concatenate([mine, none], axis=1)
        out_buf[k, 4:5, PAIR:LIST] = jnp.broadcast_to(total[k + 1 : k + 2, :], (1, 128))
        out_buf[k, 5:6, PAIR:LIST] = jnp.broadcast_to(start[k + 1 : k + 2, :], (1, 128))
    pl.semaphore_wait(barrier, NBR)
    copies = swap(peers, out_buf, recv_ref, send_sem, recv_sem)
    own_ref[:, 0:PAIR] = entries
    own_ref[:, PAIR:LIST] = jnp.zeros((8, 128), F32)
    own_ref[4:5, PAIR:LIST] = jnp.broadcast_to(total[0:1, :], (1, 128))
    w_in = w_in_ref[...]
    w_c = w_in[0:SPECIES].T
    w_p = w_in[SPECIES : 2 * SPECIES].T
    w_r = w_in[2 * SPECIES :]
    gap = jnp.zeros((WIDTH, 1), F32)
    first = jnp.concatenate([w_c, gap, w_p, gap, w_r.T], axis=1)
    first_high = first.astype(BF16).astype(F32)
    first_low = first - first_high
    wx_ref[...] = jnp.concatenate(
        [first_high, first_high[:, 16:24], first_low, jnp.zeros((WIDTH, 8), F32)], axis=1
    ).astype(BF16)
    wr_high, wr_low = halves(jnp.concatenate([w_r, jnp.zeros((8, WIDTH), F32)], axis=0))
    wr_ref[...] = jnp.concatenate([wr_high, wr_high], axis=1)
    wrl_ref[...] = wr_low
    w_mid = w_mid_ref[...]
    w_read = w_read_ref[...]
    down = jnp.concatenate(
        [exact(w_mid, w_pair_ref[...]), exact(w_mid, w_mix_ref[0:WIDTH, :])], axis=1
    )
    a_col = jnp.sum(w_mid * w_read, axis=1, keepdims=True)
    b_col = jnp.sum(w_back_ref[...] * w_read, axis=1, keepdims=True)
    ab_ref[...] = jnp.concatenate([a_col, b_col], axis=1)
    dn_high, dn_low = halves(down)
    dn_ref[...] = dn_high
    dnl_ref[...] = dn_low
    up = down.T
    up_high, up_low = halves(up)
    up_ref[...] = jnp.concatenate([up_high, up_high], axis=1)
    upl_ref[...] = up_low
    mix = jnp.concatenate(
        [w_mix_ref[pl.ds(WIDTH + degree, CH, stride=3), :] for degree in range(3)], axis=0
    )
    mb_ref[...], mbl_ref[...] = halves(mix)
    mt_ref[...], mtl_ref[...] = halves(mix.T)
    for copy in copies:
        copy.wait()


def edge_kernel(
    count_ref, src_ref, dst_ref, send_ref, own_ref, table_ref, recv_ref,
    wx_ref, up_ref, upl_ref, dn_ref, dnl_ref, mt_ref, mtl_ref, mb_ref, mbl_ref,
    wr_ref, wrl_ref, ab_ref,
    msg_ref, force_ref, energy_ref,
    edges, hots, paired, slope, mixed, mixed_low, d_value, geo, env, g_env,
    env_high, env_low, g_high, g_low, at_centre, at_partner,
):
    count = count_ref[0]
    src = src_ref[...]
    dst = dst_ref[...]
    near = jnp.concatenate([recv_ref[k, 0:4, PAIR : PAIR + GHOST] for k in range(NBR)], axis=1)
    ghosts = atom_table(near[0:3], near[3:4]).astype(BF16)
    table = table_ref[...]
    segments = jnp.concatenate([table, ghosts[:, 0:ATOM], ghosts[:, ATOM:SLOTS]], axis=0)
    found = dot(segments, one_hot(dst & 255, ATOM))
    part = dst >> 8
    picked = jnp.where(part == 0, found[0:16], jnp.where(part == 1, found[16:32], found[32:48]))
    edges[:, 0:PAIR] = jnp.concatenate(
        [joined(picked), picked[9:10], src.astype(F32), dst.astype(F32), jnp.zeros((2, PAIR), F32)],
        axis=0,
    )
    lane = lax.broadcasted_iota(I32, (8, 128), 1)
    row = lax.broadcasted_iota(I32, (8, 128), 0)

    def place(ref, size, begin, at, extra, tile):
        base = tile * 128 - at + begin
        first = base >> 7
        turn = base & 127
        low = jnp.clip(first, 0, 8)
        high = jnp.clip(first + 1, 0, 8)
        left = ref[:, pl.ds(pl.multiple_of(low * 128, 128), 128)]
        right = ref[:, pl.ds(pl.multiple_of(high * 128, 128), 128)]
        back = lax.rem(128 - turn, 128)
        taken = jnp.where(
            lane < 128 - turn, pltpu.roll(left, back, 1), pltpu.roll(right, back, 1)
        )
        here = pl.ds(pl.multiple_of(tile * 128, 128), 128)
        spot = tile * 128 + lane
        inside = (spot >= at) & (spot < at + size)
        edges[:, here] = jnp.where(inside, taken + extra, edges[:, here])

    def scalar(ref, which):
        return ref[which : which + 1, PAIR : PAIR + 128][0, 0].astype(I32)

    at = count
    jobs = []
    size = scalar(own_ref, 4)
    jobs.append((own_ref, size, 0, at, jnp.zeros((8, 128), F32), 4))
    at = at + size
    for k in range(NBR):
        ref = recv_ref.at[k]
        size = scalar(ref, 4)
        extra = jnp.where(row == 4, F32(ATOM + GHOST * k), 0.0)
        extra = jnp.where(row == 5, F32(ATOM * (3 + k)), extra)
        jobs.append((ref, size, scalar(ref, 5), at, extra, 2))
        at = at + size
    total = at
    for ref, size, begin, at, extra, usual in jobs:
        for step in range(usual):
            place(ref, size, begin, at, extra, (at >> 7) + step)
    for ref, size, begin, at, extra, usual in jobs:
        last = (at + size + 127) >> 7

        def more(tile, carry, ref=ref, size=size, begin=begin, at=at, extra=extra):
            place(ref, size, begin, at, extra, tile)
            return carry

        lax.fori_loop((at >> 7) + usual, last, more, 0)
    blocks = lax.div(total + EB - 1, EB)

    env[...] = jnp.zeros_like(env)
    g_env[...] = jnp.zeros_like(g_env)
    at_centre[...] = jnp.zeros_like(at_centre)
    at_partner[...] = jnp.zeros_like(at_partner)
    root3, root5, root15 = 3.0**0.5, 5.0**0.5, 15.0**0.5
    sends = jnp.concatenate([send_ref[k : k + 1, :] for k in range(NBR)], axis=1).astype(F32)
    own_index = lax.broadcasted_iota(I32, (1, ATOM), 1).astype(F32)
    codes = jnp.concatenate(
        [own_index, sends[:, 0:ATOM], sends[:, ATOM:SLOTS], jnp.zeros((13, ATOM), F32)], axis=0
    ).astype(BF16)

    def first_pass(block, carry):
        begin = pl.multiple_of(block * EB, EB)
        here = pl.ds(begin, EB)
        valid = begin + lax.broadcasted_iota(I32, (1, EB), 1) < total
        part = jnp.where(valid, edges[:, here], 0.0)
        code = part[4:5].astype(I32)
        seek = dot(codes, one_hot(code & 255, ATOM))
        kind = code >> 8
        centre = jnp.where(kind == 0, seek[0:1], jnp.where(kind == 1, seek[1:2], seek[2:3]))
        hot = one_hot(centre.astype(I32), ATOM)
        hots[:, here] = hot
        held = dot(table, hot)
        delta = part[0:3] - joined(held)
        length2 = delta[0:1] * delta[0:1] + delta[1:2] * delta[1:2] + delta[2:3] * delta[2:3] + 1.0
        soft = jnp.sqrt(length2)
        rinv = 1.0 / soft
        unit = delta * rinv
        ux, uy, uz = unit[0:1], unit[1:2], unit[2:3]
        turn = soft * (PI / CUTOFF) - PI / 2
        t2 = turn * turn
        cosine = -turn * (
            1 + t2 * (-1 / 6 + t2 * (1 / 120 + t2 * (-1 / 5040 + t2 * (1 / 362880 - t2 / 39916800))))
        )
        sine = 1 + t2 * (
            -1 / 2 + t2 * (1 / 24 + t2 * (-1 / 720 + t2 * (1 / 40320 + t2 * (-1 / 3628800 + t2 / 479001600))))
        )
        twice = 2 * cosine
        s_old, s_now = jnp.zeros_like(sine), sine
        c_old, c_now = jnp.ones_like(sine), cosine
        for b in range(BASIS):
            geo[RAD + b : RAD + b + 1, here] = s_now * rinv
            geo[DRAD + b : DRAD + b + 1, here] = (c_now * ((b + 1) * PI / CUTOFF) - s_now * rinv) * rinv
            s_old, s_now = s_now, twice * s_now - s_old
            c_old, c_now = c_now, twice * c_now - c_old
        angular = [
            jnp.ones_like(ux),
            root3 * ux,
            root3 * uy,
            root3 * uz,
            root15 * ux * uy,
            root15 * uy * uz,
            0.5 * root5 * (2.0 * uz * uz - ux * ux - uy * uy),
            root15 * ux * uz,
            0.5 * root15 * (ux * ux - uy * uy),
        ]
        for m in range(9):
            geo[ANG + m : ANG + m + 1, here] = angular[m]
        inner = 1.0 - length2 * (1.0 / (CUTOFF * CUTOFF))
        alive = jnp.where(valid, 1.0, 0.0)
        envelope = alive * inner * inner
        geo[ENVL : ENVL + 1, here] = envelope
        geo[DENVL : DENVL + 1, here] = alive * inner * soft * (-4.0 / (CUTOFF * CUTOFF))
        geo[RINV : RINV + 1, here] = rinv
        geo[DIR : DIR + 3, here] = unit
        radial = geo[RAD : RAD + 8, here]
        radial_low = radial - radial.astype(BF16).astype(F32)
        kinds = lax.broadcasted_iota(I32, (8, EB), 0)
        hot_c = jnp.where(kinds == held[9:10].astype(I32), 1.0, 0.0)
        hot_p = jnp.where(kinds == part[3:4].astype(I32), 1.0, 0.0)
        inputs = jnp.concatenate(
            [hot_c, hot_p, radial, radial_low, hot_c, hot_p, radial, jnp.zeros((8, EB), F32)], axis=0
        ).astype(BF16)
        pre = dot(wx_ref[...], inputs)
        gate = 1.0 / (1.0 + jnp.exp(-pre))
        act = pre * gate
        slope[:, here] = gate + act * (1.0 - gate)
        act_high, act_low = halves(act)
        after = dot(up_ref[...], jnp.concatenate([act_high, act_low], axis=0)) + dot(
            upl_ref[...], act_high
        )
        paired[:, here] = after
        geo[ERAW : ERAW + 1, here] = jnp.sum(act * ab_ref[:, 0:1], axis=0, keepdims=True)
        weights = after[0:CH] * envelope
        for m in range(9):
            term = weights if m == 0 else weights * angular[m]
            high, low = halves(term)
            rows = slice(m * CH, (m + 1) * CH)
            env[rows, :] += dot_nt(high, hot) + dot_nt(low, hot)
        return carry

    lax.fori_loop(0, blocks, first_pass, 0)
    env_high[...], env_low[...] = halves(env[...] * ENV_SCALE)
    degrees = (0, 1, 1, 1, 2, 2, 2, 2, 2)

    def second_pass(block, carry):
        here = pl.ds(pl.multiple_of(block * EB, EB), EB)
        hot = hots[:, here]
        angular = [geo[ANG + m : ANG + m + 1, here] for m in range(9)]
        envelope = geo[ENVL : ENVL + 1, here]
        around = []
        sums = [None, None, None]
        for m in range(9):
            rows = slice(m * CH, (m + 1) * CH)
            got = dot(env_high[rows, :], hot) + dot(env_low[rows, :], hot)
            around.append(got)
            term = got if m == 0 else got * angular[m]
            degree = degrees[m]
            sums[degree] = term if sums[degree] is None else sums[degree] + term
        value = paired[CH : 2 * CH, here]
        invariant = jnp.concatenate([s * value for s in sums], axis=0)
        high, low = halves(invariant)
        mt = mt_ref[...]
        pre = paired[2 * CH :, here] + dot(mt, high) + dot(mt, low) + dot(mtl_ref[...], high)
        gate = 1.0 / (1.0 + jnp.exp(-pre))
        act = pre * gate
        back = ab_ref[:, 1:2]
        geo[ERAW : ERAW + 1, here] += jnp.sum(act * back, axis=0, keepdims=True)
        d_pre = (gate + act * (1.0 - gate)) * back * envelope
        d_high, d_low = halves(d_pre)
        mixed[:, here] = d_high
        mixed_low[:, here] = d_low
        mb = mb_ref[...]
        d_inv = dot(mb, d_high) + dot(mb, d_low) + dot(mbl_ref[...], d_high)
        d_inv = [d_inv[i * CH : (i + 1) * CH] for i in range(3)]
        d_value[:, here] = d_inv[0] * sums[0] + d_inv[1] * sums[1] + d_inv[2] * sums[2]
        d_sum = [d * value for d in d_inv]
        for m in range(9):
            share = d_sum[degrees[m]]
            term = share if m == 0 else share * angular[m]
            high, low = halves(term)
            rows = slice(m * CH, (m + 1) * CH)
            g_env[rows, :] += dot_nt(high, hot) + dot_nt(low, hot)
            if m:
                geo[DANG + m - 1 : DANG + m, here] = jnp.sum(share * around[m], axis=0, keepdims=True)
        return carry

    lax.fori_loop(0, blocks, second_pass, 0)
    g_high[...], g_low[...] = halves(g_env[...] * ENV_SCALE)

    def third_pass(block, carry):
        here = pl.ds(pl.multiple_of(block * EB, EB), EB)
        hot = hots[:, here]
        angular = [geo[ANG + m : ANG + m + 1, here] for m in range(9)]
        envelope = geo[ENVL : ENVL + 1, here]
        raw = paired[0:CH, here]
        weights = raw * envelope
        d_weight = None
        d_ang = [None]
        for m in range(9):
            rows = slice(m * CH, (m + 1) * CH)
            got = dot(g_high[rows, :], hot) + dot(g_low[rows, :], hot)
            term = got if m == 0 else got * angular[m]
            d_weight = term if m == 0 else d_weight + term
            if m:
                d_ang.append(
                    geo[DANG + m - 1 : DANG + m, here] + jnp.sum(weights * got, axis=0, keepdims=True)
                )
        e_raw = geo[ERAW : ERAW + 1, here]
        d_envelope = e_raw + jnp.sum(d_weight * raw, axis=0, keepdims=True)
        pair_high, pair_low = halves(
            jnp.concatenate([d_weight * envelope, d_value[:, here]], axis=0)
        )
        both_high = jnp.concatenate([pair_high, mixed[:, here]], axis=0)
        both_low = jnp.concatenate([pair_low, mixed_low[:, here]], axis=0)
        dn = dn_ref[...]
        d_act = dot(dn, both_high) + dot(dn, both_low) + dot(dnl_ref[...], both_high)
        d_act = d_act + ab_ref[:, 0:1] * envelope
        d_pre_high, d_pre_low = halves(d_act * slope[:, here])
        d_radial = dot(wr_ref[...], jnp.concatenate([d_pre_high, d_pre_low], axis=0)) + dot(
            wrl_ref[...], d_pre_high
        )
        d_soft = jnp.sum(d_radial[0:8] * geo[DRAD : DRAD + 8, here], axis=0, keepdims=True)
        d_soft = d_soft + d_envelope * geo[DENVL : DENVL + 1, here]
        unit = geo[DIR : DIR + 3, here]
        rinv = geo[RINV : RINV + 1, here]
        ux, uy, uz = unit[0:1], unit[1:2], unit[2:3]
        d_ux = root3 * d_ang[1] + root15 * (uy * d_ang[4] + uz * d_ang[7] + ux * d_ang[8]) - root5 * ux * d_ang[6]
        d_uy = root3 * d_ang[2] + root15 * (ux * d_ang[4] + uz * d_ang[5] - uy * d_ang[8]) - root5 * uy * d_ang[6]
        d_uz = root3 * d_ang[3] + root15 * (uy * d_ang[5] + ux * d_ang[7]) + 2.0 * root5 * uz * d_ang[6]
        along = d_soft - (d_ux * ux + d_uy * uy + d_uz * uz) * rinv
        pull = [d * rinv + u * along for d, u in ((d_ux, ux), (d_uy, uy), (d_uz, uz))]
        energy = e_raw * envelope
        sent = jnp.concatenate([*pull, energy, jnp.zeros((4, EB), F32)], axis=0)
        sent = jnp.concatenate([sent, sent - sent.astype(BF16).astype(F32)], axis=0).astype(BF16)
        at_centre[...] += dot_nt(sent, hot)
        code = jnp.where(
            begin_valid(block, total), edges[5:6, here], 0.0
        ).astype(I32)
        seg = lax.broadcasted_iota(I32, (16, EB), 0) == (code >> 8)
        spread = jnp.concatenate([jnp.where(seg, g, 0.0) for g in pull], axis=0)
        high, low = halves(spread)
        hot_partner = one_hot(code & 255, ATOM)
        at_partner[...] += dot_nt(high, hot_partner) + dot_nt(low, hot_partner)
        return carry

    lax.fori_loop(0, blocks, third_pass, 0)
    sums = at_centre[...]
    sums = sums[0:8] + sums[8:16]
    parts = at_partner[...]
    mine = [parts[16 * i : 16 * i + 1] for i in range(3)]
    force_ref[...] = sums[0:3] - jnp.concatenate(mine, axis=0)
    energy_ref[...] = sums[3:4]
    msg_ref[...] = jnp.zeros_like(msg_ref)
    for k in range(NBR):
        for i in range(3):
            msg_ref[k, i : i + 1, :] = parts[16 * i + 3 + k : 16 * i + 4 + k]
            ghost = parts[16 * i + 1 + k // 4 : 16 * i + 2 + k // 4]
            msg_ref[k, 3 + i : 4 + i, 0:GHOST] = ghost[:, (k % 4) * GHOST : (k % 4 + 1) * GHOST]


def begin_valid(block, total):
    return block * EB + lax.broadcasted_iota(I32, (1, EB), 1) < total


def return_kernel(msg_ref, force_ref, send_ref, out_ref, inbox, send_sem, recv_sem):
    barrier, peers = greet()
    sends = jnp.concatenate([send_ref[k : k + 1, :] for k in range(NBR)], axis=1)
    hot = one_hot(sends, ATOM)
    pl.semaphore_wait(barrier, NBR)
    copies = swap(peers, msg_ref, inbox, send_sem, recv_sem)
    for copy in copies:
        copy.wait()
    total = force_ref[...]
    for k in range(NBR):
        total = total - inbox[k, 0:3, :]
    ghosts = jnp.concatenate([inbox[k, 3:6, 0:GHOST] for k in range(NBR)], axis=1)
    split = jnp.concatenate([*thirds(ghosts), jnp.zeros((7, SLOTS), F32)], axis=0).astype(BF16)
    back = dot_nt(split, hot)
    out_ref[...] = total - joined(back)


def per_device(
    positions, species, send_list, edge_src, edge_dst, edge_count,
    w_in, w_mid, w_pair, w_mix, w_back, w_read,
):
    sends = send_list[0]
    shape = jax.ShapeDtypeStruct
    shared = pl.pallas_call(
        share_kernel,
        out_shape=(
            shape((8, LIST), F32),
            shape((16, ATOM), BF16),
            shape((NBR, 8, LIST), F32),
            shape((WIDTH, 64), BF16),
            shape((2 * WIDTH, 2 * WIDTH), BF16),
            shape((2 * WIDTH, WIDTH), BF16),
            shape((WIDTH, 2 * WIDTH), BF16),
            shape((WIDTH, 2 * WIDTH), BF16),
            shape((WIDTH, 3 * CH), BF16),
            shape((WIDTH, 3 * CH), BF16),
            shape((3 * CH, WIDTH), BF16),
            shape((3 * CH, WIDTH), BF16),
            shape((16, 2 * WIDTH), BF16),
            shape((16, WIDTH), BF16),
            shape((WIDTH, 2), F32),
        ),
        in_specs=[SMEM] + [VMEM] * 11,
        out_specs=[VMEM, VMEM, VMEM] + [VMEM] * 12,
        scratch_shapes=[
            pltpu.VMEM((NBR, 8, LIST), F32),
            pltpu.VMEM((16, PAIR), F32),
            pltpu.SemaphoreType.DMA((NBR,)),
            pltpu.SemaphoreType.DMA((NBR,)),
        ],
        compiler_params=pltpu.CompilerParams(
            collective_id=0, has_side_effects=True, vmem_limit_bytes=48 << 20
        ),
    )(
        edge_count, positions, species.reshape(1, ATOM), sends, edge_src, edge_dst,
        w_in, w_mid, w_pair, w_mix, w_back, w_read.reshape(1, WIDTH),
    )
    messages, force, energy = pl.pallas_call(
        edge_kernel,
        out_shape=(
            shape((NBR, 8, ATOM), F32),
            shape((3, ATOM), F32),
            shape((1, ATOM), F32),
        ),
        in_specs=[SMEM] + [VMEM] * 18,
        out_specs=[VMEM] * 3,
        scratch_shapes=[
            pltpu.VMEM((8, CAP + 512), F32),
            pltpu.VMEM((ATOM, CAP), BF16),
            pltpu.VMEM((2 * WIDTH, CAP), F32),
            pltpu.VMEM((WIDTH, CAP), F32),
            pltpu.VMEM((WIDTH, CAP), BF16),
            pltpu.VMEM((WIDTH, CAP), BF16),
            pltpu.VMEM((CH, CAP), F32),
            pltpu.VMEM((ROWS, CAP), F32),
            pltpu.VMEM((9 * CH, ATOM), F32),
            pltpu.VMEM((9 * CH, ATOM), F32),
            pltpu.VMEM((9 * CH, ATOM), BF16),
            pltpu.VMEM((9 * CH, ATOM), BF16),
            pltpu.VMEM((9 * CH, ATOM), BF16),
            pltpu.VMEM((9 * CH, ATOM), BF16),
            pltpu.VMEM((16, ATOM), F32),
            pltpu.VMEM((48, ATOM), F32),
        ],
        compiler_params=pltpu.CompilerParams(vmem_limit_bytes=56 << 20),
    )(edge_count, edge_src, edge_dst, sends, *shared)
    forces = pl.pallas_call(
        return_kernel,
        out_shape=shape((3, ATOM), F32),
        in_specs=[VMEM] * 3,
        out_specs=VMEM,
        scratch_shapes=[
            pltpu.VMEM((NBR, 8, ATOM), F32),
            pltpu.SemaphoreType.DMA((NBR,)),
            pltpu.SemaphoreType.DMA((NBR,)),
        ],
        compiler_params=pltpu.CompilerParams(
            collective_id=1, has_side_effects=True, vmem_limit_bytes=16 << 20
        ),
    )(messages, force, sends)
    return forces, energy.reshape(ATOM)


def solution(mesh):
    both = ("dom", "face")
    placed = (
        P(None, both), P(both), P(both, None, None), P(both, None), P(both, None), P(both),
        P(), P(), P(), P(), P(), P(),
    )
    return jax.shard_map(
        per_device,
        mesh=mesh,
        in_specs=placed,
        out_specs=(P(None, both), P(both)),
        check_vma=False,
    )
```

```python
import functools

import jax
import jax.numpy as jnp
from jax import lax
from jax.experimental import pallas as pl
from jax.experimental.pallas import tpu as pltpu
from jax.sharding import PartitionSpec as P

CH = 64
WIDTH = 128
BASIS = 8
SPECIES = 7
ENV_SCALE = 0.2
CUTOFF = 6.0
PI = 3.141592653589793
DIRECTIONS = ((-1, -1), (-1, 0), (-1, 1), (0, -1), (0, 1), (1, -1), (1, 0), (1, 1))
NBR = 8
ATOM = 256
GHOST = 64
PAIR = 1024
SLOTS = NBR * GHOST
LIST = PAIR + 128
CAP = 10 * PAIR
EB = 1024
F32 = jnp.float32
BF16 = jnp.bfloat16
I32 = jnp.int32
MESH = pl.DeviceIdType.MESH
VMEM = pl.BlockSpec(memory_space=pltpu.VMEM)
SMEM = pl.BlockSpec(memory_space=pltpu.SMEM)
HBM = pl.BlockSpec(memory_space=pltpu.HBM)

RAD, DRAD, ANG, ENVL, DENVL, RINV, DIR, ERAW, DANG, ROWS = 0, 8, 16, 25, 26, 27, 28, 31, 32, 40


def dot(a, b):
    return lax.dot_general(a, b, (((1,), (0,)), ((), ())), preferred_element_type=F32)


def dot_nt(a, b):
    return lax.dot_general(a, b, (((1,), (1,)), ((), ())), preferred_element_type=F32)


def exact(a, b):
    return jnp.dot(a, b, precision=lax.Precision.HIGHEST, preferred_element_type=F32)


def halves(x):
    high = x.astype(BF16)
    return high, (x - high.astype(F32)).astype(BF16)


def thirds(x):
    high = x.astype(BF16).astype(F32)
    rest = x - high
    mid = rest.astype(BF16).astype(F32)
    return high, mid, rest - mid


def one_hot(row, count):
    rows = lax.broadcasted_iota(I32, (count, row.shape[1]), 0)
    return jnp.where(rows == row, 1.0, 0.0).astype(BF16)


def atom_table(coords, kinds):
    parts = thirds(coords)
    pad = jnp.zeros((6, coords.shape[1]), F32)
    return jnp.concatenate([*parts, kinds, pad], axis=0)


def joined(rows):
    return rows[0:3] + rows[3:6] + rows[6:9]


def greet():
    here = [lax.axis_index("dom"), lax.axis_index("face")]
    sizes = [lax.axis_size("dom"), lax.axis_size("face")]
    peers = []
    for shift in DIRECTIONS:
        peers.append(
            tuple(lax.rem(at + by + size, size) for at, by, size in zip(here, shift, sizes))
        )
    barrier = pltpu.get_barrier_semaphore()
    for peer in peers:
        pl.semaphore_signal(barrier, inc=1, device_id=peer, device_id_type=MESH)
    return barrier, peers


def swap(peers, out_ref, in_ref, send_sem, recv_sem):
    copies = []
    for k, peer in enumerate(peers):
        copies.append(
            pltpu.make_async_remote_copy(
                src_ref=out_ref.at[k],
                dst_ref=in_ref.at[NBR - 1 - k],
                send_sem=send_sem.at[k],
                recv_sem=recv_sem.at[NBR - 1 - k],
                device_id=peer,
                device_id_type=MESH,
            )
        )
    for copy in copies:
        copy.start()
    return copies


def share_kernel(
    count_ref, *refs,
):
    sources, refs = refs[:11], refs[11:]
    (
        own_ref, table_ref, recv_ref, wx_ref, up_ref, upl_ref, dn_ref, dnl_ref,
        mt_ref, mtl_ref, mb_ref, mbl_ref, wr_ref, wrl_ref, ab_ref,
    ) = refs[:15]
    held, refs = refs[15:26], refs[26:]
    out_buf, order_buf, load_sem, send_sem, recv_sem = refs
    (
        pos_ref, spec_ref, send_ref, src_ref, dst_ref,
        w_in_ref, w_mid_ref, w_pair_ref, w_mix_ref, w_back_ref, w_read_ref,
    ) = held
    loads = [
        pltpu.make_async_copy(source, target, load_sem.at[i])
        for i, (source, target) in enumerate(zip(sources, held))
    ]
    for load in loads:
        load.start()
    barrier, peers = greet()
    for load in loads[:5]:
        load.wait()
    table = atom_table(pos_ref[...], spec_ref[...].astype(F32)).astype(BF16)
    table_ref[...] = table
    sends = jnp.concatenate([send_ref[k : k + 1, :] for k in range(NBR)], axis=1)
    ghosts = dot(table, one_hot(sends, ATOM))
    ghost_rows = jnp.concatenate([joined(ghosts), ghosts[9:10]], axis=0)
    src = src_ref[...]
    dst = dst_ref[...]
    lanes = lax.broadcasted_iota(I32, (1, PAIR), 1)
    live = lanes < count_ref[0]
    ghost = dst >= ATOM
    away = dst - ATOM
    bucket = jnp.where(ghost, (away >> 6) + 1, 0)
    bucket = jnp.where(live, bucket, 15)
    place = jnp.where(ghost, away & 63, dst)
    member = jnp.where(lax.broadcasted_iota(I32, (16, PAIR), 0) == bucket, 1.0, 0.0)
    before = lax.broadcasted_iota(I32, (ATOM, ATOM), 0) < lax.broadcasted_iota(I32, (ATOM, ATOM), 1)
    before = jnp.where(before, 1.0, 0.0).astype(BF16)
    pieces = [member[:, i * ATOM : (i + 1) * ATOM] for i in range(PAIR // ATOM)]
    ranks = dot(jnp.concatenate(pieces, axis=0).astype(BF16), before)
    sums = [jnp.sum(piece, axis=1, keepdims=True) for piece in pieces]
    total = sums[0] + sums[1] + sums[2] + sums[3]
    start = jnp.zeros((16, 1), F32)
    index = lax.broadcasted_iota(I32, (16, 1), 0)
    for b in range(NBR + 1):
        start = start + jnp.where(index > b, total[b : b + 1, :], 0.0)
    offset = start
    spots = []
    for i, piece in enumerate(pieces):
        where = ranks[16 * i : 16 * (i + 1)] + offset
        spots.append(jnp.sum(piece * where, axis=0, keepdims=True))
        offset = offset + sums[i]
    spot = jnp.concatenate(spots, axis=1)
    spot = jnp.where(live, spot, -1.0).astype(I32)
    picked = dot(table, one_hot(src, ATOM))
    data = jnp.concatenate(
        [picked[0:10], place.astype(F32), src.astype(F32), jnp.zeros((4, PAIR), F32)], axis=0
    ).astype(BF16)
    for i in range(PAIR // ATOM):
        rows = lax.broadcasted_iota(I32, (ATOM, PAIR), 0) + i * ATOM
        chosen = jnp.where(rows == spot, 1.0, 0.0).astype(BF16)
        order_buf[:, i * ATOM : (i + 1) * ATOM] = dot_nt(data, chosen)
    ordered = order_buf[...]
    entries = jnp.concatenate(
        [joined(ordered), ordered[9:12], jnp.zeros((2, PAIR), F32)], axis=0
    )
    none = jnp.zeros((8, GHOST), F32)
    for k in range(NBR):
        out_buf[k, :, 0:PAIR] = entries
        mine = jnp.concatenate([ghost_rows[:, k * GHOST : (k + 1) * GHOST], none[0:4]], axis=0)
        out_buf[k, :, PAIR:LIST] = jnp.concatenate([mine, none], axis=1)
        out_buf[k, 4:5, PAIR:LIST] = jnp.broadcast_to(total[k + 1 : k + 2, :], (1, 128))
        out_buf[k, 5:6, PAIR:LIST] = jnp.broadcast_to(start[k + 1 : k + 2, :], (1, 128))
    pl.semaphore_wait(barrier, NBR)
    copies = swap(peers, out_buf, recv_ref, send_sem, recv_sem)
    own_ref[0:8, 0:PAIR] = entries
    own_ref[:, PAIR:LIST] = jnp.zeros((16, 128), F32)
    own_ref[8:9, 0:PAIR] = src.astype(F32)
    own_ref[9:10, 0:PAIR] = dst.astype(F32)
    own_ref[10:11, 0:SLOTS] = sends.astype(F32)
    own_ref[11:12, PAIR:LIST] = jnp.full((1, 128), count_ref[0], I32).astype(F32)
    for load in loads[5:]:
        load.wait()
    own_ref[4:5, PAIR:LIST] = jnp.broadcast_to(total[0:1, :], (1, 128))
    w_in = w_in_ref[...]
    w_c = w_in[0:SPECIES].T
    w_p = w_in[SPECIES : 2 * SPECIES].T
    w_r = w_in[2 * SPECIES :]
    gap = jnp.zeros((WIDTH, 1), F32)
    first = jnp.concatenate([w_c, gap, w_p, gap, w_r.T], axis=1)
    first_high = first.astype(BF16).astype(F32)
    first_low = first - first_high
    wx_ref[...] = jnp.concatenate(
        [first_high, first_high[:, 16:24], first_low, jnp.zeros((WIDTH, 8), F32)], axis=1
    ).astype(BF16)
    wr_high, wr_low = halves(jnp.concatenate([w_r, jnp.zeros((8, WIDTH), F32)], axis=0))
    wr_ref[...] = jnp.concatenate([wr_high, wr_high], axis=1)
    wrl_ref[...] = wr_low
    w_mid = w_mid_ref[...]
    w_read = w_read_ref[...]
    down = jnp.concatenate(
        [exact(w_mid, w_pair_ref[...]), exact(w_mid, w_mix_ref[0:WIDTH, :])], axis=1
    )
    a_col = jnp.sum(w_mid * w_read, axis=1, keepdims=True)
    b_col = jnp.sum(w_back_ref[...] * w_read, axis=1, keepdims=True)
    ab_ref[...] = jnp.concatenate([a_col, b_col], axis=1)
    dn_high, dn_low = halves(down)
    dn_ref[...] = dn_high
    dnl_ref[...] = dn_low
    up = down.T
    up_high, up_low = halves(up)
    up_ref[...] = jnp.concatenate([up_high, up_high], axis=1)
    upl_ref[...] = up_low
    mix = jnp.concatenate(
        [w_mix_ref[pl.ds(WIDTH + degree, CH, stride=3), :] for degree in range(3)], axis=0
    )
    mb_ref[...], mbl_ref[...] = halves(mix)
    mt_ref[...], mtl_ref[...] = halves(mix.T)
    for copy in copies:
        copy.wait()


def edge_kernel(
    own_ref, table_ref, recv_ref,
    wx_ref, up_ref, upl_ref, dn_ref, dnl_ref, mt_ref, mtl_ref, mb_ref, mbl_ref,
    wr_ref, wrl_ref, ab_ref,
    msg_ref, force_ref, energy_ref,
    edges, hots, paired, slope, mixed, mixed_low, d_value, geo, env, g_env,
    fields, terms, around, at_centre, at_partner,
):
    count = own_ref[11:12, PAIR : PAIR + 128][0, 0].astype(I32)
    src = own_ref[8:9, 0:PAIR]
    dst = own_ref[9:10, 0:PAIR].astype(I32)
    near = jnp.concatenate([recv_ref[k, 0:4, PAIR : PAIR + GHOST] for k in range(NBR)], axis=1)
    ghosts = atom_table(near[0:3], near[3:4]).astype(BF16)
    table = table_ref[...]
    segments = jnp.concatenate([table, ghosts[:, 0:ATOM], ghosts[:, ATOM:SLOTS]], axis=0)
    found = dot(segments, one_hot(dst & 255, ATOM))
    part = dst >> 8
    picked = jnp.where(part == 0, found[0:16], jnp.where(part == 1, found[16:32], found[32:48]))
    edges[:, 0:PAIR] = jnp.concatenate(
        [joined(picked), picked[9:10], src, dst.astype(F32), jnp.zeros((2, PAIR), F32)],
        axis=0,
    )
    lane = lax.broadcasted_iota(I32, (8, 128), 1)
    row = lax.broadcasted_iota(I32, (8, 128), 0)

    def place(ref, size, begin, at, extra, tile):
        base = tile * 128 - at + begin
        first = base >> 7
        turn = base & 127
        low = jnp.clip(first, 0, 8)
        high = jnp.clip(first + 1, 0, 8)
        left = ref[0:8, pl.ds(pl.multiple_of(low * 128, 128), 128)]
        right = ref[0:8, pl.ds(pl.multiple_of(high * 128, 128), 128)]
        back = lax.rem(128 - turn, 128)
        taken = jnp.where(
            lane < 128 - turn, pltpu.roll(left, back, 1), pltpu.roll(right, back, 1)
        )
        here = pl.ds(pl.multiple_of(tile * 128, 128), 128)
        spot = tile * 128 + lane
        inside = (spot >= at) & (spot < at + size)
        edges[:, here] = jnp.where(inside, taken + extra, edges[:, here])

    def scalar(ref, which):
        return ref[which : which + 1, PAIR : PAIR + 128][0, 0].astype(I32)

    at = count
    jobs = []
    size = scalar(own_ref, 4)
    jobs.append((own_ref, size, 0, at, jnp.zeros((8, 128), F32), 4))
    at = at + size
    for k in range(NBR):
        ref = recv_ref.at[k]
        size = scalar(ref, 4)
        extra = jnp.where(row == 4, F32(ATOM + GHOST * k), 0.0)
        extra = jnp.where(row == 5, F32(ATOM * (3 + k)), extra)
        jobs.append((ref, size, scalar(ref, 5), at, extra, 2))
        at = at + size
    total = at
    for ref, size, begin, at, extra, usual in jobs:
        for step in range(usual):
            place(ref, size, begin, at, extra, (at >> 7) + step)
    for ref, size, begin, at, extra, usual in jobs:
        last = (at + size + 127) >> 7

        def more(tile, carry, ref=ref, size=size, begin=begin, at=at, extra=extra):
            place(ref, size, begin, at, extra, tile)
            return carry

        lax.fori_loop((at >> 7) + usual, last, more, 0)
    blocks = lax.div(total + EB - 1, EB)

    env[...] = jnp.zeros_like(env)
    g_env[...] = jnp.zeros_like(g_env)
    at_centre[...] = jnp.zeros_like(at_centre)
    at_partner[...] = jnp.zeros_like(at_partner)
    root3, root5, root15 = 3.0**0.5, 5.0**0.5, 15.0**0.5
    sends = own_ref[10:11, 0:SLOTS]
    own_index = lax.broadcasted_iota(I32, (1, ATOM), 1).astype(F32)
    codes = jnp.concatenate(
        [own_index, sends[:, 0:ATOM], sends[:, ATOM:SLOTS], jnp.zeros((13, ATOM), F32)], axis=0
    ).astype(BF16)

    def first_pass(block, carry):
        begin = pl.multiple_of(block * EB, EB)
        here = pl.ds(begin, EB)
        valid = begin + lax.broadcasted_iota(I32, (1, EB), 1) < total
        part = jnp.where(valid, edges[:, here], 0.0)
        code = part[4:5].astype(I32)
        seek = dot(codes, one_hot(code & 255, ATOM))
        kind = code >> 8
        centre = jnp.where(kind == 0, seek[0:1], jnp.where(kind == 1, seek[1:2], seek[2:3]))
        hot = one_hot(centre.astype(I32), ATOM)
        hots[:, here] = hot
        held = dot(table, hot)
        delta = part[0:3] - joined(held)
        length2 = delta[0:1] * delta[0:1] + delta[1:2] * delta[1:2] + delta[2:3] * delta[2:3] + 1.0
        soft = jnp.sqrt(length2)
        rinv = 1.0 / soft
        unit = delta * rinv
        ux, uy, uz = unit[0:1], unit[1:2], unit[2:3]
        turn = soft * (PI / CUTOFF) - PI / 2
        t2 = turn * turn
        cosine = -turn * (
            1 + t2 * (-1 / 6 + t2 * (1 / 120 + t2 * (-1 / 5040 + t2 * (1 / 362880 - t2 / 39916800))))
        )
        sine = 1 + t2 * (
            -1 / 2 + t2 * (1 / 24 + t2 * (-1 / 720 + t2 * (1 / 40320 + t2 * (-1 / 3628800 + t2 / 479001600))))
        )
        twice = 2 * cosine
        s_old, s_now = jnp.zeros_like(sine), sine
        c_old, c_now = jnp.ones_like(sine), cosine
        for b in range(BASIS):
            geo[RAD + b : RAD + b + 1, here] = s_now * rinv
            geo[DRAD + b : DRAD + b + 1, here] = (c_now * ((b + 1) * PI / CUTOFF) - s_now * rinv) * rinv
            s_old, s_now = s_now, twice * s_now - s_old
            c_old, c_now = c_now, twice * c_now - c_old
        angular = [
            jnp.ones_like(ux),
            root3 * ux,
            root3 * uy,
            root3 * uz,
            root15 * ux * uy,
            root15 * uy * uz,
            0.5 * root5 * (2.0 * uz * uz - ux * ux - uy * uy),
            root15 * ux * uz,
            0.5 * root15 * (ux * ux - uy * uy),
        ]
        for m in range(9):
            geo[ANG + m : ANG + m + 1, here] = angular[m]
        inner = 1.0 - length2 * (1.0 / (CUTOFF * CUTOFF))
        alive = jnp.where(valid, 1.0, 0.0)
        envelope = alive * inner * inner
        geo[ENVL : ENVL + 1, here] = envelope
        geo[DENVL : DENVL + 1, here] = alive * inner * soft * (-4.0 / (CUTOFF * CUTOFF))
        geo[RINV : RINV + 1, here] = rinv
        geo[DIR : DIR + 3, here] = unit
        radial = geo[RAD : RAD + 8, here]
        radial_low = radial - radial.astype(BF16).astype(F32)
        kinds = lax.broadcasted_iota(I32, (8, EB), 0)
        hot_c = jnp.where(kinds == held[9:10].astype(I32), 1.0, 0.0)
        hot_p = jnp.where(kinds == part[3:4].astype(I32), 1.0, 0.0)
        inputs = jnp.concatenate(
            [hot_c, hot_p, radial, radial_low, hot_c, hot_p, radial, jnp.zeros((8, EB), F32)], axis=0
        ).astype(BF16)
        pre = dot(wx_ref[...], inputs)
        gate = 1.0 / (1.0 + jnp.exp(-pre))
        act = pre * gate
        slope[:, here] = gate + act * (1.0 - gate)
        act_high, act_low = halves(act)
        after = dot(up_ref[...], jnp.concatenate([act_high, act_low], axis=0)) + dot(
            upl_ref[...], act_high
        )
        paired[:, here] = after
        geo[ERAW : ERAW + 1, here] = jnp.sum(act * ab_ref[:, 0:1], axis=0, keepdims=True)
        weights = after[0:CH] * envelope
        for m in range(9):
            term = weights if m == 0 else weights * angular[m]
            rows = slice(m * CH, (m + 1) * CH)
            terms[rows, 0:EB], terms[rows, EB:] = halves(term)
        env[...] += dot_nt(terms[...], jnp.concatenate([hot, hot], axis=1))
        return carry

    lax.fori_loop(0, blocks, first_pass, 0)
    fields[:, 0:ATOM], fields[:, ATOM:] = halves(env[...] * ENV_SCALE)
    degrees = (0, 1, 1, 1, 2, 2, 2, 2, 2)

    def second_pass(block, carry):
        here = pl.ds(pl.multiple_of(block * EB, EB), EB)
        hot = hots[:, here]
        angular = [geo[ANG + m : ANG + m + 1, here] for m in range(9)]
        envelope = geo[ENVL : ENVL + 1, here]
        around[...] = dot(fields[...], jnp.concatenate([hot, hot], axis=0))
        sums = [None, None, None]
        for m in range(9):
            got = around[m * CH : (m + 1) * CH, :]
            term = got if m == 0 else got * angular[m]
            degree = degrees[m]
            sums[degree] = term if sums[degree] is None else sums[degree] + term
        value = paired[CH : 2 * CH, here]
        invariant = jnp.concatenate([s * value for s in sums], axis=0)
        high, low = halves(invariant)
        mt = mt_ref[...]
        pre = paired[2 * CH :, here] + dot(mt, high) + dot(mt, low) + dot(mtl_ref[...], high)
        gate = 1.0 / (1.0 + jnp.exp(-pre))
        act = pre * gate
        back = ab_ref[:, 1:2]
        geo[ERAW : ERAW + 1, here] += jnp.sum(act * back, axis=0, keepdims=True)
        d_pre = (gate + act * (1.0 - gate)) * back * envelope
        d_high, d_low = halves(d_pre)
        mixed[:, here] = d_high
        mixed_low[:, here] = d_low
        mb = mb_ref[...]
        d_inv = dot(mb, d_high) + dot(mb, d_low) + dot(mbl_ref[...], d_high)
        d_inv = [d_inv[i * CH : (i + 1) * CH] for i in range(3)]
        d_value[:, here] = d_inv[0] * sums[0] + d_inv[1] * sums[1] + d_inv[2] * sums[2]
        d_sum = [d * value for d in d_inv]
        for m in range(9):
            share = d_sum[degrees[m]]
            term = share if m == 0 else share * angular[m]
            rows = slice(m * CH, (m + 1) * CH)
            terms[rows, 0:EB], terms[rows, EB:] = halves(term)
            if m:
                geo[DANG + m - 1 : DANG + m, here] = jnp.sum(share * around[rows, :], axis=0, keepdims=True)
        g_env[...] += dot_nt(terms[...], jnp.concatenate([hot, hot], axis=1))
        return carry

    lax.fori_loop(0, blocks, second_pass, 0)
    fields[:, 0:ATOM], fields[:, ATOM:] = halves(g_env[...] * ENV_SCALE)

    def third_pass(block, carry):
        here = pl.ds(pl.multiple_of(block * EB, EB), EB)
        hot = hots[:, here]
        angular = [geo[ANG + m : ANG + m + 1, here] for m in range(9)]
        envelope = geo[ENVL : ENVL + 1, here]
        raw = paired[0:CH, here]
        weights = raw * envelope
        d_weight = None
        d_ang = [None]
        around[...] = dot(fields[...], jnp.concatenate([hot, hot], axis=0))
        for m in range(9):
            got = around[m * CH : (m + 1) * CH, :]
            term = got if m == 0 else got * angular[m]
            d_weight = term if m == 0 else d_weight + term
            if m:
                d_ang.append(
                    geo[DANG + m - 1 : DANG + m, here] + jnp.sum(weights * got, axis=0, keepdims=True)
                )
        e_raw = geo[ERAW : ERAW + 1, here]
        d_envelope = e_raw + jnp.sum(d_weight * raw, axis=0, keepdims=True)
        pair_high, pair_low = halves(
            jnp.concatenate([d_weight * envelope, d_value[:, here]], axis=0)
        )
        both_high = jnp.concatenate([pair_high, mixed[:, here]], axis=0)
        both_low = jnp.concatenate([pair_low, mixed_low[:, here]], axis=0)
        dn = dn_ref[...]
        d_act = dot(dn, both_high) + dot(dn, both_low) + dot(dnl_ref[...], both_high)
        d_act = d_act + ab_ref[:, 0:1] * envelope
        d_pre_high, d_pre_low = halves(d_act * slope[:, here])
        d_radial = dot(wr_ref[...], jnp.concatenate([d_pre_high, d_pre_low], axis=0)) + dot(
            wrl_ref[...], d_pre_high
        )
        d_soft = jnp.sum(d_radial[0:8] * geo[DRAD : DRAD + 8, here], axis=0, keepdims=True)
        d_soft = d_soft + d_envelope * geo[DENVL : DENVL + 1, here]
        unit = geo[DIR : DIR + 3, here]
        rinv = geo[RINV : RINV + 1, here]
        ux, uy, uz = unit[0:1], unit[1:2], unit[2:3]
        d_ux = root3 * d_ang[1] + root15 * (uy * d_ang[4] + uz * d_ang[7] + ux * d_ang[8]) - root5 * ux * d_ang[6]
        d_uy = root3 * d_ang[2] + root15 * (ux * d_ang[4] + uz * d_ang[5] - uy * d_ang[8]) - root5 * uy * d_ang[6]
        d_uz = root3 * d_ang[3] + root15 * (uy * d_ang[5] + ux * d_ang[7]) + 2.0 * root5 * uz * d_ang[6]
        along = d_soft - (d_ux * ux + d_uy * uy + d_uz * uz) * rinv
        pull = [d * rinv + u * along for d, u in ((d_ux, ux), (d_uy, uy), (d_uz, uz))]
        energy = e_raw * envelope
        sent = jnp.concatenate([*pull, energy, jnp.zeros((4, EB), F32)], axis=0)
        sent = jnp.concatenate([sent, sent - sent.astype(BF16).astype(F32)], axis=0).astype(BF16)
        at_centre[...] += dot_nt(sent, hot)
        code = jnp.where(
            begin_valid(block, total), edges[5:6, here], 0.0
        ).astype(I32)
        seg = lax.broadcasted_iota(I32, (16, EB), 0) == (code >> 8)
        spread = jnp.concatenate([jnp.where(seg, g, 0.0) for g in pull], axis=0)
        high, low = halves(spread)
        hot_partner = one_hot(code & 255, ATOM)
        at_partner[...] += dot_nt(high, hot_partner) + dot_nt(low, hot_partner)
        return carry

    lax.fori_loop(0, blocks, third_pass, 0)
    sums = at_centre[...]
    sums = sums[0:8] + sums[8:16]
    parts = at_partner[...]
    mine = [parts[16 * i : 16 * i + 1] for i in range(3)]
    force_ref[...] = sums[0:3] - jnp.concatenate(mine, axis=0)
    energy_ref[...] = sums[3:4]
    msg_ref[...] = jnp.zeros_like(msg_ref)
    for k in range(NBR):
        for i in range(3):
            msg_ref[k, i : i + 1, :] = parts[16 * i + 3 + k : 16 * i + 4 + k]
            ghost = parts[16 * i + 1 + k // 4 : 16 * i + 2 + k // 4]
            msg_ref[k, 3 + i : 4 + i, 0:GHOST] = ghost[:, (k % 4) * GHOST : (k % 4 + 1) * GHOST]


def begin_valid(block, total):
    return block * EB + lax.broadcasted_iota(I32, (1, EB), 1) < total


def return_kernel(msg_ref, force_ref, own_ref, out_ref, inbox, send_sem, recv_sem):
    barrier, peers = greet()
    sends = own_ref[10:11, 0:SLOTS].astype(I32)
    hot = one_hot(sends, ATOM)
    pl.semaphore_wait(barrier, NBR)
    copies = swap(peers, msg_ref, inbox, send_sem, recv_sem)
    for copy in copies:
        copy.wait()
    total = force_ref[...]
    for k in range(NBR):
        total = total - inbox[k, 0:3, :]
    ghosts = jnp.concatenate([inbox[k, 3:6, 0:GHOST] for k in range(NBR)], axis=1)
    split = jnp.concatenate([*thirds(ghosts), jnp.zeros((7, SLOTS), F32)], axis=0).astype(BF16)
    back = dot_nt(split, hot)
    out_ref[...] = total - joined(back)


def edge_call(*operands):
    shape = jax.ShapeDtypeStruct
    return pl.pallas_call(
        edge_kernel,
        out_shape=(
            shape((NBR, 8, ATOM), F32),
            shape((3, ATOM), F32),
            shape((1, ATOM), F32),
        ),
        in_specs=[VMEM] * 15,
        out_specs=[VMEM] * 3,
        scratch_shapes=[
            pltpu.VMEM((8, CAP + 512), F32),
            pltpu.VMEM((ATOM, CAP), BF16),
            pltpu.VMEM((2 * WIDTH, CAP), F32),
            pltpu.VMEM((WIDTH, CAP), F32),
            pltpu.VMEM((WIDTH, CAP), BF16),
            pltpu.VMEM((WIDTH, CAP), BF16),
            pltpu.VMEM((CH, CAP), F32),
            pltpu.VMEM((ROWS, CAP), F32),
            pltpu.VMEM((9 * CH, ATOM), F32),
            pltpu.VMEM((9 * CH, ATOM), F32),
            pltpu.VMEM((9 * CH, 2 * ATOM), BF16),
            pltpu.VMEM((9 * CH, 2 * EB), BF16),
            pltpu.VMEM((9 * CH, EB), F32),
            pltpu.VMEM((16, ATOM), F32),
            pltpu.VMEM((48, ATOM), F32),
        ],
        compiler_params=pltpu.CompilerParams(vmem_limit_bytes=48 << 20),
    )(*operands)


def per_device(
    positions, species, send_list, edge_src, edge_dst, edge_count,
    w_in, w_mid, w_pair, w_mix, w_back, w_read,
):
    sends = send_list[0]
    shape = jax.ShapeDtypeStruct
    shared = pl.pallas_call(
        share_kernel,
        out_shape=(
            shape((16, LIST), F32),
            shape((16, ATOM), BF16),
            shape((NBR, 8, LIST), F32),
            shape((WIDTH, 64), BF16),
            shape((2 * WIDTH, 2 * WIDTH), BF16),
            shape((2 * WIDTH, WIDTH), BF16),
            shape((WIDTH, 2 * WIDTH), BF16),
            shape((WIDTH, 2 * WIDTH), BF16),
            shape((WIDTH, 3 * CH), BF16),
            shape((WIDTH, 3 * CH), BF16),
            shape((3 * CH, WIDTH), BF16),
            shape((3 * CH, WIDTH), BF16),
            shape((16, 2 * WIDTH), BF16),
            shape((16, WIDTH), BF16),
            shape((WIDTH, 2), F32),
        ),
        in_specs=[SMEM] + [HBM] * 11,
        out_specs=[VMEM] * 15,
        scratch_shapes=[
            pltpu.VMEM((3, ATOM), F32),
            pltpu.VMEM((1, ATOM), I32),
            pltpu.VMEM((NBR, GHOST), I32),
            pltpu.VMEM((1, PAIR), I32),
            pltpu.VMEM((1, PAIR), I32),
            pltpu.VMEM((2 * SPECIES + BASIS, WIDTH), F32),
            pltpu.VMEM((WIDTH, WIDTH), F32),
            pltpu.VMEM((WIDTH, WIDTH), F32),
            pltpu.VMEM((WIDTH + 3 * CH, WIDTH), F32),
            pltpu.VMEM((WIDTH, WIDTH), F32),
            pltpu.VMEM((1, WIDTH), F32),
            pltpu.VMEM((NBR, 8, LIST), F32),
            pltpu.VMEM((16, PAIR), F32),
            pltpu.SemaphoreType.DMA((11,)),
            pltpu.SemaphoreType.DMA((NBR,)),
            pltpu.SemaphoreType.DMA((NBR,)),
        ],
        compiler_params=pltpu.CompilerParams(
            collective_id=0, has_side_effects=True, vmem_limit_bytes=8 << 20
        ),
    )(
        edge_count,
        *(
            pltpu.with_memory_space_constraint(x, pltpu.HBM)
            for x in (
                positions, species.reshape(1, ATOM), sends, edge_src, edge_dst,
                w_in, w_mid, w_pair, w_mix, w_back, w_read.reshape(1, WIDTH),
            )
        ),
    )
    messages, force, energy = edge_call(*shared)
    forces = pl.pallas_call(
        return_kernel,
        out_shape=shape((3, ATOM), F32),
        in_specs=[VMEM] * 3,
        out_specs=VMEM,
        scratch_shapes=[
            pltpu.VMEM((NBR, 8, ATOM), F32),
            pltpu.SemaphoreType.DMA((NBR,)),
            pltpu.SemaphoreType.DMA((NBR,)),
        ],
        compiler_params=pltpu.CompilerParams(
            collective_id=1, has_side_effects=True, vmem_limit_bytes=4 << 20
        ),
    )(messages, force, shared[0])
    return forces, energy.reshape(ATOM)


def solution(mesh):
    both = ("dom", "face")
    placed = (
        P(None, both), P(both), P(both, None, None), P(both, None), P(both, None), P(both),
        P(), P(), P(), P(), P(), P(),
    )
    return jax.shard_map(
        per_device,
        mesh=mesh,
        in_specs=placed,
        out_specs=(P(None, both), P(both)),
        check_vma=False,
    )
```

```python
import functools

import jax
import jax.numpy as jnp
from jax import lax
from jax.experimental import pallas as pl
from jax.experimental.pallas import tpu as pltpu
from jax.sharding import PartitionSpec as P

CH = 64
WIDTH = 128
BASIS = 8
SPECIES = 7
ENV_SCALE = 0.2
CUTOFF = 6.0
PI = 3.141592653589793
DIRECTIONS = ((-1, -1), (-1, 0), (-1, 1), (0, -1), (0, 1), (1, -1), (1, 0), (1, 1))
NBR = 8
ATOM = 256
GHOST = 64
PAIR = 1024
SLOTS = NBR * GHOST
LIST = PAIR + 128
CAP = 10 * PAIR
EB = 2048
SB = 2048
NSUB = EB // SB
F32 = jnp.float32
BF16 = jnp.bfloat16
I32 = jnp.int32
MESH = pl.DeviceIdType.MESH
VMEM = pl.BlockSpec(memory_space=pltpu.VMEM)
SMEM = pl.BlockSpec(memory_space=pltpu.SMEM)
HBM = pl.BlockSpec(memory_space=pltpu.HBM)

RAD, DRAD, ANG, ENVL, DENVL, RINV, DIR, ERAW, DANG, ROWS = 0, 8, 16, 25, 26, 27, 28, 31, 32, 40


def dot(a, b):
    return lax.dot_general(a, b, (((1,), (0,)), ((), ())), preferred_element_type=F32)


def dot_nt(a, b):
    return lax.dot_general(a, b, (((1,), (1,)), ((), ())), preferred_element_type=F32)


def exact(a, b):
    return jnp.dot(a, b, precision=lax.Precision.HIGHEST, preferred_element_type=F32)


def halves(x):
    high = x.astype(BF16)
    return high, (x - high.astype(F32)).astype(BF16)


def thirds(x):
    high = x.astype(BF16).astype(F32)
    rest = x - high
    mid = rest.astype(BF16).astype(F32)
    return high, mid, rest - mid


def sigmoid(x):
    return 0.5 * jnp.tanh(0.5 * x) + 0.5


def triple(weight):
    high, low = halves(weight)
    return jnp.concatenate([high, high, low], axis=1)


def stacked(x):
    high, low = halves(x)
    return jnp.concatenate([high, low, high], axis=0)


def one_hot(row, count):
    rows = lax.broadcasted_iota(I32, (count, row.shape[1]), 0)
    return jnp.where(rows == row, 1.0, 0.0).astype(BF16)


def atom_table(coords, kinds):
    parts = thirds(coords)
    pad = jnp.zeros((6, coords.shape[1]), F32)
    return jnp.concatenate([*parts, kinds, pad], axis=0)


def joined(rows):
    return rows[0:3] + rows[3:6] + rows[6:9]


def greet():
    here = [lax.axis_index("dom"), lax.axis_index("face")]
    sizes = [lax.axis_size("dom"), lax.axis_size("face")]
    peers = []
    for shift in DIRECTIONS:
        peers.append(
            tuple(lax.rem(at + by + size, size) for at, by, size in zip(here, shift, sizes))
        )
    barrier = pltpu.get_barrier_semaphore()
    for peer in peers:
        pl.semaphore_signal(barrier, inc=1, device_id=peer, device_id_type=MESH)
    return barrier, peers


def swap(peers, out_ref, in_ref, send_sem, recv_sem):
    copies = []
    for k, peer in enumerate(peers):
        copies.append(
            pltpu.make_async_remote_copy(
                src_ref=out_ref.at[k],
                dst_ref=in_ref.at[NBR - 1 - k],
                send_sem=send_sem.at[k],
                recv_sem=recv_sem.at[NBR - 1 - k],
                device_id=peer,
                device_id_type=MESH,
            )
        )
    for copy in copies:
        copy.start()
    return copies


def share_kernel(
    count_ref, *refs,
):
    sources, refs = refs[:11], refs[11:]
    (
        own_ref, table_ref, recv_ref, wx_ref, up_ref, dn_ref, mt_ref, mb_ref, wr_ref, ab_ref,
    ) = refs[:10]
    held, refs = refs[10:21], refs[21:]
    out_buf, order_buf, load_sem, send_sem, recv_sem = refs
    (
        pos_ref, spec_ref, send_ref, src_ref, dst_ref,
        w_in_ref, w_mid_ref, w_pair_ref, w_mix_ref, w_back_ref, w_read_ref,
    ) = held
    loads = [
        pltpu.make_async_copy(source, target, load_sem.at[i])
        for i, (source, target) in enumerate(zip(sources, held))
    ]
    for load in loads:
        load.start()
    barrier, peers = greet()
    for load in loads[:5]:
        load.wait()
    table = atom_table(pos_ref[...], spec_ref[...].astype(F32)).astype(BF16)
    table_ref[...] = table
    sends = jnp.concatenate([send_ref[k : k + 1, :] for k in range(NBR)], axis=1)
    ghosts = dot(table, one_hot(sends, ATOM))
    ghost_rows = jnp.concatenate([joined(ghosts), ghosts[9:10]], axis=0)
    src = src_ref[...]
    dst = dst_ref[...]
    lanes = lax.broadcasted_iota(I32, (1, PAIR), 1)
    live = lanes < count_ref[0]
    ghost = dst >= ATOM
    away = dst - ATOM
    bucket = jnp.where(ghost, (away >> 6) + 1, 0)
    bucket = jnp.where(live, bucket, 15)
    place = jnp.where(ghost, away & 63, dst)
    member = jnp.where(lax.broadcasted_iota(I32, (16, PAIR), 0) == bucket, 1.0, 0.0)
    before = lax.broadcasted_iota(I32, (ATOM, ATOM), 0) < lax.broadcasted_iota(I32, (ATOM, ATOM), 1)
    before = jnp.where(before, 1.0, 0.0).astype(BF16)
    pieces = [member[:, i * ATOM : (i + 1) * ATOM] for i in range(PAIR // ATOM)]
    ranks = dot(jnp.concatenate(pieces, axis=0).astype(BF16), before)
    sums = [jnp.sum(piece, axis=1, keepdims=True) for piece in pieces]
    total = sums[0] + sums[1] + sums[2] + sums[3]
    start = jnp.zeros((16, 1), F32)
    index = lax.broadcasted_iota(I32, (16, 1), 0)
    for b in range(NBR + 1):
        start = start + jnp.where(index > b, total[b : b + 1, :], 0.0)
    offset = start
    spots = []
    for i, piece in enumerate(pieces):
        where = ranks[16 * i : 16 * (i + 1)] + offset
        spots.append(jnp.sum(piece * where, axis=0, keepdims=True))
        offset = offset + sums[i]
    spot = jnp.concatenate(spots, axis=1)
    spot = jnp.where(live, spot, -1.0).astype(I32)
    picked = dot(table, one_hot(src, ATOM))
    data = jnp.concatenate(
        [picked[0:10], place.astype(F32), src.astype(F32), jnp.zeros((4, PAIR), F32)], axis=0
    ).astype(BF16)
    for i in range(PAIR // ATOM):
        rows = lax.broadcasted_iota(I32, (ATOM, PAIR), 0) + i * ATOM
        chosen = jnp.where(rows == spot, 1.0, 0.0).astype(BF16)
        order_buf[:, i * ATOM : (i + 1) * ATOM] = dot_nt(data, chosen)
    ordered = order_buf[...]
    entries = jnp.concatenate(
        [joined(ordered), ordered[9:12], jnp.zeros((2, PAIR), F32)], axis=0
    )
    none = jnp.zeros((8, GHOST), F32)
    for k in range(NBR):
        out_buf[k, :, 0:PAIR] = entries
        mine = jnp.concatenate([ghost_rows[:, k * GHOST : (k + 1) * GHOST], none[0:4]], axis=0)
        out_buf[k, :, PAIR:LIST] = jnp.concatenate([mine, none], axis=1)
        out_buf[k, 4:5, PAIR:LIST] = jnp.broadcast_to(total[k + 1 : k + 2, :], (1, 128))
        out_buf[k, 5:6, PAIR:LIST] = jnp.broadcast_to(start[k + 1 : k + 2, :], (1, 128))
    pl.semaphore_wait(barrier, NBR)
    copies = swap(peers, out_buf, recv_ref, send_sem, recv_sem)
    own_ref[0:8, 0:PAIR] = entries
    own_ref[:, PAIR:LIST] = jnp.zeros((16, 128), F32)
    own_ref[8:9, 0:PAIR] = src.astype(F32)
    own_ref[9:10, 0:PAIR] = dst.astype(F32)
    own_ref[10:11, 0:SLOTS] = sends.astype(F32)
    own_ref[11:12, PAIR:LIST] = jnp.full((1, 128), count_ref[0], I32).astype(F32)
    for load in loads[5:]:
        load.wait()
    own_ref[4:5, PAIR:LIST] = jnp.broadcast_to(total[0:1, :], (1, 128))
    w_in = w_in_ref[...]
    w_c = w_in[0:SPECIES].T
    w_p = w_in[SPECIES : 2 * SPECIES].T
    w_r = w_in[2 * SPECIES :]
    gap = jnp.zeros((WIDTH, 1), F32)
    first = jnp.concatenate([w_c, gap, w_p, gap, w_r.T], axis=1)
    first_high = first.astype(BF16).astype(F32)
    first_low = first - first_high
    wx_ref[...] = jnp.concatenate(
        [first_high, first_high[:, 16:24], first_low, jnp.zeros((WIDTH, 8), F32)], axis=1
    ).astype(BF16)
    wr_high, wr_low = halves(jnp.concatenate([w_r, jnp.zeros((8, WIDTH), F32)], axis=0))
    wr_ref[...] = jnp.concatenate([wr_high, wr_high, wr_low], axis=1)
    w_mid = w_mid_ref[...]
    w_read = w_read_ref[...]
    down = jnp.concatenate(
        [exact(w_mid, w_pair_ref[...]), exact(w_mid, w_mix_ref[0:WIDTH, :])], axis=1
    )
    a_col = jnp.sum(w_mid * w_read, axis=1, keepdims=True)
    b_col = jnp.sum(w_back_ref[...] * w_read, axis=1, keepdims=True)
    ab_ref[...] = jnp.concatenate([a_col, b_col], axis=1)
    dn_ref[...] = triple(down)
    up_ref[...] = triple(down.T)
    mix = jnp.concatenate(
        [w_mix_ref[pl.ds(WIDTH + degree, CH, stride=3), :] for degree in range(3)], axis=0
    )
    mb_ref[...] = triple(mix)
    mt_ref[...] = triple(mix.T)
    for copy in copies:
        copy.wait()


def edge_kernel(
    own_ref, table_ref, recv_ref,
    wx_ref, up_ref, dn_ref, mt_ref, mb_ref, wr_ref, ab_ref,
    msg_ref, force_ref, energy_ref,
    edges, hots, paired, slope, mixed, mixed_low, d_value, geo, env, g_env,
    fields, terms, around, at_centre, at_partner,
):
    count = own_ref[11:12, PAIR : PAIR + 128][0, 0].astype(I32)
    src = own_ref[8:9, 0:PAIR]
    dst = own_ref[9:10, 0:PAIR].astype(I32)
    near = jnp.concatenate([recv_ref[k, 0:4, PAIR : PAIR + GHOST] for k in range(NBR)], axis=1)
    ghosts = atom_table(near[0:3], near[3:4]).astype(BF16)
    table = table_ref[...]
    segments = jnp.concatenate([table, ghosts[:, 0:ATOM], ghosts[:, ATOM:SLOTS]], axis=0)
    found = dot(segments, one_hot(dst & 255, ATOM))
    part = dst >> 8
    picked = jnp.where(part == 0, found[0:16], jnp.where(part == 1, found[16:32], found[32:48]))
    edges[:, 0:PAIR] = jnp.concatenate(
        [joined(picked), picked[9:10], src, dst.astype(F32), jnp.zeros((2, PAIR), F32)],
        axis=0,
    )
    lane = lax.broadcasted_iota(I32, (8, 128), 1)
    row = lax.broadcasted_iota(I32, (8, 128), 0)

    def place(ref, size, begin, at, extra, tile):
        base = tile * 128 - at + begin
        first = base >> 7
        turn = base & 127
        low = jnp.clip(first, 0, 8)
        high = jnp.clip(first + 1, 0, 8)
        left = ref[0:8, pl.ds(pl.multiple_of(low * 128, 128), 128)]
        right = ref[0:8, pl.ds(pl.multiple_of(high * 128, 128), 128)]
        back = lax.rem(128 - turn, 128)
        taken = jnp.where(
            lane < 128 - turn, pltpu.roll(left, back, 1), pltpu.roll(right, back, 1)
        )
        here = pl.ds(pl.multiple_of(tile * 128, 128), 128)
        spot = tile * 128 + lane
        inside = (spot >= at) & (spot < at + size)
        edges[:, here] = jnp.where(inside, taken + extra, edges[:, here])

    def scalar(ref, which):
        return ref[which : which + 1, PAIR : PAIR + 128][0, 0].astype(I32)

    at = count
    jobs = []
    size = scalar(own_ref, 4)
    jobs.append((own_ref, size, 0, at, jnp.zeros((8, 128), F32), 4))
    at = at + size
    for k in range(NBR):
        ref = recv_ref.at[k]
        size = scalar(ref, 4)
        extra = jnp.where(row == 4, F32(ATOM + GHOST * k), 0.0)
        extra = jnp.where(row == 5, F32(ATOM * (3 + k)), extra)
        jobs.append((ref, size, scalar(ref, 5), at, extra, 2))
        at = at + size
    total = at
    for ref, size, begin, at, extra, usual in jobs:
        for step in range(usual):
            place(ref, size, begin, at, extra, (at >> 7) + step)
    for ref, size, begin, at, extra, usual in jobs:
        last = (at + size + 127) >> 7

        def more(tile, carry, ref=ref, size=size, begin=begin, at=at, extra=extra):
            place(ref, size, begin, at, extra, tile)
            return carry

        lax.fori_loop((at >> 7) + usual, last, more, 0)
    blocks = lax.div(total + EB - 1, EB)

    env[...] = jnp.zeros_like(env)
    g_env[...] = jnp.zeros_like(g_env)
    at_centre[...] = jnp.zeros_like(at_centre)
    at_partner[...] = jnp.zeros_like(at_partner)
    root3, root5, root15 = 3.0**0.5, 5.0**0.5, 15.0**0.5
    sends = own_ref[10:11, 0:SLOTS]
    own_index = lax.broadcasted_iota(I32, (1, ATOM), 1).astype(F32)
    codes = jnp.concatenate(
        [own_index, sends[:, 0:ATOM], sends[:, ATOM:SLOTS], jnp.zeros((13, ATOM), F32)], axis=0
    ).astype(BF16)

    def first_geometry(begin):
        here = pl.ds(pl.multiple_of(begin, SB), SB)
        valid = begin + lax.broadcasted_iota(I32, (1, SB), 1) < total
        part = jnp.where(valid, edges[:, here], 0.0)
        code = part[4:5].astype(I32)
        seek = dot(codes, one_hot(code & 255, ATOM))
        kind = code >> 8
        centre = jnp.where(kind == 0, seek[0:1], jnp.where(kind == 1, seek[1:2], seek[2:3]))
        hot = one_hot(centre.astype(I32), ATOM)
        hots[:, here] = hot
        held = dot(table, hot)
        delta = part[0:3] - joined(held)
        length2 = delta[0:1] * delta[0:1] + delta[1:2] * delta[1:2] + delta[2:3] * delta[2:3] + 1.0
        soft = jnp.sqrt(length2)
        rinv = 1.0 / soft
        unit = delta * rinv
        ux, uy, uz = unit[0:1], unit[1:2], unit[2:3]
        turn = soft * (PI / CUTOFF) - PI / 2
        t2 = turn * turn
        cosine = -turn * (
            1 + t2 * (-1 / 6 + t2 * (1 / 120 + t2 * (-1 / 5040 + t2 * (1 / 362880 - t2 / 39916800))))
        )
        sine = 1 + t2 * (
            -1 / 2 + t2 * (1 / 24 + t2 * (-1 / 720 + t2 * (1 / 40320 + t2 * (-1 / 3628800 + t2 / 479001600))))
        )
        twice = 2 * cosine
        s_old, s_now = jnp.zeros_like(sine), sine
        c_old, c_now = jnp.ones_like(sine), cosine
        for b in range(BASIS):
            geo[RAD + b : RAD + b + 1, here] = s_now * rinv
            geo[DRAD + b : DRAD + b + 1, here] = (c_now * ((b + 1) * PI / CUTOFF) - s_now * rinv) * rinv
            s_old, s_now = s_now, twice * s_now - s_old
            c_old, c_now = c_now, twice * c_now - c_old
        angular = [
            jnp.ones_like(ux),
            root3 * ux,
            root3 * uy,
            root3 * uz,
            root15 * ux * uy,
            root15 * uy * uz,
            0.5 * root5 * (2.0 * uz * uz - ux * ux - uy * uy),
            root15 * ux * uz,
            0.5 * root15 * (ux * ux - uy * uy),
        ]
        for m in range(9):
            geo[ANG + m : ANG + m + 1, here] = angular[m]
        inner = 1.0 - length2 * (1.0 / (CUTOFF * CUTOFF))
        alive = jnp.where(valid, 1.0, 0.0)
        geo[ENVL : ENVL + 1, here] = alive * inner * inner
        geo[DENVL : DENVL + 1, here] = alive * inner * soft * (-4.0 / (CUTOFF * CUTOFF))
        geo[RINV : RINV + 1, here] = rinv
        geo[DIR : DIR + 3, here] = unit
        radial = geo[RAD : RAD + 8, here]
        radial_low = radial - radial.astype(BF16).astype(F32)
        kinds = lax.broadcasted_iota(I32, (8, SB), 0)
        hot_c = jnp.where(kinds == held[9:10].astype(I32), 1.0, 0.0)
        hot_p = jnp.where(kinds == part[3:4].astype(I32), 1.0, 0.0)
        inputs = jnp.concatenate(
            [hot_c, hot_p, radial, radial_low, hot_c, hot_p, radial, jnp.zeros((8, SB), F32)], axis=0
        ).astype(BF16)
        return dot(wx_ref[...], inputs)

    def first_layers(begin, pre):
        here = pl.ds(pl.multiple_of(begin, SB), SB)
        gate = sigmoid(pre)
        act = pre * gate
        slope[:, here] = gate + act * (1.0 - gate)
        after = dot(up_ref[...], stacked(act))
        paired[:, here] = after
        geo[ERAW : ERAW + 1, here] = jnp.sum(act * ab_ref[:, 0:1], axis=0, keepdims=True)

    def first_terms(sub, begin):
        here = pl.ds(pl.multiple_of(begin, SB), SB)
        weights = paired[0:CH, here] * geo[ENVL : ENVL + 1, here]
        at = sub * SB
        for m in range(9):
            term = weights if m == 0 else weights * geo[ANG + m : ANG + m + 1, here]
            rows = slice(m * CH, (m + 1) * CH)
            terms[rows, at : at + SB], terms[rows, EB + at : EB + at + SB] = halves(term)

    def first_pass(block, carry):
        begin = pl.multiple_of(block * EB, EB)
        pres = [first_geometry(begin + i * SB) for i in range(NSUB)]
        for i in range(NSUB):
            first_layers(begin + i * SB, pres[i])
        for i in range(NSUB):
            first_terms(i, begin + i * SB)
        hot = hots[:, pl.ds(begin, EB)]
        env[...] += dot_nt(terms[...], jnp.concatenate([hot, hot], axis=1))
        return carry

    lax.fori_loop(0, blocks, first_pass, 0)
    fields[:, 0:ATOM], fields[:, ATOM:] = halves(env[...] * ENV_SCALE)
    degrees = (0, 1, 1, 1, 2, 2, 2, 2, 2)

    def gather(sub, begin):
        hot = hots[:, pl.ds(pl.multiple_of(begin, SB), SB)]
        both = jnp.concatenate([hot, hot], axis=0)
        for lo, hi in ((0, 288), (288, 576)):
            around[lo:hi, sub * SB : (sub + 1) * SB] = dot(fields[lo:hi, :], both)

    def second_middle(sub, begin):
        here = pl.ds(pl.multiple_of(begin, SB), SB)
        at = sub * SB
        there = slice(at, at + SB)
        envelope = geo[ENVL : ENVL + 1, here]
        sums = [None, None, None]
        for m in range(9):
            got = around[m * CH : (m + 1) * CH, there]
            term = got if m == 0 else got * geo[ANG + m : ANG + m + 1, here]
            degree = degrees[m]
            sums[degree] = term if sums[degree] is None else sums[degree] + term
        value = paired[CH : 2 * CH, here]
        invariant = jnp.concatenate([s * value for s in sums], axis=0)
        pre = paired[2 * CH :, here] + dot(mt_ref[...], stacked(invariant))
        gate = sigmoid(pre)
        act = pre * gate
        back = ab_ref[:, 1:2]
        geo[ERAW : ERAW + 1, here] += jnp.sum(act * back, axis=0, keepdims=True)
        d_pre = (gate + act * (1.0 - gate)) * back * envelope
        d_high, d_low = halves(d_pre)
        mixed[:, here] = d_high
        mixed_low[:, here] = d_low
        d_inv = dot(mb_ref[...], jnp.concatenate([d_high, d_low, d_high], axis=0))
        d_inv = [d_inv[i * CH : (i + 1) * CH] for i in range(3)]
        d_value[:, here] = d_inv[0] * sums[0] + d_inv[1] * sums[1] + d_inv[2] * sums[2]
        d_sum = [d * value for d in d_inv]
        for m in range(9):
            share = d_sum[degrees[m]]
            term = share if m == 0 else share * geo[ANG + m : ANG + m + 1, here]
            rows = slice(m * CH, (m + 1) * CH)
            terms[rows, at : at + SB], terms[rows, EB + at : EB + at + SB] = halves(term)
            if m:
                geo[DANG + m - 1 : DANG + m, here] = jnp.sum(share * around[rows, there], axis=0, keepdims=True)

    def second_pass(block, carry):
        begin = pl.multiple_of(block * EB, EB)
        gather(0, begin)
        for i in range(NSUB):
            if i + 1 < NSUB:
                gather(i + 1, begin + (i + 1) * SB)
            second_middle(i, begin + i * SB)
        hot = hots[:, pl.ds(begin, EB)]
        both = jnp.concatenate([hot, hot], axis=1)
        for lo, hi in ((0, 288), (288, 576)):
            g_env[lo:hi, :] += dot_nt(terms[lo:hi, :], both)
        return carry

    lax.fori_loop(0, blocks, second_pass, 0)
    fields[:, 0:ATOM], fields[:, ATOM:] = halves(g_env[...] * ENV_SCALE)

    def third_middle(sub, begin):
        here = pl.ds(pl.multiple_of(begin, SB), SB)
        there = slice(sub * SB, (sub + 1) * SB)
        hot = hots[:, here]
        envelope = geo[ENVL : ENVL + 1, here]
        raw = paired[0:CH, here]
        weights = raw * envelope
        d_weight = None
        d_ang = [None]
        for m in range(9):
            got = around[m * CH : (m + 1) * CH, there]
            term = got if m == 0 else got * geo[ANG + m : ANG + m + 1, here]
            d_weight = term if m == 0 else d_weight + term
            if m:
                d_ang.append(
                    geo[DANG + m - 1 : DANG + m, here] + jnp.sum(weights * got, axis=0, keepdims=True)
                )
        e_raw = geo[ERAW : ERAW + 1, here]
        d_envelope = e_raw + jnp.sum(d_weight * raw, axis=0, keepdims=True)
        pair_high, pair_low = halves(
            jnp.concatenate([d_weight * envelope, d_value[:, here]], axis=0)
        )
        both_high = jnp.concatenate([pair_high, mixed[:, here]], axis=0)
        both_low = jnp.concatenate([pair_low, mixed_low[:, here]], axis=0)
        d_act = dot(dn_ref[...], jnp.concatenate([both_high, both_low, both_high], axis=0))
        d_act = d_act + ab_ref[:, 0:1] * envelope
        d_radial = dot(wr_ref[...], stacked(d_act * slope[:, here]))
        d_soft = jnp.sum(d_radial[0:8] * geo[DRAD : DRAD + 8, here], axis=0, keepdims=True)
        d_soft = d_soft + d_envelope * geo[DENVL : DENVL + 1, here]
        unit = geo[DIR : DIR + 3, here]
        rinv = geo[RINV : RINV + 1, here]
        ux, uy, uz = unit[0:1], unit[1:2], unit[2:3]
        d_ux = root3 * d_ang[1] + root15 * (uy * d_ang[4] + uz * d_ang[7] + ux * d_ang[8]) - root5 * ux * d_ang[6]
        d_uy = root3 * d_ang[2] + root15 * (ux * d_ang[4] + uz * d_ang[5] - uy * d_ang[8]) - root5 * uy * d_ang[6]
        d_uz = root3 * d_ang[3] + root15 * (uy * d_ang[5] + ux * d_ang[7]) + 2.0 * root5 * uz * d_ang[6]
        along = d_soft - (d_ux * ux + d_uy * uy + d_uz * uz) * rinv
        pull = [d * rinv + u * along for d, u in ((d_ux, ux), (d_uy, uy), (d_uz, uz))]
        energy = e_raw * envelope
        sent = jnp.concatenate([*pull, energy, jnp.zeros((4, SB), F32)], axis=0)
        sent = jnp.concatenate([sent, sent - sent.astype(BF16).astype(F32)], axis=0).astype(BF16)
        at_centre[...] += dot_nt(sent, hot)
        valid = begin + lax.broadcasted_iota(I32, (1, SB), 1) < total
        code = jnp.where(valid, edges[5:6, here], 0.0).astype(I32)
        seg = lax.broadcasted_iota(I32, (16, SB), 0) == (code >> 8)
        spread = jnp.concatenate([jnp.where(seg, g, 0.0) for g in pull], axis=0)
        high, low = halves(spread)
        hot_partner = one_hot(code & 255, ATOM)
        at_partner[...] += dot_nt(high, hot_partner) + dot_nt(low, hot_partner)

    def third_pass(block, carry):
        begin = pl.multiple_of(block * EB, EB)
        gather(0, begin)
        for i in range(NSUB):
            if i + 1 < NSUB:
                gather(i + 1, begin + (i + 1) * SB)
            third_middle(i, begin + i * SB)
        return carry

    lax.fori_loop(0, blocks, third_pass, 0)
    sums = at_centre[...]
    sums = sums[0:8] + sums[8:16]
    parts = at_partner[...]
    mine = [parts[16 * i : 16 * i + 1] for i in range(3)]
    force_ref[...] = sums[0:3] - jnp.concatenate(mine, axis=0)
    energy_ref[...] = sums[3:4]
    msg_ref[...] = jnp.zeros_like(msg_ref)
    for k in range(NBR):
        for i in range(3):
            msg_ref[k, i : i + 1, :] = parts[16 * i + 3 + k : 16 * i + 4 + k]
            ghost = parts[16 * i + 1 + k // 4 : 16 * i + 2 + k // 4]
            msg_ref[k, 3 + i : 4 + i, 0:GHOST] = ghost[:, (k % 4) * GHOST : (k % 4 + 1) * GHOST]


def return_kernel(msg_ref, force_ref, own_ref, out_ref, inbox, send_sem, recv_sem):
    barrier, peers = greet()
    sends = own_ref[10:11, 0:SLOTS].astype(I32)
    hot = one_hot(sends, ATOM)
    pl.semaphore_wait(barrier, NBR)
    copies = swap(peers, msg_ref, inbox, send_sem, recv_sem)
    for copy in copies:
        copy.wait()
    total = force_ref[...]
    for k in range(NBR):
        total = total - inbox[k, 0:3, :]
    ghosts = jnp.concatenate([inbox[k, 3:6, 0:GHOST] for k in range(NBR)], axis=1)
    split = jnp.concatenate([*thirds(ghosts), jnp.zeros((7, SLOTS), F32)], axis=0).astype(BF16)
    back = dot_nt(split, hot)
    out_ref[...] = total - joined(back)


def edge_call(*operands):
    shape = jax.ShapeDtypeStruct
    return pl.pallas_call(
        edge_kernel,
        out_shape=(
            shape((NBR, 8, ATOM), F32),
            shape((3, ATOM), F32),
            shape((1, ATOM), F32),
        ),
        in_specs=[VMEM] * 10,
        out_specs=[VMEM] * 3,
        scratch_shapes=[
            pltpu.VMEM((8, CAP + 512), F32),
            pltpu.VMEM((ATOM, CAP), BF16),
            pltpu.VMEM((2 * WIDTH, CAP), F32),
            pltpu.VMEM((WIDTH, CAP), F32),
            pltpu.VMEM((WIDTH, CAP), BF16),
            pltpu.VMEM((WIDTH, CAP), BF16),
            pltpu.VMEM((CH, CAP), F32),
            pltpu.VMEM((ROWS, CAP), F32),
            pltpu.VMEM((9 * CH, ATOM), F32),
            pltpu.VMEM((9 * CH, ATOM), F32),
            pltpu.VMEM((9 * CH, 2 * ATOM), BF16),
            pltpu.VMEM((9 * CH, 2 * EB), BF16),
            pltpu.VMEM((9 * CH, EB), F32),
            pltpu.VMEM((16, ATOM), F32),
            pltpu.VMEM((48, ATOM), F32),
        ],
        compiler_params=pltpu.CompilerParams(vmem_limit_bytes=48 << 20),
    )(*operands)


def per_device(
    positions, species, send_list, edge_src, edge_dst, edge_count,
    w_in, w_mid, w_pair, w_mix, w_back, w_read,
):
    sends = send_list[0]
    shape = jax.ShapeDtypeStruct
    shared = pl.pallas_call(
        share_kernel,
        out_shape=(
            shape((16, LIST), F32),
            shape((16, ATOM), BF16),
            shape((NBR, 8, LIST), F32),
            shape((WIDTH, 64), BF16),
            shape((2 * WIDTH, 3 * WIDTH), BF16),
            shape((WIDTH, 6 * WIDTH), BF16),
            shape((WIDTH, 9 * CH), BF16),
            shape((3 * CH, 3 * WIDTH), BF16),
            shape((16, 3 * WIDTH), BF16),
            shape((WIDTH, 2), F32),
        ),
        in_specs=[SMEM] + [HBM] * 11,
        out_specs=[VMEM] * 10,
        scratch_shapes=[
            pltpu.VMEM((3, ATOM), F32),
            pltpu.VMEM((1, ATOM), I32),
            pltpu.VMEM((NBR, GHOST), I32),
            pltpu.VMEM((1, PAIR), I32),
            pltpu.VMEM((1, PAIR), I32),
            pltpu.VMEM((2 * SPECIES + BASIS, WIDTH), F32),
            pltpu.VMEM((WIDTH, WIDTH), F32),
            pltpu.VMEM((WIDTH, WIDTH), F32),
            pltpu.VMEM((WIDTH + 3 * CH, WIDTH), F32),
            pltpu.VMEM((WIDTH, WIDTH), F32),
            pltpu.VMEM((1, WIDTH), F32),
            pltpu.VMEM((NBR, 8, LIST), F32),
            pltpu.VMEM((16, PAIR), F32),
            pltpu.SemaphoreType.DMA((11,)),
            pltpu.SemaphoreType.DMA((NBR,)),
            pltpu.SemaphoreType.DMA((NBR,)),
        ],
        compiler_params=pltpu.CompilerParams(
            collective_id=0, has_side_effects=True, vmem_limit_bytes=8 << 20
        ),
    )(
        edge_count,
        *(
            pltpu.with_memory_space_constraint(x, pltpu.HBM)
            for x in (
                positions, species.reshape(1, ATOM), sends, edge_src, edge_dst,
                w_in, w_mid, w_pair, w_mix, w_back, w_read.reshape(1, WIDTH),
            )
        ),
    )
    messages, force, energy = edge_call(*shared)
    forces = pl.pallas_call(
        return_kernel,
        out_shape=shape((3, ATOM), F32),
        in_specs=[VMEM] * 3,
        out_specs=VMEM,
        scratch_shapes=[
            pltpu.VMEM((NBR, 8, ATOM), F32),
            pltpu.SemaphoreType.DMA((NBR,)),
            pltpu.SemaphoreType.DMA((NBR,)),
        ],
        compiler_params=pltpu.CompilerParams(
            collective_id=1, has_side_effects=True, vmem_limit_bytes=4 << 20
        ),
    )(messages, force, shared[0])
    return forces, energy.reshape(ATOM)


def solution(mesh):
    both = ("dom", "face")
    placed = (
        P(None, both), P(both), P(both, None, None), P(both, None), P(both, None), P(both),
        P(), P(), P(), P(), P(), P(),
    )
    return jax.shard_map(
        per_device,
        mesh=mesh,
        in_specs=placed,
        out_specs=(P(None, both), P(both)),
        check_vma=False,
    )
```

```python
import functools

import jax
import jax.numpy as jnp
from jax import lax
from jax.experimental import pallas as pl
from jax.experimental.pallas import tpu as pltpu
from jax.sharding import PartitionSpec as P

CH = 64
WIDTH = 128
BASIS = 8
SPECIES = 7
ENV_SCALE = 0.2
CUTOFF = 6.0
PI = 3.141592653589793
DIRECTIONS = ((-1, -1), (-1, 0), (-1, 1), (0, -1), (0, 1), (1, -1), (1, 0), (1, 1))
NBR = 8
ATOM = 256
GHOST = 64
PAIR = 1024
SLOTS = NBR * GHOST
LIST = PAIR + 128
CAP = 10 * PAIR
MAIN = 2048
EXTRA = 512
F32 = jnp.float32
BF16 = jnp.bfloat16
I32 = jnp.int32
MESH = pl.DeviceIdType.MESH
VMEM = pl.BlockSpec(memory_space=pltpu.VMEM)
SMEM = pl.BlockSpec(memory_space=pltpu.SMEM)
HBM = pl.BlockSpec(memory_space=pltpu.HBM)

RAD, DRAD, ANG, ENVL, DENVL, RINV, DIR, ERAW, DANG, CODE, ROWS = 0, 8, 16, 25, 26, 27, 28, 31, 32, 40, 48
FIELD = 9 * CH
ROOT3, ROOT5, ROOT15 = 3.0**0.5, 5.0**0.5, 15.0**0.5
DEGREES = (0, 1, 1, 1, 2, 2, 2, 2, 2)


def dot(a, b):
    return lax.dot_general(a, b, (((1,), (0,)), ((), ())), preferred_element_type=F32)


def dot_nt(a, b):
    return lax.dot_general(a, b, (((1,), (1,)), ((), ())), preferred_element_type=F32)


def exact(a, b):
    return jnp.dot(a, b, precision=lax.Precision.HIGHEST, preferred_element_type=F32)


def halves(x):
    high = x.astype(BF16)
    return high, (x - high.astype(F32)).astype(BF16)


def thirds(x):
    high = x.astype(BF16).astype(F32)
    rest = x - high
    mid = rest.astype(BF16).astype(F32)
    return high, mid, rest - mid


def sigmoid(x):
    return 0.5 * jnp.tanh(0.5 * x) + 0.5


def triple(weight):
    high, low = halves(weight)
    return jnp.concatenate([high, high, low], axis=1)


def stacked(x):
    high, low = halves(x)
    return jnp.concatenate([high, low, high], axis=0)


def one_hot(row, count):
    rows = lax.broadcasted_iota(I32, (count, row.shape[1]), 0)
    return jnp.where(rows == row, 1.0, 0.0).astype(BF16)


def atom_table(coords, kinds):
    parts = thirds(coords)
    pad = jnp.zeros((6, coords.shape[1]), F32)
    return jnp.concatenate([*parts, kinds, pad], axis=0)


def joined(rows):
    return rows[0:3] + rows[3:6] + rows[6:9]


def greet():
    here = [lax.axis_index("dom"), lax.axis_index("face")]
    sizes = [lax.axis_size("dom"), lax.axis_size("face")]
    peers = []
    for shift in DIRECTIONS:
        peers.append(
            tuple(lax.rem(at + by + size, size) for at, by, size in zip(here, shift, sizes))
        )
    barrier = pltpu.get_barrier_semaphore()
    for peer in peers:
        pl.semaphore_signal(barrier, inc=1, device_id=peer, device_id_type=MESH)
    return barrier, peers


def swap(peers, out_ref, in_ref, send_sem, recv_sem):
    copies = []
    for k, peer in enumerate(peers):
        copies.append(
            pltpu.make_async_remote_copy(
                src_ref=out_ref.at[k],
                dst_ref=in_ref.at[NBR - 1 - k],
                send_sem=send_sem.at[k],
                recv_sem=recv_sem.at[NBR - 1 - k],
                device_id=peer,
                device_id_type=MESH,
            )
        )
    for copy in copies:
        copy.start()
    return copies


def share_kernel(
    count_ref, *refs,
):
    sources, refs = refs[:11], refs[11:]
    (
        own_ref, table_ref, recv_ref, wx_ref, up_ref, dn_ref, mt_ref, mb_ref, wr_ref, ab_ref, cols_ref,
    ) = refs[:11]
    held, refs = refs[11:22], refs[22:]
    out_buf, order_buf, load_sem, send_sem, recv_sem = refs
    (
        pos_ref, spec_ref, send_ref, src_ref, dst_ref,
        w_in_ref, w_mid_ref, w_pair_ref, w_mix_ref, w_back_ref, w_read_ref,
    ) = held
    loads = [
        pltpu.make_async_copy(source, target, load_sem.at[i])
        for i, (source, target) in enumerate(zip(sources, held))
    ]
    for load in loads:
        load.start()
    barrier, peers = greet()
    for load in loads[:5]:
        load.wait()
    table = atom_table(pos_ref[...], spec_ref[...].astype(F32)).astype(BF16)
    table_ref[...] = table
    sends = jnp.concatenate([send_ref[k : k + 1, :] for k in range(NBR)], axis=1)
    ghosts = dot(table, one_hot(sends, ATOM))
    ghost_rows = jnp.concatenate([joined(ghosts), ghosts[9:10]], axis=0)
    src = src_ref[...]
    dst = dst_ref[...]
    lanes = lax.broadcasted_iota(I32, (1, PAIR), 1)
    live = lanes < count_ref[0]
    ghost = dst >= ATOM
    away = dst - ATOM
    bucket = jnp.where(ghost, (away >> 6) + 1, 0)
    bucket = jnp.where(live, bucket, 15)
    place = jnp.where(ghost, away & 63, dst)
    member = jnp.where(lax.broadcasted_iota(I32, (16, PAIR), 0) == bucket, 1.0, 0.0)
    before = lax.broadcasted_iota(I32, (ATOM, ATOM), 0) < lax.broadcasted_iota(I32, (ATOM, ATOM), 1)
    before = jnp.where(before, 1.0, 0.0).astype(BF16)
    pieces = [member[:, i * ATOM : (i + 1) * ATOM] for i in range(PAIR // ATOM)]
    ranks = dot(jnp.concatenate(pieces, axis=0).astype(BF16), before)
    sums = [jnp.sum(piece, axis=1, keepdims=True) for piece in pieces]
    total = sums[0] + sums[1] + sums[2] + sums[3]
    start = jnp.zeros((16, 1), F32)
    index = lax.broadcasted_iota(I32, (16, 1), 0)
    for b in range(NBR + 1):
        start = start + jnp.where(index > b, total[b : b + 1, :], 0.0)
    offset = start
    spots = []
    for i, piece in enumerate(pieces):
        where = ranks[16 * i : 16 * (i + 1)] + offset
        spots.append(jnp.sum(piece * where, axis=0, keepdims=True))
        offset = offset + sums[i]
    spot = jnp.concatenate(spots, axis=1)
    spot = jnp.where(live, spot, -1.0).astype(I32)
    picked = dot(table, one_hot(src, ATOM))
    data = jnp.concatenate(
        [picked[0:10], place.astype(F32), src.astype(F32), jnp.zeros((4, PAIR), F32)], axis=0
    ).astype(BF16)
    for i in range(PAIR // ATOM):
        rows = lax.broadcasted_iota(I32, (ATOM, PAIR), 0) + i * ATOM
        chosen = jnp.where(rows == spot, 1.0, 0.0).astype(BF16)
        order_buf[:, i * ATOM : (i + 1) * ATOM] = dot_nt(data, chosen)
    ordered = order_buf[...]
    entries = jnp.concatenate(
        [joined(ordered), ordered[9:12], jnp.zeros((2, PAIR), F32)], axis=0
    )
    none = jnp.zeros((8, GHOST), F32)
    for k in range(NBR):
        out_buf[k, :, 0:PAIR] = entries
        mine = jnp.concatenate([ghost_rows[:, k * GHOST : (k + 1) * GHOST], none[0:4]], axis=0)
        out_buf[k, :, PAIR:LIST] = jnp.concatenate([mine, none], axis=1)
        out_buf[k, 4:5, PAIR:LIST] = jnp.broadcast_to(total[k + 1 : k + 2, :], (1, 128))
        out_buf[k, 5:6, PAIR:LIST] = jnp.broadcast_to(start[k + 1 : k + 2, :], (1, 128))
    pl.semaphore_wait(barrier, NBR)
    copies = swap(peers, out_buf, recv_ref, send_sem, recv_sem)
    own_ref[0:8, 0:PAIR] = entries
    own_ref[:, PAIR:LIST] = jnp.zeros((16, 128), F32)
    own_ref[8:9, 0:PAIR] = src.astype(F32)
    own_ref[9:10, 0:PAIR] = dst.astype(F32)
    own_ref[10:11, 0:SLOTS] = sends.astype(F32)
    cols_ref[...] = send_ref[...].astype(F32).T
    own_ref[11:12, PAIR:LIST] = jnp.full((1, 128), count_ref[0], I32).astype(F32)
    for load in loads[5:]:
        load.wait()
    own_ref[4:5, PAIR:LIST] = jnp.broadcast_to(total[0:1, :], (1, 128))
    w_in = w_in_ref[...]
    w_c = w_in[0:SPECIES].T
    w_p = w_in[SPECIES : 2 * SPECIES].T
    w_r = w_in[2 * SPECIES :]
    gap = jnp.zeros((WIDTH, 1), F32)
    first = jnp.concatenate([w_c, gap, w_p, gap, w_r.T], axis=1)
    first_high = first.astype(BF16).astype(F32)
    first_low = first - first_high
    wx_ref[...] = jnp.concatenate(
        [first_high, first_high[:, 16:24], first_low, jnp.zeros((WIDTH, 8), F32)], axis=1
    ).astype(BF16)
    wr_high, wr_low = halves(jnp.concatenate([w_r, jnp.zeros((8, WIDTH), F32)], axis=0))
    wr_ref[...] = jnp.concatenate([wr_high, wr_high, wr_low], axis=1)
    w_mid = w_mid_ref[...]
    w_read = w_read_ref[...]
    down = jnp.concatenate(
        [exact(w_mid, w_pair_ref[...]), exact(w_mid, w_mix_ref[0:WIDTH, :])], axis=1
    )
    a_col = jnp.sum(w_mid * w_read, axis=1, keepdims=True)
    b_col = jnp.sum(w_back_ref[...] * w_read, axis=1, keepdims=True)
    ab_ref[...] = jnp.concatenate([a_col, b_col], axis=1)
    dn_ref[...] = triple(down)
    up_ref[...] = triple(down.T)
    mix = jnp.concatenate(
        [w_mix_ref[pl.ds(WIDTH + degree, CH, stride=3), :] for degree in range(3)], axis=0
    )
    mb_ref[...] = triple(mix)
    mt_ref[...] = triple(mix.T)
    for copy in copies:
        copy.wait()


def gather(fields, hot, around):
    width = hot.shape[1]
    both = jnp.concatenate([hot, hot], axis=0)
    for lo, hi in ((0, 288), (288, FIELD)):
        around[lo:hi, 0:width] = dot(fields[lo:hi, :], both)


def scatter(terms, hot, total, count):
    width = hot.shape[1]
    both = jnp.concatenate([hot, hot], axis=1)
    for lo, hi in ((0, 288), (288, count)):
        total[lo:hi, :] += dot_nt(terms[lo:hi, 0 : 2 * width], both)


def third_pass(store, begin, width, fields, around, dn_ref, wr_ref, ab_ref):
    hots, slope, mixed, mixed_low, d_value, raw_ref, geo = store
    here = pl.ds(begin, width)
    gather(fields, hots[:, here], around)
    envelope = geo[ENVL : ENVL + 1, here]
    raw = raw_ref[:, here]
    weights = raw * envelope
    d_weight = None
    d_ang = [None]
    for m in range(9):
        got = around[m * CH : (m + 1) * CH, 0:width]
        term = got if m == 0 else got * geo[ANG + m : ANG + m + 1, here]
        d_weight = term if m == 0 else d_weight + term
        if m:
            d_ang.append(
                geo[DANG + m - 1 : DANG + m, here] + jnp.sum(weights * got, axis=0, keepdims=True)
            )
    d_envelope = geo[ERAW : ERAW + 1, here] + jnp.sum(d_weight * raw, axis=0, keepdims=True)
    pair_high, pair_low = halves(jnp.concatenate([d_weight * envelope, d_value[:, here]], axis=0))
    both_high = jnp.concatenate([pair_high, mixed[:, here]], axis=0)
    both_low = jnp.concatenate([pair_low, mixed_low[:, here]], axis=0)
    d_act = dot(dn_ref[...], jnp.concatenate([both_high, both_low, both_high], axis=0))
    d_act = d_act + ab_ref[:, 0:1] * envelope
    d_radial = dot(wr_ref[...], stacked(d_act * slope[:, here]))
    d_soft = jnp.sum(d_radial[0:8] * geo[DRAD : DRAD + 8, here], axis=0, keepdims=True)
    d_soft = d_soft + d_envelope * geo[DENVL : DENVL + 1, here]
    unit = geo[DIR : DIR + 3, here]
    rinv = geo[RINV : RINV + 1, here]
    ux, uy, uz = unit[0:1], unit[1:2], unit[2:3]
    d_ux = ROOT3 * d_ang[1] + ROOT15 * (uy * d_ang[4] + uz * d_ang[7] + ux * d_ang[8]) - ROOT5 * ux * d_ang[6]
    d_uy = ROOT3 * d_ang[2] + ROOT15 * (ux * d_ang[4] + uz * d_ang[5] - uy * d_ang[8]) - ROOT5 * uy * d_ang[6]
    d_uz = ROOT3 * d_ang[3] + ROOT15 * (uy * d_ang[5] + ux * d_ang[7]) + 2.0 * ROOT5 * uz * d_ang[6]
    along = d_soft - (d_ux * ux + d_uy * uy + d_uz * uz) * rinv
    return [d * rinv + u * along for d, u in ((d_ux, ux), (d_uy, uy), (d_uz, uz))]


def to_partners(pull, geo, begin, width, at_partner):
    code = geo[CODE : CODE + 1, pl.ds(begin, width)].astype(I32)
    seg = lax.broadcasted_iota(I32, (16, width), 0) == (code >> 8)
    high, low = halves(jnp.concatenate([jnp.where(seg, g, 0.0) for g in pull], axis=0))
    hot = one_hot(code & 255, ATOM)
    at_partner[...] += dot_nt(
        jnp.concatenate([high, low], axis=1), jnp.concatenate([hot, hot], axis=1)
    )


def to_centres(pull, hots, begin, width, at_centre):
    sent = jnp.concatenate([*pull, jnp.zeros((5, width), F32)], axis=0)
    sent = jnp.concatenate([sent, sent - sent.astype(BF16).astype(F32)], axis=0).astype(BF16)
    at_centre[...] += dot_nt(sent, hots[:, pl.ds(begin, width)])


def edge_kernel(
    own_ref, table_ref, recv_ref,
    wx_ref, up_ref, dn_ref, mt_ref, mb_ref, wr_ref, ab_ref, cols_ref,
    energy_ref, fields, at_centre, at_partner, hots, slope, mixed, mixed_low, d_value, raw, geo,
    edges, value, base, more_hots, more_slope, more_mixed, more_low, more_d_value, more_raw, more_geo,
    more_value, more_base, env, g_env, terms, around,
):
    first_store = (hots, slope, mixed, mixed_low, d_value, raw, geo, value, base)
    more_store = (
        more_hots, more_slope, more_mixed, more_low, more_d_value, more_raw, more_geo,
        more_value, more_base,
    )
    count = own_ref[11:12, PAIR : PAIR + 128][0, 0].astype(I32)
    src = own_ref[8:9, 0:PAIR]
    dst = own_ref[9:10, 0:PAIR].astype(I32)
    near = jnp.concatenate([recv_ref[k, 0:4, PAIR : PAIR + GHOST] for k in range(NBR)], axis=1)
    ghosts = atom_table(near[0:3], near[3:4]).astype(BF16)
    table = table_ref[...]
    segments = jnp.concatenate([table, ghosts[:, 0:ATOM], ghosts[:, ATOM:SLOTS]], axis=0)
    found = dot(segments, one_hot(dst & 255, ATOM))
    part = dst >> 8
    picked = jnp.where(part == 0, found[0:16], jnp.where(part == 1, found[16:32], found[32:48]))
    edges[:, 0:PAIR] = jnp.concatenate(
        [joined(picked), picked[9:10], src, dst.astype(F32), jnp.zeros((2, PAIR), F32)],
        axis=0,
    )
    lane = lax.broadcasted_iota(I32, (8, 128), 1)
    row = lax.broadcasted_iota(I32, (8, 128), 0)

    def place(ref, size, begin, at, k, tile):
        base = tile * 128 - at + begin
        first = base >> 7
        turn = base & 127
        low = jnp.clip(first, 0, 8)
        high = jnp.clip(first + 1, 0, 8)
        left = ref[0:8, pl.ds(pl.multiple_of(low * 128, 128), 128)]
        right = ref[0:8, pl.ds(pl.multiple_of(high * 128, 128), 128)]
        back = lax.rem(128 - turn, 128)
        taken = jnp.where(
            lane < 128 - turn, pltpu.roll(left, back, 1), pltpu.roll(right, back, 1)
        )
        if k is not None:
            match = lax.broadcasted_iota(I32, (GHOST, 128), 0) == taken[4:5].astype(I32)
            atom = jnp.sum(jnp.where(match, cols_ref[:, k : k + 1], 0.0), axis=0, keepdims=True)
            taken = jnp.where(row == 4, atom, taken)
            taken = jnp.where(row == 5, taken + F32(ATOM * (3 + k)), taken)
        here = pl.ds(pl.multiple_of(tile * 128, 128), 128)
        spot = tile * 128 + lane
        inside = (spot >= at) & (spot < at + size)
        edges[:, here] = jnp.where(inside, taken, edges[:, here])

    def scalar(ref, which):
        return ref[which : which + 1, PAIR : PAIR + 128][0, 0].astype(I32)

    at = count
    jobs = []
    size = scalar(own_ref, 4)
    jobs.append((own_ref, size, 0, at, None, 4))
    at = at + size
    for k in range(NBR):
        ref = recv_ref.at[k]
        size = scalar(ref, 4)
        jobs.append((ref, size, scalar(ref, 5), at, k, 2))
        at = at + size
    total = at
    for ref, size, begin, at, k, usual in jobs:
        for step in range(usual):
            place(ref, size, begin, at, k, (at >> 7) + step)
    for ref, size, begin, at, k, usual in jobs:
        last = (at + size + 127) >> 7

        def more(tile, carry, ref=ref, size=size, begin=begin, at=at, k=k):
            place(ref, size, begin, at, k, tile)
            return carry

        lax.fori_loop((at >> 7) + usual, last, more, 0)
    extra_blocks = lax.div(jnp.maximum(total - MAIN, 0) + EXTRA - 1, EXTRA)

    env[...] = jnp.zeros_like(env)
    g_env[...] = jnp.zeros_like(g_env)
    terms[FIELD:, :] = jnp.zeros((16, 2 * MAIN), BF16)
    at_centre[...] = jnp.zeros_like(at_centre)
    at_partner[...] = jnp.zeros_like(at_partner)

    def first_pass(store, begin, width, offset):
        hots, slope, _, _, _, raw, geo, value, base = store
        here = pl.ds(begin, width)
        valid = begin + offset + lax.broadcasted_iota(I32, (1, width), 1) < total
        part = jnp.where(valid, edges[:, pl.ds(begin + offset, width)], 0.0)
        hot = one_hot(part[4:5].astype(I32), ATOM)
        hots[:, here] = hot
        geo[CODE : CODE + 1, here] = part[5:6]
        held = dot(table, hot)
        delta = part[0:3] - joined(held)
        length2 = delta[0:1] * delta[0:1] + delta[1:2] * delta[1:2] + delta[2:3] * delta[2:3] + 1.0
        soft = jnp.sqrt(length2)
        rinv = 1.0 / soft
        unit = delta * rinv
        ux, uy, uz = unit[0:1], unit[1:2], unit[2:3]
        turn = soft * (PI / CUTOFF) - PI / 2
        t2 = turn * turn
        cosine = -turn * (
            1 + t2 * (-1 / 6 + t2 * (1 / 120 + t2 * (-1 / 5040 + t2 * (1 / 362880 - t2 / 39916800))))
        )
        sine = 1 + t2 * (
            -1 / 2 + t2 * (1 / 24 + t2 * (-1 / 720 + t2 * (1 / 40320 + t2 * (-1 / 3628800 + t2 / 479001600))))
        )
        twice = 2 * cosine
        s_old, s_now = jnp.zeros_like(sine), sine
        c_old, c_now = jnp.ones_like(sine), cosine
        for b in range(BASIS):
            geo[RAD + b : RAD + b + 1, here] = s_now * rinv
            geo[DRAD + b : DRAD + b + 1, here] = (c_now * ((b + 1) * PI / CUTOFF) - s_now * rinv) * rinv
            s_old, s_now = s_now, twice * s_now - s_old
            c_old, c_now = c_now, twice * c_now - c_old
        angular = [
            jnp.ones_like(ux),
            ROOT3 * ux,
            ROOT3 * uy,
            ROOT3 * uz,
            ROOT15 * ux * uy,
            ROOT15 * uy * uz,
            0.5 * ROOT5 * (2.0 * uz * uz - ux * ux - uy * uy),
            ROOT15 * ux * uz,
            0.5 * ROOT15 * (ux * ux - uy * uy),
        ]
        for m in range(9):
            geo[ANG + m : ANG + m + 1, here] = angular[m]
        inner = 1.0 - length2 * (1.0 / (CUTOFF * CUTOFF))
        alive = jnp.where(valid, 1.0, 0.0)
        envelope = alive * inner * inner
        geo[ENVL : ENVL + 1, here] = envelope
        geo[DENVL : DENVL + 1, here] = alive * inner * soft * (-4.0 / (CUTOFF * CUTOFF))
        geo[RINV : RINV + 1, here] = rinv
        geo[DIR : DIR + 3, here] = unit
        radial = geo[RAD : RAD + 8, here]
        radial_low = radial - radial.astype(BF16).astype(F32)
        kinds = lax.broadcasted_iota(I32, (8, width), 0)
        hot_c = jnp.where(kinds == held[9:10].astype(I32), 1.0, 0.0)
        hot_p = jnp.where(kinds == part[3:4].astype(I32), 1.0, 0.0)
        inputs = jnp.concatenate(
            [hot_c, hot_p, radial, radial_low, hot_c, hot_p, radial, jnp.zeros((8, width), F32)], axis=0
        ).astype(BF16)
        pre = dot(wx_ref[...], inputs)
        gate = sigmoid(pre)
        act = pre * gate
        slope[:, here] = gate + act * (1.0 - gate)
        after = dot(up_ref[...], stacked(act))
        raw[:, here] = after[0:CH]
        value[:, here] = after[CH : 2 * CH]
        base[:, here] = after[2 * CH :]
        geo[ERAW : ERAW + 1, here] = jnp.sum(act * ab_ref[:, 0:1], axis=0, keepdims=True)
        weights = after[0:CH] * envelope
        for m in range(9):
            term = weights if m == 0 else weights * angular[m]
            rows = slice(m * CH, (m + 1) * CH)
            terms[rows, 0:width], terms[rows, width : 2 * width] = halves(term)
        scatter(terms, hot, env, FIELD)

    def second_pass(store, begin, width):
        hots, _, mixed, mixed_low, d_value, _, geo, value, base = store
        here = pl.ds(begin, width)
        hot = hots[:, here]
        gather(fields, hot, around)
        envelope = geo[ENVL : ENVL + 1, here]
        sums = [None, None, None]
        for m in range(9):
            got = around[m * CH : (m + 1) * CH, 0:width]
            term = got if m == 0 else got * geo[ANG + m : ANG + m + 1, here]
            degree = DEGREES[m]
            sums[degree] = term if sums[degree] is None else sums[degree] + term
        held = value[:, here]
        invariant = jnp.concatenate([s * held for s in sums], axis=0)
        pre = base[:, here] + dot(mt_ref[...], stacked(invariant))
        gate = sigmoid(pre)
        act = pre * gate
        back = ab_ref[:, 1:2]
        e_raw = geo[ERAW : ERAW + 1, here] + jnp.sum(act * back, axis=0, keepdims=True)
        geo[ERAW : ERAW + 1, here] = e_raw
        energy = e_raw * envelope
        energy = jnp.concatenate([energy, jnp.zeros((15, width), F32)], axis=0)
        terms[FIELD:, 0:width], terms[FIELD:, width : 2 * width] = halves(energy)
        d_pre = (gate + act * (1.0 - gate)) * back * envelope
        d_high, d_low = halves(d_pre)
        mixed[:, here] = d_high
        mixed_low[:, here] = d_low
        d_inv = dot(mb_ref[...], jnp.concatenate([d_high, d_low, d_high], axis=0))
        d_inv = [d_inv[i * CH : (i + 1) * CH] for i in range(3)]
        d_value[:, here] = d_inv[0] * sums[0] + d_inv[1] * sums[1] + d_inv[2] * sums[2]
        d_sum = [d * held for d in d_inv]
        for m in range(9):
            share = d_sum[DEGREES[m]]
            term = share if m == 0 else share * geo[ANG + m : ANG + m + 1, here]
            rows = slice(m * CH, (m + 1) * CH)
            terms[rows, 0:width], terms[rows, width : 2 * width] = halves(term)
            if m:
                geo[DANG + m - 1 : DANG + m, here] = jnp.sum(
                    share * around[rows, 0:width], axis=0, keepdims=True
                )
        scatter(terms, hot, g_env, FIELD + 16)

    def rest(step):
        def body(block, carry):
            step(pl.multiple_of(block * EXTRA, EXTRA))
            return carry

        lax.fori_loop(0, extra_blocks, body, 0)

    first_pass(first_store, 0, MAIN, 0)
    rest(lambda begin: first_pass(more_store, begin, EXTRA, MAIN))
    fields[:, 0:ATOM], fields[:, ATOM:] = halves(env[...] * ENV_SCALE)
    second_pass(first_store, 0, MAIN)
    rest(lambda begin: second_pass(more_store, begin, EXTRA))
    energy_ref[...] = g_env[FIELD : FIELD + 1, :]
    fields[:, 0:ATOM], fields[:, ATOM:] = halves(g_env[0:FIELD, :] * ENV_SCALE)

    def third(begin):
        pull = third_pass(
            (more_hots, more_slope, more_mixed, more_low, more_d_value, more_raw, more_geo),
            begin, EXTRA, fields, around, dn_ref, wr_ref, ab_ref,
        )
        to_partners(pull, more_geo, begin, EXTRA, at_partner)
        to_centres(pull, more_hots, begin, EXTRA, at_centre)

    rest(third)


def return_kernel(
    own_ref, dn_ref, wr_ref, ab_ref,
    fields, more_centre, more_partner, hots, slope, mixed, mixed_low, d_value, raw, geo,
    out_ref, outbox, inbox, around, at_centre, at_partner, send_sem, recv_sem,
):
    barrier, peers = greet()
    at_centre[...] = more_centre[...]
    at_partner[...] = more_partner[...]
    store = (hots, slope, mixed, mixed_low, d_value, raw, geo)
    pull = third_pass(store, 0, MAIN, fields, around, dn_ref, wr_ref, ab_ref)
    to_partners(pull, geo, 0, MAIN, at_partner)
    parts = at_partner[...]
    outbox[...] = jnp.zeros_like(outbox)
    for k in range(NBR):
        for i in range(3):
            outbox[k, i : i + 1, :] = parts[16 * i + 3 + k : 16 * i + 4 + k]
            ghost = parts[16 * i + 1 + k // 4 : 16 * i + 2 + k // 4]
            outbox[k, 3 + i : 4 + i, 0:GHOST] = ghost[:, (k % 4) * GHOST : (k % 4 + 1) * GHOST]
    pl.semaphore_wait(barrier, NBR)
    copies = swap(peers, outbox, inbox, send_sem, recv_sem)
    to_centres(pull, hots, 0, MAIN, at_centre)
    sends = own_ref[10:11, 0:SLOTS].astype(I32)
    hot = one_hot(sends, ATOM)
    sums = at_centre[...]
    total = sums[0:3] + sums[8:11]
    total = total - jnp.concatenate([parts[16 * i : 16 * i + 1] for i in range(3)], axis=0)
    for copy in copies:
        copy.wait()
    for k in range(NBR):
        total = total - inbox[k, 0:3, :]
    ghosts = jnp.concatenate([inbox[k, 3:6, 0:GHOST] for k in range(NBR)], axis=1)
    split = jnp.concatenate([*thirds(ghosts), jnp.zeros((7, SLOTS), F32)], axis=0).astype(BF16)
    back = dot_nt(split, hot)
    out_ref[...] = total - joined(back)


def edge_call(*operands):
    shape = jax.ShapeDtypeStruct
    rest = CAP - MAIN

    def store(lanes, make):
        return [
            make((ATOM, lanes), BF16),
            make((WIDTH, lanes), F32),
            make((WIDTH, lanes), BF16),
            make((WIDTH, lanes), BF16),
            make((CH, lanes), F32),
            make((CH, lanes), F32),
            make((ROWS, lanes), F32),
        ]

    return pl.pallas_call(
        edge_kernel,
        out_shape=(
            shape((1, ATOM), F32),
            shape((FIELD, 2 * ATOM), BF16),
            shape((16, ATOM), F32),
            shape((48, ATOM), F32),
            *store(MAIN, shape),
        ),
        in_specs=[VMEM] * 11,
        out_specs=[VMEM] * 11,
        scratch_shapes=[
            pltpu.VMEM((8, CAP + 512), F32),
            pltpu.VMEM((CH, MAIN), F32),
            pltpu.VMEM((WIDTH, MAIN), F32),
            *store(rest, pltpu.VMEM),
            pltpu.VMEM((CH, rest), F32),
            pltpu.VMEM((WIDTH, rest), F32),
            pltpu.VMEM((FIELD, ATOM), F32),
            pltpu.VMEM((FIELD + 16, ATOM), F32),
            pltpu.VMEM((FIELD + 16, 2 * MAIN), BF16),
            pltpu.VMEM((FIELD, MAIN), F32),
        ],
        compiler_params=pltpu.CompilerParams(vmem_limit_bytes=46 << 20),
    )(*operands)


def per_device(
    positions, species, send_list, edge_src, edge_dst, edge_count,
    w_in, w_mid, w_pair, w_mix, w_back, w_read,
):
    sends = send_list[0]
    shape = jax.ShapeDtypeStruct
    shared = pl.pallas_call(
        share_kernel,
        out_shape=(
            shape((16, LIST), F32),
            shape((16, ATOM), BF16),
            shape((NBR, 8, LIST), F32),
            shape((WIDTH, 64), BF16),
            shape((2 * WIDTH, 3 * WIDTH), BF16),
            shape((WIDTH, 6 * WIDTH), BF16),
            shape((WIDTH, 9 * CH), BF16),
            shape((3 * CH, 3 * WIDTH), BF16),
            shape((16, 3 * WIDTH), BF16),
            shape((WIDTH, 2), F32),
            shape((GHOST, NBR), F32),
        ),
        in_specs=[SMEM] + [HBM] * 11,
        out_specs=[VMEM] * 11,
        scratch_shapes=[
            pltpu.VMEM((3, ATOM), F32),
            pltpu.VMEM((1, ATOM), I32),
            pltpu.VMEM((NBR, GHOST), I32),
            pltpu.VMEM((1, PAIR), I32),
            pltpu.VMEM((1, PAIR), I32),
            pltpu.VMEM((2 * SPECIES + BASIS, WIDTH), F32),
            pltpu.VMEM((WIDTH, WIDTH), F32),
            pltpu.VMEM((WIDTH, WIDTH), F32),
            pltpu.VMEM((WIDTH + 3 * CH, WIDTH), F32),
            pltpu.VMEM((WIDTH, WIDTH), F32),
            pltpu.VMEM((1, WIDTH), F32),
            pltpu.VMEM((NBR, 8, LIST), F32),
            pltpu.VMEM((16, PAIR), F32),
            pltpu.SemaphoreType.DMA((11,)),
            pltpu.SemaphoreType.DMA((NBR,)),
            pltpu.SemaphoreType.DMA((NBR,)),
        ],
        compiler_params=pltpu.CompilerParams(
            collective_id=0, has_side_effects=True, vmem_limit_bytes=8 << 20
        ),
    )(
        edge_count,
        *(
            pltpu.with_memory_space_constraint(x, pltpu.HBM)
            for x in (
                positions, species.reshape(1, ATOM), sends, edge_src, edge_dst,
                w_in, w_mid, w_pair, w_mix, w_back, w_read.reshape(1, WIDTH),
            )
        ),
    )
    energy, *kept = edge_call(*shared)
    own, dn, wr, ab = shared[0], shared[5], shared[8], shared[9]
    forces = pl.pallas_call(
        return_kernel,
        out_shape=shape((3, ATOM), F32),
        in_specs=[VMEM] * 14,
        out_specs=VMEM,
        scratch_shapes=[
            pltpu.VMEM((NBR, 8, ATOM), F32),
            pltpu.VMEM((NBR, 8, ATOM), F32),
            pltpu.VMEM((FIELD, MAIN), F32),
            pltpu.VMEM((16, ATOM), F32),
            pltpu.VMEM((48, ATOM), F32),
            pltpu.SemaphoreType.DMA((NBR,)),
            pltpu.SemaphoreType.DMA((NBR,)),
        ],
        compiler_params=pltpu.CompilerParams(
            collective_id=1, has_side_effects=True, vmem_limit_bytes=20 << 20
        ),
    )(own, dn, wr, ab, *kept)
    return forces, energy.reshape(ATOM)


def solution(mesh):
    both = ("dom", "face")
    placed = (
        P(None, both), P(both), P(both, None, None), P(both, None), P(both, None), P(both),
        P(), P(), P(), P(), P(), P(),
    )
    return jax.shard_map(
        per_device,
        mesh=mesh,
        in_specs=placed,
        out_specs=(P(None, both), P(both)),
        check_vma=False,
    )
```

```python
import functools

import jax
import jax.numpy as jnp
from jax import lax
from jax.experimental import pallas as pl
from jax.experimental.pallas import tpu as pltpu
from jax.sharding import PartitionSpec as P

CH = 64
WIDTH = 128
BASIS = 8
SPECIES = 7
ENV_SCALE = 0.2
CUTOFF = 6.0
PI = 3.141592653589793
DIRECTIONS = ((-1, -1), (-1, 0), (-1, 1), (0, -1), (0, 1), (1, -1), (1, 0), (1, 1))
NBR = 8
ATOM = 256
GHOST = 64
PAIR = 1024
SLOTS = NBR * GHOST
LIST = 512
CAP = 10 * PAIR
MAIN = 2048
EXTRA = 512
F32 = jnp.float32
BF16 = jnp.bfloat16
I32 = jnp.int32
MESH = pl.DeviceIdType.MESH
VMEM = pl.BlockSpec(memory_space=pltpu.VMEM)
SMEM = pl.BlockSpec(memory_space=pltpu.SMEM)
HBM = pl.BlockSpec(memory_space=pltpu.HBM)

RAD, DRAD, ANG, ENVL, DENVL, RINV, DIR, ERAW, DANG, CODE, ROWS = 0, 8, 16, 25, 26, 27, 28, 31, 32, 40, 48
FIELD = 9 * CH
ROOT3, ROOT5, ROOT15 = 3.0**0.5, 5.0**0.5, 15.0**0.5
DEGREES = (0, 1, 1, 1, 2, 2, 2, 2, 2)


def dot(a, b):
    return lax.dot_general(a, b, (((1,), (0,)), ((), ())), preferred_element_type=F32)


def dot_nt(a, b):
    return lax.dot_general(a, b, (((1,), (1,)), ((), ())), preferred_element_type=F32)


def exact(a, b):
    return jnp.dot(a, b, precision=lax.Precision.HIGHEST, preferred_element_type=F32)


def halves(x):
    high = x.astype(BF16)
    return high, (x - high.astype(F32)).astype(BF16)


def thirds(x):
    high = x.astype(BF16).astype(F32)
    rest = x - high
    mid = rest.astype(BF16).astype(F32)
    return high, mid, rest - mid


def sigmoid(x):
    return 0.5 * jnp.tanh(0.5 * x) + 0.5


def triple(weight):
    high, low = halves(weight)
    return jnp.concatenate([high, high, low], axis=1)


def stacked(x):
    high, low = halves(x)
    return jnp.concatenate([high, low, high], axis=0)


def one_hot(row, count):
    rows = lax.broadcasted_iota(I32, (count, row.shape[1]), 0)
    return jnp.where(rows == row, 1.0, 0.0).astype(BF16)


def atom_table(coords, kinds):
    parts = thirds(coords)
    pad = jnp.zeros((6, coords.shape[1]), F32)
    return jnp.concatenate([*parts, kinds, pad], axis=0)


def joined(rows):
    return rows[0:3] + rows[3:6] + rows[6:9]


def greet():
    here = [lax.axis_index("dom"), lax.axis_index("face")]
    sizes = [lax.axis_size("dom"), lax.axis_size("face")]
    peers = []
    for shift in DIRECTIONS:
        peers.append(
            tuple(lax.rem(at + by + size, size) for at, by, size in zip(here, shift, sizes))
        )
    barrier = pltpu.get_barrier_semaphore()
    for peer in peers:
        pl.semaphore_signal(barrier, inc=1, device_id=peer, device_id_type=MESH)
    return barrier, peers


def swap(peers, out_ref, in_ref, send_sem, recv_sem):
    copies = []
    for k, peer in enumerate(peers):
        copies.append(
            pltpu.make_async_remote_copy(
                src_ref=out_ref.at[k],
                dst_ref=in_ref.at[NBR - 1 - k],
                send_sem=send_sem.at[k],
                recv_sem=recv_sem.at[NBR - 1 - k],
                device_id=peer,
                device_id_type=MESH,
            )
        )
    for copy in copies:
        copy.start()
    return copies


def share_kernel(
    count_ref, *refs,
):
    sources, refs = refs[:11], refs[11:]
    (
        own_ref, table_ref, recv_ref, wx_ref, up_ref, dn_ref, mt_ref, mb_ref, wr_ref, ab_ref, cols_ref,
        home_ref,
    ) = refs[:12]
    held, refs = refs[12:23], refs[23:]
    out_buf, order_buf, load_sem, send_sem, recv_sem = refs
    (
        pos_ref, spec_ref, send_ref, src_ref, dst_ref,
        w_in_ref, w_mid_ref, w_pair_ref, w_mix_ref, w_back_ref, w_read_ref,
    ) = held
    loads = [
        pltpu.make_async_copy(source, target, load_sem.at[i])
        for i, (source, target) in enumerate(zip(sources, held))
    ]
    for load in loads:
        load.start()
    barrier, peers = greet()
    for load in loads[:5]:
        load.wait()
    table = atom_table(pos_ref[...], spec_ref[...].astype(F32)).astype(BF16)
    table_ref[...] = table
    sends = jnp.concatenate([send_ref[k : k + 1, :] for k in range(NBR)], axis=1)
    ghosts = dot(table, one_hot(sends, ATOM))
    ghost_rows = jnp.concatenate([joined(ghosts), ghosts[9:10]], axis=0)
    src = src_ref[...]
    dst = dst_ref[...]
    lanes = lax.broadcasted_iota(I32, (1, PAIR), 1)
    live = lanes < count_ref[0]
    ghost = dst >= ATOM
    away = dst - ATOM
    bucket = jnp.where(ghost, (away >> 6) + 1, 0)
    bucket = jnp.where(live, bucket, 15)
    place = jnp.where(ghost, away & 63, dst)
    member = jnp.where(lax.broadcasted_iota(I32, (16, PAIR), 0) == bucket, 1.0, 0.0)
    before = lax.broadcasted_iota(I32, (ATOM, ATOM), 0) < lax.broadcasted_iota(I32, (ATOM, ATOM), 1)
    before = jnp.where(before, 1.0, 0.0).astype(BF16)
    pieces = [member[:, i * ATOM : (i + 1) * ATOM] for i in range(PAIR // ATOM)]
    ranks = dot(jnp.concatenate(pieces, axis=0).astype(BF16), before)
    sums = [jnp.sum(piece, axis=1, keepdims=True) for piece in pieces]
    total = sums[0] + sums[1] + sums[2] + sums[3]
    start = jnp.zeros((16, 1), F32)
    index = lax.broadcasted_iota(I32, (16, 1), 0)
    for b in range(NBR + 1):
        start = start + jnp.where(index > b, total[b : b + 1, :], 0.0)
    offset = start
    spots = []
    for i, piece in enumerate(pieces):
        where = ranks[16 * i : 16 * (i + 1)] + offset
        spots.append(jnp.sum(piece * where, axis=0, keepdims=True))
        offset = offset + sums[i]
    spot = jnp.concatenate(spots, axis=1)
    spot = jnp.where(live, spot, -1.0).astype(I32)
    data = jnp.concatenate(
        [place.astype(F32), src.astype(F32), jnp.zeros((14, PAIR), F32)], axis=0
    ).astype(BF16)
    for i in range(PAIR // ATOM):
        rows = lax.broadcasted_iota(I32, (ATOM, PAIR), 0) + i * ATOM
        chosen = jnp.where(rows == spot, 1.0, 0.0).astype(BF16)
        ordered = dot_nt(data, chosen)
        for j in range(2):
            for half in range(2):
                order_buf[2 * i + half : 2 * i + half + 1, j * 128 : (j + 1) * 128] = ordered[
                    j : j + 1, half * 128 : (half + 1) * 128
                ]
    atoms = jnp.concatenate([pos_ref[...], spec_ref[...].astype(F32)], axis=0)
    for i in range(4):
        for half in range(2):
            order_buf[2 * i + half : 2 * i + half + 1, 256:384] = atoms[
                i : i + 1, half * 128 : (half + 1) * 128
            ]
    entries = order_buf[...]
    none = jnp.zeros((8, GHOST), F32)
    indices = sends.astype(F32)
    for k in range(NBR):
        out_buf[k, :, 0:384] = entries
        part = slice(k * GHOST, (k + 1) * GHOST)
        mine = jnp.concatenate([ghost_rows[:, part], none[0:2], indices[:, part], none[0:1]], axis=0)
        out_buf[k, :, 384:LIST] = jnp.concatenate([mine, none], axis=1)
        out_buf[k, 4:5, 384:LIST] = jnp.broadcast_to(total[k + 1 : k + 2, :], (1, 128))
        out_buf[k, 5:6, 384:LIST] = jnp.broadcast_to(start[k + 1 : k + 2, :], (1, 128))
    pl.semaphore_wait(barrier, NBR)
    copies = swap(peers, out_buf, recv_ref, send_sem, recv_sem)
    home_ref[:, 0:384] = entries
    home_ref[:, 384:LIST] = jnp.zeros((8, 128), F32)
    home_ref[4:5, 384:LIST] = jnp.broadcast_to(total[0:1, :], (1, 128))
    own_ref[0:1, :] = src.astype(F32)
    own_ref[1:2, :] = dst.astype(F32)
    own_ref[2:3, :] = jnp.full((1, PAIR), count_ref[0], I32).astype(F32)
    cols_ref[...] = send_ref[...].astype(F32).T
    for load in loads[5:]:
        load.wait()
    w_in = w_in_ref[...]
    w_c = w_in[0:SPECIES].T
    w_p = w_in[SPECIES : 2 * SPECIES].T
    w_r = w_in[2 * SPECIES :]
    gap = jnp.zeros((WIDTH, 1), F32)
    first = jnp.concatenate([w_c, gap, w_p, gap, w_r.T], axis=1)
    first_high = first.astype(BF16).astype(F32)
    first_low = first - first_high
    wx_ref[...] = jnp.concatenate(
        [first_high, first_high[:, 16:24], first_low, jnp.zeros((WIDTH, 8), F32)], axis=1
    ).astype(BF16)
    wr_high, wr_low = halves(jnp.concatenate([w_r, jnp.zeros((8, WIDTH), F32)], axis=0))
    wr_ref[...] = jnp.concatenate([wr_high, wr_high, wr_low], axis=1)
    w_mid = w_mid_ref[...]
    w_read = w_read_ref[...]
    down = jnp.concatenate(
        [exact(w_mid, w_pair_ref[...]), exact(w_mid, w_mix_ref[0:WIDTH, :])], axis=1
    )
    a_col = jnp.sum(w_mid * w_read, axis=1, keepdims=True)
    b_col = jnp.sum(w_back_ref[...] * w_read, axis=1, keepdims=True)
    ab_ref[...] = jnp.concatenate([a_col, b_col], axis=1)
    dn_ref[...] = triple(down)
    up_ref[...] = triple(down.T)
    mix = jnp.concatenate(
        [w_mix_ref[pl.ds(WIDTH + degree, CH, stride=3), :] for degree in range(3)], axis=0
    )
    mb_ref[...] = triple(mix)
    mt_ref[...] = triple(mix.T)
    for copy in copies:
        copy.wait()


def gather(fields, hot, around):
    width = hot.shape[1]
    both = jnp.concatenate([hot, hot], axis=0)
    for lo, hi in ((0, 288), (288, FIELD)):
        around[lo:hi, 0:width] = dot(fields[lo:hi, :], both)


def scatter(terms, hot, total, count):
    width = hot.shape[1]
    both = jnp.concatenate([hot, hot], axis=1)
    for lo, hi in ((0, 288), (288, count)):
        total[lo:hi, :] += dot_nt(terms[lo:hi, 0 : 2 * width], both)


def third_pass(store, begin, width, fields, around, dn_ref, wr_ref, ab_ref):
    hots, slope, mixed, mixed_low, d_value, raw_ref, geo = store
    here = pl.ds(begin, width)
    gather(fields, hots[:, here], around)
    envelope = geo[ENVL : ENVL + 1, here]
    raw = raw_ref[:, here]
    weights = raw * envelope
    d_weight = None
    d_ang = [None]
    for m in range(9):
        got = around[m * CH : (m + 1) * CH, 0:width]
        term = got if m == 0 else got * geo[ANG + m : ANG + m + 1, here]
        d_weight = term if m == 0 else d_weight + term
        if m:
            d_ang.append(
                geo[DANG + m - 1 : DANG + m, here] + jnp.sum(weights * got, axis=0, keepdims=True)
            )
    d_envelope = geo[ERAW : ERAW + 1, here] + jnp.sum(d_weight * raw, axis=0, keepdims=True)
    pair_high, pair_low = halves(jnp.concatenate([d_weight * envelope, d_value[:, here]], axis=0))
    both_high = jnp.concatenate([pair_high, mixed[:, here]], axis=0)
    both_low = jnp.concatenate([pair_low, mixed_low[:, here]], axis=0)
    d_act = dot(dn_ref[...], jnp.concatenate([both_high, both_low, both_high], axis=0))
    d_act = d_act + ab_ref[:, 0:1] * envelope
    d_radial = dot(wr_ref[...], stacked(d_act * slope[:, here]))
    d_soft = jnp.sum(d_radial[0:8] * geo[DRAD : DRAD + 8, here], axis=0, keepdims=True)
    d_soft = d_soft + d_envelope * geo[DENVL : DENVL + 1, here]
    unit = geo[DIR : DIR + 3, here]
    rinv = geo[RINV : RINV + 1, here]
    ux, uy, uz = unit[0:1], unit[1:2], unit[2:3]
    d_ux = ROOT3 * d_ang[1] + ROOT15 * (uy * d_ang[4] + uz * d_ang[7] + ux * d_ang[8]) - ROOT5 * ux * d_ang[6]
    d_uy = ROOT3 * d_ang[2] + ROOT15 * (ux * d_ang[4] + uz * d_ang[5] - uy * d_ang[8]) - ROOT5 * uy * d_ang[6]
    d_uz = ROOT3 * d_ang[3] + ROOT15 * (uy * d_ang[5] + ux * d_ang[7]) + 2.0 * ROOT5 * uz * d_ang[6]
    along = d_soft - (d_ux * ux + d_uy * uy + d_uz * uz) * rinv
    return [d * rinv + u * along for d, u in ((d_ux, ux), (d_uy, uy), (d_uz, uz))]


def to_partners(pull, geo, begin, width, at_partner):
    code = geo[CODE : CODE + 1, pl.ds(begin, width)].astype(I32)
    seg = lax.broadcasted_iota(I32, (16, width), 0) == (code >> 8)
    high, low = halves(jnp.concatenate([jnp.where(seg, g, 0.0) for g in pull], axis=0))
    hot = one_hot(code & 255, ATOM)
    at_partner[...] += dot_nt(
        jnp.concatenate([high, low], axis=1), jnp.concatenate([hot, hot], axis=1)
    )


def to_centres(pull, hots, begin, width, at_centre):
    sent = jnp.concatenate([*pull, jnp.zeros((5, width), F32)], axis=0)
    sent = jnp.concatenate([sent, sent - sent.astype(BF16).astype(F32)], axis=0).astype(BF16)
    at_centre[...] += dot_nt(sent, hots[:, pl.ds(begin, width)])


def edge_kernel(
    own_ref, table_ref, recv_ref,
    wx_ref, up_ref, dn_ref, mt_ref, mb_ref, wr_ref, ab_ref, cols_ref, home_ref,
    energy_ref, fields, at_centre, at_partner, hots, slope, mixed, mixed_low, d_value, raw, geo,
    edges, base, more_hots, more_slope, more_mixed, more_low, more_d_value, more_raw, more_geo,
    more_base, env, g_env, terms, around, lines,
):
    first_store = (hots, slope, mixed, mixed_low, d_value, raw, geo, base)
    more_store = (
        more_hots, more_slope, more_mixed, more_low, more_d_value, more_raw, more_geo,
        more_base,
    )
    count = own_ref[2:3, 0:128][0, 0].astype(I32)
    src = own_ref[0:1, :]
    dst = own_ref[1:2, :].astype(I32)
    near = jnp.concatenate([recv_ref[k, :, 384 : 384 + GHOST] for k in range(NBR)], axis=1)
    ghosts = jnp.concatenate(
        [*thirds(near[0:3]), near[3:4], near[6:7], jnp.zeros((5, SLOTS), F32)], axis=0
    ).astype(BF16)
    table = table_ref[...]
    segments = jnp.concatenate([table, ghosts[:, 0:ATOM], ghosts[:, ATOM:SLOTS]], axis=0)
    found = dot(segments, one_hot(dst & 255, ATOM))
    part = dst >> 8
    picked = jnp.where(part == 0, found[0:16], jnp.where(part == 1, found[16:32], found[32:48]))
    beyond = (((dst - ATOM) >> 6) + 3).astype(F32) * ATOM + picked[10:11]
    code = jnp.where(part == 0, dst.astype(F32), beyond)
    edges[:, 0:PAIR] = jnp.concatenate(
        [joined(picked), picked[9:10], src, code, jnp.zeros((2, PAIR), F32)], axis=0
    )
    lane = lax.broadcasted_iota(I32, (8, 128), 1)
    row = lax.broadcasted_iota(I32, (8, 128), 0)

    def kept(ref):
        halves_of = [
            jnp.concatenate([ref[2 * i : 2 * i + 1, 256:384], ref[2 * i + 1 : 2 * i + 2, 256:384]], axis=1)
            for i in range(4)
        ]
        return atom_table(jnp.concatenate(halves_of[0:3], axis=0), halves_of[3]).astype(BF16)

    def place(ref, size, begin, at, k, held, tile):
        base = tile * 128 - at + begin
        first = base >> 7
        turn = base & 127
        low = jnp.clip(first, 0, 7)
        high = jnp.clip(first + 1, 0, 7)
        which = NBR if k is None else k
        left, right = lines[which, low], lines[which, high]
        back = lax.rem(128 - turn, 128)
        taken = jnp.where(
            lane < 128 - turn, pltpu.roll(left, back, 1), pltpu.roll(right, back, 1)
        )
        found = dot(held, one_hot(taken[5:6].astype(I32), ATOM))
        partner = jnp.concatenate([joined(found), found[9:10], jnp.zeros((4, 128), F32)], axis=0)
        if k is not None:
            match = lax.broadcasted_iota(I32, (GHOST, 128), 0) == taken[4:5].astype(I32)
            atom = jnp.sum(jnp.where(match, cols_ref[:, k : k + 1], 0.0), axis=0, keepdims=True)
            taken = jnp.where(row == 4, atom, taken + F32(ATOM * (3 + k)))
        taken = jnp.where(row < 4, partner, taken)
        here = pl.ds(pl.multiple_of(tile * 128, 128), 128)
        spot = tile * 128 + lane
        inside = (spot >= at) & (spot < at + size)
        edges[:, here] = jnp.where(inside, taken, edges[:, here])

    def scalar(ref, which):
        return ref[which : which + 1, 384:LIST][0, 0].astype(I32)

    for k, ref in enumerate([recv_ref.at[k] for k in range(NBR)] + [home_ref]):
        for i in range(PAIR // 128):
            lines[k, i] = jnp.where(row == 4, ref[i : i + 1, 0:128], ref[i : i + 1, 128:256])
    at = count
    jobs = []
    size = scalar(home_ref, 4)
    jobs.append((home_ref, size, 0, at, None, kept(home_ref), 4))
    at = at + size
    for k in range(NBR):
        ref = recv_ref.at[k]
        size = scalar(ref, 4)
        jobs.append((ref, size, scalar(ref, 5), at, k, kept(ref), 2))
        at = at + size
    total = at
    for ref, size, begin, at, k, held, usual in jobs:
        for step in range(usual):
            place(ref, size, begin, at, k, held, (at >> 7) + step)
    for ref, size, begin, at, k, held, usual in jobs:
        last = (at + size + 127) >> 7

        def more(tile, carry, ref=ref, size=size, begin=begin, at=at, k=k, held=held):
            place(ref, size, begin, at, k, held, tile)
            return carry

        lax.fori_loop((at >> 7) + usual, last, more, 0)
    extra_blocks = lax.div(jnp.maximum(total - MAIN, 0) + EXTRA - 1, EXTRA)

    env[...] = jnp.zeros_like(env)
    g_env[...] = jnp.zeros_like(g_env)
    terms[FIELD:, :] = jnp.zeros((16, 2 * MAIN), BF16)
    at_centre[...] = jnp.zeros_like(at_centre)
    at_partner[...] = jnp.zeros_like(at_partner)

    def first_pass(store, begin, width, offset):
        hots, slope, _, _, value, raw, geo, base = store
        here = pl.ds(begin, width)
        valid = begin + offset + lax.broadcasted_iota(I32, (1, width), 1) < total
        part = jnp.where(valid, edges[:, pl.ds(begin + offset, width)], 0.0)
        hot = one_hot(part[4:5].astype(I32), ATOM)
        hots[:, here] = hot
        geo[CODE : CODE + 1, here] = part[5:6]
        held = dot(table, hot)
        delta = part[0:3] - joined(held)
        length2 = delta[0:1] * delta[0:1] + delta[1:2] * delta[1:2] + delta[2:3] * delta[2:3] + 1.0
        soft = jnp.sqrt(length2)
        rinv = 1.0 / soft
        unit = delta * rinv
        ux, uy, uz = unit[0:1], unit[1:2], unit[2:3]
        turn = soft * (PI / CUTOFF) - PI / 2
        t2 = turn * turn
        cosine = -turn * (
            1 + t2 * (-1 / 6 + t2 * (1 / 120 + t2 * (-1 / 5040 + t2 * (1 / 362880 - t2 / 39916800))))
        )
        sine = 1 + t2 * (
            -1 / 2 + t2 * (1 / 24 + t2 * (-1 / 720 + t2 * (1 / 40320 + t2 * (-1 / 3628800 + t2 / 479001600))))
        )
        twice = 2 * cosine
        s_old, s_now = jnp.zeros_like(sine), sine
        c_old, c_now = jnp.ones_like(sine), cosine
        for b in range(BASIS):
            geo[RAD + b : RAD + b + 1, here] = s_now * rinv
            geo[DRAD + b : DRAD + b + 1, here] = (c_now * ((b + 1) * PI / CUTOFF) - s_now * rinv) * rinv
            s_old, s_now = s_now, twice * s_now - s_old
            c_old, c_now = c_now, twice * c_now - c_old
        angular = [
            jnp.ones_like(ux),
            ROOT3 * ux,
            ROOT3 * uy,
            ROOT3 * uz,
            ROOT15 * ux * uy,
            ROOT15 * uy * uz,
            0.5 * ROOT5 * (2.0 * uz * uz - ux * ux - uy * uy),
            ROOT15 * ux * uz,
            0.5 * ROOT15 * (ux * ux - uy * uy),
        ]
        for m in range(9):
            geo[ANG + m : ANG + m + 1, here] = angular[m]
        inner = 1.0 - length2 * (1.0 / (CUTOFF * CUTOFF))
        alive = jnp.where(valid, 1.0, 0.0)
        envelope = alive * inner * inner
        geo[ENVL : ENVL + 1, here] = envelope
        geo[DENVL : DENVL + 1, here] = alive * inner * soft * (-4.0 / (CUTOFF * CUTOFF))
        geo[RINV : RINV + 1, here] = rinv
        geo[DIR : DIR + 3, here] = unit
        radial = geo[RAD : RAD + 8, here]
        radial_low = radial - radial.astype(BF16).astype(F32)
        kinds = lax.broadcasted_iota(I32, (8, width), 0)
        hot_c = jnp.where(kinds == held[9:10].astype(I32), 1.0, 0.0)
        hot_p = jnp.where(kinds == part[3:4].astype(I32), 1.0, 0.0)
        inputs = jnp.concatenate(
            [hot_c, hot_p, radial, radial_low, hot_c, hot_p, radial, jnp.zeros((8, width), F32)], axis=0
        ).astype(BF16)
        pre = dot(wx_ref[...], inputs)
        gate = sigmoid(pre)
        act = pre * gate
        slope[:, here] = gate + act * (1.0 - gate)
        after = dot(up_ref[...], stacked(act))
        raw[:, here] = after[0:CH]
        value[:, here] = after[CH : 2 * CH]
        base[:, here] = after[2 * CH :]
        geo[ERAW : ERAW + 1, here] = jnp.sum(act * ab_ref[:, 0:1], axis=0, keepdims=True)
        weights = after[0:CH] * envelope
        for m in range(9):
            term = weights if m == 0 else weights * angular[m]
            rows = slice(m * CH, (m + 1) * CH)
            terms[rows, 0:width], terms[rows, width : 2 * width] = halves(term)
        scatter(terms, hot, env, FIELD)

    def second_pass(store, begin, width):
        hots, _, mixed, mixed_low, value, _, geo, base = store
        here = pl.ds(begin, width)
        hot = hots[:, here]
        gather(fields, hot, around)
        envelope = geo[ENVL : ENVL + 1, here]
        sums = [None, None, None]
        for m in range(9):
            got = around[m * CH : (m + 1) * CH, 0:width]
            term = got if m == 0 else got * geo[ANG + m : ANG + m + 1, here]
            degree = DEGREES[m]
            sums[degree] = term if sums[degree] is None else sums[degree] + term
        held = value[:, here]
        invariant = jnp.concatenate([s * held for s in sums], axis=0)
        pre = base[:, here] + dot(mt_ref[...], stacked(invariant))
        gate = sigmoid(pre)
        act = pre * gate
        back = ab_ref[:, 1:2]
        e_raw = geo[ERAW : ERAW + 1, here] + jnp.sum(act * back, axis=0, keepdims=True)
        geo[ERAW : ERAW + 1, here] = e_raw
        energy = e_raw * envelope
        energy = jnp.concatenate([energy, jnp.zeros((15, width), F32)], axis=0)
        terms[FIELD:, 0:width], terms[FIELD:, width : 2 * width] = halves(energy)
        d_pre = (gate + act * (1.0 - gate)) * back * envelope
        d_high, d_low = halves(d_pre)
        mixed[:, here] = d_high
        mixed_low[:, here] = d_low
        d_inv = dot(mb_ref[...], jnp.concatenate([d_high, d_low, d_high], axis=0))
        d_inv = [d_inv[i * CH : (i + 1) * CH] for i in range(3)]
        value[:, here] = d_inv[0] * sums[0] + d_inv[1] * sums[1] + d_inv[2] * sums[2]
        d_sum = [d * held for d in d_inv]
        for m in range(9):
            share = d_sum[DEGREES[m]]
            term = share if m == 0 else share * geo[ANG + m : ANG + m + 1, here]
            rows = slice(m * CH, (m + 1) * CH)
            terms[rows, 0:width], terms[rows, width : 2 * width] = halves(term)
            if m:
                geo[DANG + m - 1 : DANG + m, here] = jnp.sum(
                    share * around[rows, 0:width], axis=0, keepdims=True
                )
        scatter(terms, hot, g_env, FIELD + 16)

    def rest(step):
        def body(block, carry):
            step(pl.multiple_of(block * EXTRA, EXTRA))
            return carry

        lax.fori_loop(0, extra_blocks, body, 0)

    first_pass(first_store, 0, MAIN, 0)
    rest(lambda begin: first_pass(more_store, begin, EXTRA, MAIN))
    fields[:, 0:ATOM], fields[:, ATOM:] = halves(env[...] * ENV_SCALE)
    second_pass(first_store, 0, MAIN)
    rest(lambda begin: second_pass(more_store, begin, EXTRA))
    energy_ref[...] = g_env[FIELD : FIELD + 1, :]
    fields[:, 0:ATOM], fields[:, ATOM:] = halves(g_env[0:FIELD, :] * ENV_SCALE)

    def third(begin):
        pull = third_pass(
            (more_hots, more_slope, more_mixed, more_low, more_d_value, more_raw, more_geo),
            begin, EXTRA, fields, around, dn_ref, wr_ref, ab_ref,
        )
        to_partners(pull, more_geo, begin, EXTRA, at_partner)
        to_centres(pull, more_hots, begin, EXTRA, at_centre)

    rest(third)


def return_kernel(
    dn_ref, wr_ref, ab_ref,
    fields, more_centre, more_partner, hots, slope, mixed, mixed_low, d_value, raw, geo,
    out_ref, outbox, inbox, around, at_centre, at_partner, send_sem, recv_sem,
):
    barrier, peers = greet()
    at_centre[...] = more_centre[...]
    at_partner[...] = more_partner[...]
    store = (hots, slope, mixed, mixed_low, d_value, raw, geo)
    pull = third_pass(store, 0, MAIN, fields, around, dn_ref, wr_ref, ab_ref)
    to_partners(pull, geo, 0, MAIN, at_partner)
    parts = at_partner[...]
    for k in range(NBR):
        for i in range(3):
            for half in range(2):
                outbox[k, 3 * half + i : 3 * half + i + 1, :] = parts[
                    16 * i + 3 + k : 16 * i + 4 + k, half * 128 : (half + 1) * 128
                ]
        outbox[k, 6:8, :] = jnp.zeros((2, 128), F32)
    pl.semaphore_wait(barrier, NBR)
    copies = swap(peers, outbox, inbox, send_sem, recv_sem)
    to_centres(pull, hots, 0, MAIN, at_centre)
    sums = at_centre[...]
    total = sums[0:3] + sums[8:11]
    total = total - jnp.concatenate([parts[16 * i : 16 * i + 1] for i in range(3)], axis=0)
    for copy in copies:
        copy.wait()
    arrived = inbox[0]
    for k in range(1, NBR):
        arrived = arrived + inbox[k]
    out_ref[...] = total - jnp.concatenate([arrived[0:3], arrived[3:6]], axis=1)


def edge_call(*operands):
    shape = jax.ShapeDtypeStruct
    rest = CAP - MAIN

    def store(lanes, make):
        return [
            make((ATOM, lanes), BF16),
            make((WIDTH, lanes), F32),
            make((WIDTH, lanes), BF16),
            make((WIDTH, lanes), BF16),
            make((CH, lanes), F32),
            make((CH, lanes), F32),
            make((ROWS, lanes), F32),
        ]

    return pl.pallas_call(
        edge_kernel,
        out_shape=(
            shape((1, ATOM), F32),
            shape((FIELD, 2 * ATOM), BF16),
            shape((16, ATOM), F32),
            shape((48, ATOM), F32),
            *store(MAIN, shape),
        ),
        in_specs=[VMEM] * 12,
        out_specs=[VMEM] * 11,
        scratch_shapes=[
            pltpu.VMEM((8, CAP + 512), F32),
            pltpu.VMEM((WIDTH, MAIN), F32),
            *store(rest, pltpu.VMEM),
            pltpu.VMEM((WIDTH, rest), F32),
            pltpu.VMEM((FIELD, ATOM), F32),
            pltpu.VMEM((FIELD + 16, ATOM), F32),
            pltpu.VMEM((FIELD + 16, 2 * MAIN), BF16),
            pltpu.VMEM((FIELD, MAIN), F32),
            pltpu.VMEM((NBR + 1, PAIR // 128, 8, 128), F32),
        ],
        compiler_params=pltpu.CompilerParams(vmem_limit_bytes=46 << 20),
    )(*operands)


def per_device(
    positions, species, send_list, edge_src, edge_dst, edge_count,
    w_in, w_mid, w_pair, w_mix, w_back, w_read,
):
    sends = send_list[0]
    shape = jax.ShapeDtypeStruct
    shared = pl.pallas_call(
        share_kernel,
        out_shape=(
            shape((8, PAIR), F32),
            shape((16, ATOM), BF16),
            shape((NBR, 8, LIST), F32),
            shape((WIDTH, 64), BF16),
            shape((2 * WIDTH, 3 * WIDTH), BF16),
            shape((WIDTH, 6 * WIDTH), BF16),
            shape((WIDTH, 9 * CH), BF16),
            shape((3 * CH, 3 * WIDTH), BF16),
            shape((16, 3 * WIDTH), BF16),
            shape((WIDTH, 2), F32),
            shape((GHOST, NBR), F32),
            shape((8, LIST), F32),
        ),
        in_specs=[SMEM] + [HBM] * 11,
        out_specs=[VMEM] * 12,
        scratch_shapes=[
            pltpu.VMEM((3, ATOM), F32),
            pltpu.VMEM((1, ATOM), I32),
            pltpu.VMEM((NBR, GHOST), I32),
            pltpu.VMEM((1, PAIR), I32),
            pltpu.VMEM((1, PAIR), I32),
            pltpu.VMEM((2 * SPECIES + BASIS, WIDTH), F32),
            pltpu.VMEM((WIDTH, WIDTH), F32),
            pltpu.VMEM((WIDTH, WIDTH), F32),
            pltpu.VMEM((WIDTH + 3 * CH, WIDTH), F32),
            pltpu.VMEM((WIDTH, WIDTH), F32),
            pltpu.VMEM((1, WIDTH), F32),
            pltpu.VMEM((NBR, 8, LIST), F32),
            pltpu.VMEM((8, 384), F32),
            pltpu.SemaphoreType.DMA((11,)),
            pltpu.SemaphoreType.DMA((NBR,)),
            pltpu.SemaphoreType.DMA((NBR,)),
        ],
        compiler_params=pltpu.CompilerParams(
            collective_id=0, has_side_effects=True, vmem_limit_bytes=8 << 20
        ),
    )(
        edge_count,
        *(
            pltpu.with_memory_space_constraint(x, pltpu.HBM)
            for x in (
                positions, species.reshape(1, ATOM), sends, edge_src, edge_dst,
                w_in, w_mid, w_pair, w_mix, w_back, w_read.reshape(1, WIDTH),
            )
        ),
    )
    energy, *kept = edge_call(*shared)
    dn, wr, ab = shared[5], shared[8], shared[9]
    forces = pl.pallas_call(
        return_kernel,
        out_shape=shape((3, ATOM), F32),
        in_specs=[VMEM] * 13,
        out_specs=VMEM,
        scratch_shapes=[
            pltpu.VMEM((NBR, 8, 128), F32),
            pltpu.VMEM((NBR, 8, 128), F32),
            pltpu.VMEM((FIELD, MAIN), F32),
            pltpu.VMEM((16, ATOM), F32),
            pltpu.VMEM((48, ATOM), F32),
            pltpu.SemaphoreType.DMA((NBR,)),
            pltpu.SemaphoreType.DMA((NBR,)),
        ],
        compiler_params=pltpu.CompilerParams(
            collective_id=1, has_side_effects=True, vmem_limit_bytes=20 << 20
        ),
    )(dn, wr, ab, *kept)
    return forces, energy.reshape(ATOM)


def solution(mesh):
    both = ("dom", "face")
    placed = (
        P(None, both), P(both), P(both, None, None), P(both, None), P(both, None), P(both),
        P(), P(), P(), P(), P(), P(),
    )
    return jax.shard_map(
        per_device,
        mesh=mesh,
        in_specs=placed,
        out_specs=(P(None, both), P(both)),
        check_vma=False,
    )
```

```python
import functools

import jax
import jax.numpy as jnp
from jax import lax
from jax.experimental import pallas as pl
from jax.experimental.pallas import tpu as pltpu
from jax.sharding import PartitionSpec as P

CH = 64
WIDTH = 128
BASIS = 8
SPECIES = 7
ENV_SCALE = 0.2
CUTOFF = 6.0
PI = 3.141592653589793
DIRECTIONS = ((-1, -1), (-1, 0), (-1, 1), (0, -1), (0, 1), (1, -1), (1, 0), (1, 1))
NBR = 8
ATOM = 256
GHOST = 64
PAIR = 1024
SLOTS = NBR * GHOST
LIST = 512
CAP = 10 * PAIR
MAIN = 2048
EXTRA = 512
F32 = jnp.float32
BF16 = jnp.bfloat16
I32 = jnp.int32
MESH = pl.DeviceIdType.MESH
VMEM = pl.BlockSpec(memory_space=pltpu.VMEM)
SMEM = pl.BlockSpec(memory_space=pltpu.SMEM)
HBM = pl.BlockSpec(memory_space=pltpu.HBM)

RAD, DRAD, ANG, ENVL, DENVL, RINV, DIR, ERAW, DANG, CODE, ROWS = 0, 8, 16, 25, 26, 27, 28, 31, 32, 40, 48
FIELD = 9 * CH
ROOT3, ROOT5, ROOT15 = 3.0**0.5, 5.0**0.5, 15.0**0.5
DEGREES = (0, 1, 1, 1, 2, 2, 2, 2, 2)


def dot(a, b):
    return lax.dot_general(a, b, (((1,), (0,)), ((), ())), preferred_element_type=F32)


def dot_nt(a, b):
    return lax.dot_general(a, b, (((1,), (1,)), ((), ())), preferred_element_type=F32)


def exact(a, b):
    return jnp.dot(a, b, precision=lax.Precision.HIGHEST, preferred_element_type=F32)


def halves(x):
    high = x.astype(BF16)
    return high, (x - high.astype(F32)).astype(BF16)


def thirds(x):
    high = x.astype(BF16).astype(F32)
    rest = x - high
    mid = rest.astype(BF16).astype(F32)
    return high, mid, rest - mid


def sigmoid(x):
    return 0.5 * jnp.tanh(0.5 * x) + 0.5


def triple(weight):
    high, low = halves(weight)
    return jnp.concatenate([high, high, low], axis=1)


def stacked(x):
    high, low = halves(x)
    return jnp.concatenate([high, low, high], axis=0)


def one_hot(row, count):
    rows = lax.broadcasted_iota(I32, (count, row.shape[1]), 0).astype(F32).astype(BF16)
    match = rows == row.astype(F32).astype(BF16)
    return jnp.where(match, jnp.ones_like(rows), jnp.zeros_like(rows))


def atom_table(coords, kinds):
    parts = thirds(coords)
    pad = jnp.zeros((6, coords.shape[1]), F32)
    return jnp.concatenate([*parts, kinds, pad], axis=0)


def joined(rows):
    return rows[0:3] + rows[3:6] + rows[6:9]


def greet():
    here = [lax.axis_index("dom"), lax.axis_index("face")]
    sizes = [lax.axis_size("dom"), lax.axis_size("face")]
    peers = []
    for shift in DIRECTIONS:
        peers.append(
            tuple(lax.rem(at + by + size, size) for at, by, size in zip(here, shift, sizes))
        )
    barrier = pltpu.get_barrier_semaphore()
    for peer in peers:
        pl.semaphore_signal(barrier, inc=1, device_id=peer, device_id_type=MESH)
    return barrier, peers


def swap(peers, out_ref, in_ref, send_sem, recv_sem):
    copies = []
    for k, peer in enumerate(peers):
        copies.append(
            pltpu.make_async_remote_copy(
                src_ref=out_ref.at[k],
                dst_ref=in_ref.at[NBR - 1 - k],
                send_sem=send_sem.at[k],
                recv_sem=recv_sem.at[NBR - 1 - k],
                device_id=peer,
                device_id_type=MESH,
            )
        )
    for copy in copies:
        copy.start()
    return copies


def share_kernel(
    count_ref, *refs,
):
    sources, refs = refs[:11], refs[11:]
    (
        own_ref, table_ref, recv_ref, wx_ref, up_ref, dn_ref, mt_ref, mb_ref, wr_ref, ab_ref, cols_ref,
        home_ref,
    ) = refs[:12]
    held, refs = refs[12:23], refs[23:]
    out_buf, order_buf, load_sem, send_sem, recv_sem = refs
    (
        pos_ref, spec_ref, send_ref, src_ref, dst_ref,
        w_in_ref, w_mid_ref, w_pair_ref, w_mix_ref, w_back_ref, w_read_ref,
    ) = held
    loads = [
        pltpu.make_async_copy(source, target, load_sem.at[i])
        for i, (source, target) in enumerate(zip(sources, held))
    ]
    for load in loads:
        load.start()
    barrier, peers = greet()
    for load in loads[:5]:
        load.wait()
    table = atom_table(pos_ref[...], spec_ref[...].astype(F32)).astype(BF16)
    table_ref[...] = table
    sends = jnp.concatenate([send_ref[k : k + 1, :] for k in range(NBR)], axis=1)
    ghosts = dot(table, one_hot(sends, ATOM))
    ghost_rows = jnp.concatenate([joined(ghosts), ghosts[9:10]], axis=0)
    src = src_ref[...]
    dst = dst_ref[...]
    lanes = lax.broadcasted_iota(I32, (1, PAIR), 1)
    live = lanes < count_ref[0]
    ghost = dst >= ATOM
    away = dst - ATOM
    bucket = jnp.where(ghost, (away >> 6) + 1, 0)
    bucket = jnp.where(live, bucket, 15)
    place = jnp.where(ghost, away & 63, dst)
    member = jnp.where(lax.broadcasted_iota(I32, (16, PAIR), 0) == bucket, 1.0, 0.0)
    before = lax.broadcasted_iota(I32, (ATOM, ATOM), 0) < lax.broadcasted_iota(I32, (ATOM, ATOM), 1)
    before = jnp.where(before, 1.0, 0.0).astype(BF16)
    pieces = [member[:, i * ATOM : (i + 1) * ATOM] for i in range(PAIR // ATOM)]
    ranks = dot(jnp.concatenate(pieces, axis=0).astype(BF16), before)
    sums = [jnp.sum(piece, axis=1, keepdims=True) for piece in pieces]
    total = sums[0] + sums[1] + sums[2] + sums[3]
    start = jnp.zeros((16, 1), F32)
    index = lax.broadcasted_iota(I32, (16, 1), 0)
    for b in range(NBR + 1):
        start = start + jnp.where(index > b, total[b : b + 1, :], 0.0)
    offset = start
    spots = []
    for i, piece in enumerate(pieces):
        where = ranks[16 * i : 16 * (i + 1)] + offset
        spots.append(jnp.sum(piece * where, axis=0, keepdims=True))
        offset = offset + sums[i]
    spot = jnp.concatenate(spots, axis=1)
    spot = jnp.where(live, spot, -1.0).astype(I32)
    data = jnp.concatenate(
        [place.astype(F32), src.astype(F32), jnp.zeros((14, PAIR), F32)], axis=0
    ).astype(BF16)
    for i in range(PAIR // ATOM):
        rows = lax.broadcasted_iota(I32, (ATOM, PAIR), 0) + i * ATOM
        chosen = jnp.where(rows == spot, 1.0, 0.0).astype(BF16)
        ordered = dot_nt(data, chosen)
        for j in range(2):
            for half in range(2):
                order_buf[2 * i + half : 2 * i + half + 1, j * 128 : (j + 1) * 128] = ordered[
                    j : j + 1, half * 128 : (half + 1) * 128
                ]
    atoms = jnp.concatenate([pos_ref[...], spec_ref[...].astype(F32)], axis=0)
    for i in range(4):
        for half in range(2):
            order_buf[2 * i + half : 2 * i + half + 1, 256:384] = atoms[
                i : i + 1, half * 128 : (half + 1) * 128
            ]
    entries = order_buf[...]
    none = jnp.zeros((8, GHOST), F32)
    indices = sends.astype(F32)
    for k in range(NBR):
        out_buf[k, :, 0:384] = entries
        part = slice(k * GHOST, (k + 1) * GHOST)
        mine = jnp.concatenate([ghost_rows[:, part], none[0:2], indices[:, part], none[0:1]], axis=0)
        out_buf[k, :, 384:LIST] = jnp.concatenate([mine, none], axis=1)
        out_buf[k, 4:5, 384:LIST] = jnp.broadcast_to(total[k + 1 : k + 2, :], (1, 128))
        out_buf[k, 5:6, 384:LIST] = jnp.broadcast_to(start[k + 1 : k + 2, :], (1, 128))
    pl.semaphore_wait(barrier, NBR)
    copies = swap(peers, out_buf, recv_ref, send_sem, recv_sem)
    home_ref[:, 0:384] = entries
    home_ref[:, 384:LIST] = jnp.zeros((8, 128), F32)
    home_ref[4:5, 384:LIST] = jnp.broadcast_to(total[0:1, :], (1, 128))
    own_ref[0:1, :] = src.astype(F32)
    own_ref[1:2, :] = dst.astype(F32)
    own_ref[2:3, :] = jnp.full((1, PAIR), count_ref[0], I32).astype(F32)
    cols_ref[...] = send_ref[...].astype(F32).T
    for load in loads[5:]:
        load.wait()
    w_in = w_in_ref[...]
    w_c = w_in[0:SPECIES].T
    w_p = w_in[SPECIES : 2 * SPECIES].T
    w_r = w_in[2 * SPECIES :]
    gap = jnp.zeros((WIDTH, 1), F32)
    first = jnp.concatenate([w_c, gap, w_p, gap, w_r.T], axis=1)
    first_high = first.astype(BF16).astype(F32)
    first_low = first - first_high
    wx_ref[...] = jnp.concatenate(
        [first_high, first_high[:, 16:24], first_low, jnp.zeros((WIDTH, 8), F32)], axis=1
    ).astype(BF16)
    wr_high, wr_low = halves(jnp.concatenate([w_r, jnp.zeros((8, WIDTH), F32)], axis=0))
    wr_ref[...] = jnp.concatenate([wr_high, wr_high, wr_low], axis=1)
    w_mid = w_mid_ref[...]
    w_read = w_read_ref[...]
    down = jnp.concatenate(
        [exact(w_mid, w_pair_ref[...]), exact(w_mid, w_mix_ref[0:WIDTH, :])], axis=1
    )
    a_col = jnp.sum(w_mid * w_read, axis=1, keepdims=True)
    b_col = jnp.sum(w_back_ref[...] * w_read, axis=1, keepdims=True)
    ab_ref[...] = jnp.concatenate([a_col, b_col], axis=1)
    dn_ref[...] = triple(down)
    up_ref[...] = triple(down.T)
    mix = jnp.concatenate(
        [w_mix_ref[pl.ds(WIDTH + degree, CH, stride=3), :] for degree in range(3)], axis=0
    )
    mb_ref[...] = triple(mix)
    mt_ref[...] = triple(mix.T)
    for copy in copies:
        copy.wait()


def gather(fields, hot, around):
    width = hot.shape[1]
    around[:, 0:width] = dot(fields[...], jnp.concatenate([hot, hot], axis=0))


def scatter(terms, hot, total, count):
    width = hot.shape[1]
    for part in (slice(0, width), slice(width, 2 * width)):
        total[0:count, :] += dot_nt(terms[0:count, part], hot)


def third_pass(store, begin, width, fields, around, dn_ref, wr_ref, ab_ref):
    hots, slope, mixed, mixed_low, d_value, raw_ref, geo = store
    here = pl.ds(begin, width)
    gather(fields, hots[:, here], around)
    envelope = geo[ENVL : ENVL + 1, here]
    raw = raw_ref[:, here]
    weights = raw * envelope
    d_weight = None
    d_ang = [None]
    for m in range(9):
        got = around[m * CH : (m + 1) * CH, 0:width]
        term = got if m == 0 else got * geo[ANG + m : ANG + m + 1, here]
        d_weight = term if m == 0 else d_weight + term
        if m:
            d_ang.append(
                geo[DANG + m - 1 : DANG + m, here] + jnp.sum(weights * got, axis=0, keepdims=True)
            )
    d_envelope = geo[ERAW : ERAW + 1, here] + jnp.sum(d_weight * raw, axis=0, keepdims=True)
    pair_high, pair_low = halves(jnp.concatenate([d_weight * envelope, d_value[:, here]], axis=0))
    both_high = jnp.concatenate([pair_high, mixed[:, here]], axis=0)
    both_low = jnp.concatenate([pair_low, mixed_low[:, here]], axis=0)
    d_act = dot(dn_ref[...], jnp.concatenate([both_high, both_low, both_high], axis=0))
    d_act = d_act + ab_ref[:, 0:1] * envelope
    d_radial = dot(wr_ref[...], stacked(d_act * slope[:, here]))
    d_soft = jnp.sum(d_radial[0:8] * geo[DRAD : DRAD + 8, here], axis=0, keepdims=True)
    d_soft = d_soft + d_envelope * geo[DENVL : DENVL + 1, here]
    unit = geo[DIR : DIR + 3, here]
    rinv = geo[RINV : RINV + 1, here]
    ux, uy, uz = unit[0:1], unit[1:2], unit[2:3]
    d_ux = ROOT3 * d_ang[1] + ROOT15 * (uy * d_ang[4] + uz * d_ang[7] + ux * d_ang[8]) - ROOT5 * ux * d_ang[6]
    d_uy = ROOT3 * d_ang[2] + ROOT15 * (ux * d_ang[4] + uz * d_ang[5] - uy * d_ang[8]) - ROOT5 * uy * d_ang[6]
    d_uz = ROOT3 * d_ang[3] + ROOT15 * (uy * d_ang[5] + ux * d_ang[7]) + 2.0 * ROOT5 * uz * d_ang[6]
    along = d_soft - (d_ux * ux + d_uy * uy + d_uz * uz) * rinv
    return [d * rinv + u * along for d, u in ((d_ux, ux), (d_uy, uy), (d_uz, uz))]


def to_partners(pull, geo, begin, width, at_partner):
    code = geo[CODE : CODE + 1, pl.ds(begin, width)].astype(I32)
    seg = lax.broadcasted_iota(I32, (16, width), 0) == (code >> 8)
    high, low = halves(jnp.concatenate([jnp.where(seg, g, 0.0) for g in pull], axis=0))
    hot = one_hot(code & 255, ATOM)
    sums = dot_nt(jnp.concatenate([high, low], axis=0), hot)
    at_partner[...] += sums[0:48] + sums[48:96]


def to_centres(pull, hots, begin, width, at_centre):
    sent = jnp.concatenate([*pull, jnp.zeros((5, width), F32)], axis=0)
    sent = jnp.concatenate([sent, sent - sent.astype(BF16).astype(F32)], axis=0).astype(BF16)
    at_centre[...] += dot_nt(sent, hots[:, pl.ds(begin, width)])


def edge_kernel(
    own_ref, table_ref, recv_ref,
    wx_ref, up_ref, dn_ref, mt_ref, mb_ref, wr_ref, ab_ref, cols_ref, home_ref,
    energy_ref, fields, at_centre, at_partner, hots, slope, mixed, mixed_low, d_value, raw, geo,
    edges, base, more_hots, more_slope, more_mixed, more_low, more_d_value, more_raw, more_geo,
    more_base, env, g_env, terms, around, lines,
):
    first_store = (hots, slope, mixed, mixed_low, d_value, raw, geo, base)
    more_store = (
        more_hots, more_slope, more_mixed, more_low, more_d_value, more_raw, more_geo,
        more_base,
    )
    count = own_ref[2:3, 0:128][0, 0].astype(I32)
    src = own_ref[0:1, :]
    dst = own_ref[1:2, :].astype(I32)
    near = jnp.concatenate([recv_ref[k, :, 384 : 384 + GHOST] for k in range(NBR)], axis=1)
    ghosts = jnp.concatenate(
        [*thirds(near[0:3]), near[3:4], near[6:7], jnp.zeros((5, SLOTS), F32)], axis=0
    ).astype(BF16)
    table = table_ref[...]
    segments = jnp.concatenate([table, ghosts[:, 0:ATOM], ghosts[:, ATOM:SLOTS]], axis=0)
    found = dot(segments, one_hot(dst & 255, ATOM))
    part = dst >> 8
    picked = jnp.where(part == 0, found[0:16], jnp.where(part == 1, found[16:32], found[32:48]))
    beyond = (((dst - ATOM) >> 6) + 3).astype(F32) * ATOM + picked[10:11]
    code = jnp.where(part == 0, dst.astype(F32), beyond)
    edges[:, 0:PAIR] = jnp.concatenate(
        [joined(picked), picked[9:10], src, code, jnp.zeros((2, PAIR), F32)], axis=0
    )
    lane = lax.broadcasted_iota(I32, (8, 128), 1)
    row = lax.broadcasted_iota(I32, (8, 128), 0)

    def kept(ref):
        halves_of = [
            jnp.concatenate([ref[2 * i : 2 * i + 1, 256:384], ref[2 * i + 1 : 2 * i + 2, 256:384]], axis=1)
            for i in range(4)
        ]
        return atom_table(jnp.concatenate(halves_of[0:3], axis=0), halves_of[3]).astype(BF16)

    def place(ref, size, begin, at, k, held, tile):
        base = tile * 128 - at + begin
        first = base >> 7
        turn = base & 127
        low = jnp.clip(first, 0, 7)
        high = jnp.clip(first + 1, 0, 7)
        which = NBR if k is None else k
        left, right = lines[which, low], lines[which, high]
        back = lax.rem(128 - turn, 128)
        taken = jnp.where(
            lane < 128 - turn, pltpu.roll(left, back, 1), pltpu.roll(right, back, 1)
        )
        found = dot(held, one_hot(taken[5:6].astype(I32), ATOM))
        partner = jnp.concatenate([joined(found), found[9:10], jnp.zeros((4, 128), F32)], axis=0)
        if k is not None:
            match = lax.broadcasted_iota(I32, (GHOST, 128), 0) == taken[4:5].astype(I32)
            atom = jnp.sum(jnp.where(match, cols_ref[:, k : k + 1], 0.0), axis=0, keepdims=True)
            taken = jnp.where(row == 4, atom, taken + F32(ATOM * (3 + k)))
        taken = jnp.where(row < 4, partner, taken)
        here = pl.ds(pl.multiple_of(tile * 128, 128), 128)
        spot = tile * 128 + lane
        inside = (spot >= at) & (spot < at + size)
        edges[:, here] = jnp.where(inside, taken, edges[:, here])

    def scalar(ref, which):
        return ref[which : which + 1, 384:LIST][0, 0].astype(I32)

    for k, ref in enumerate([recv_ref.at[k] for k in range(NBR)] + [home_ref]):
        for i in range(PAIR // 128):
            lines[k, i] = jnp.where(row == 4, ref[i : i + 1, 0:128], ref[i : i + 1, 128:256])
    at = count
    jobs = []
    size = scalar(home_ref, 4)
    jobs.append((home_ref, size, 0, at, None, kept(home_ref), 4))
    at = at + size
    for k in range(NBR):
        ref = recv_ref.at[k]
        size = scalar(ref, 4)
        jobs.append((ref, size, scalar(ref, 5), at, k, kept(ref), 2))
        at = at + size
    total = at
    for ref, size, begin, at, k, held, usual in jobs:
        for step in range(usual):
            place(ref, size, begin, at, k, held, (at >> 7) + step)
    for ref, size, begin, at, k, held, usual in jobs:
        last = (at + size + 127) >> 7

        def more(tile, carry, ref=ref, size=size, begin=begin, at=at, k=k, held=held):
            place(ref, size, begin, at, k, held, tile)
            return carry

        lax.fori_loop((at >> 7) + usual, last, more, 0)
    extra_blocks = lax.div(jnp.maximum(total - MAIN, 0) + EXTRA - 1, EXTRA)

    env[...] = jnp.zeros_like(env)
    g_env[...] = jnp.zeros_like(g_env)
    terms[FIELD:, :] = jnp.zeros((16, 2 * MAIN), BF16)
    at_centre[...] = jnp.zeros_like(at_centre)
    at_partner[...] = jnp.zeros_like(at_partner)

    def first_pass(store, begin, width, offset):
        hots, slope, _, _, value, raw, geo, base = store
        here = pl.ds(begin, width)
        valid = begin + offset + lax.broadcasted_iota(I32, (1, width), 1) < total
        part = jnp.where(valid, edges[:, pl.ds(begin + offset, width)], 0.0)
        hot = one_hot(part[4:5].astype(I32), ATOM)
        hots[:, here] = hot
        geo[CODE : CODE + 1, here] = part[5:6]
        held = dot(table, hot)
        delta = part[0:3] - joined(held)
        length2 = delta[0:1] * delta[0:1] + delta[1:2] * delta[1:2] + delta[2:3] * delta[2:3] + 1.0
        soft = jnp.sqrt(length2)
        rinv = 1.0 / soft
        unit = delta * rinv
        ux, uy, uz = unit[0:1], unit[1:2], unit[2:3]
        turn = soft * (PI / CUTOFF) - PI / 2
        t2 = turn * turn
        cosine = -turn * (
            1 + t2 * (-1 / 6 + t2 * (1 / 120 + t2 * (-1 / 5040 + t2 * (1 / 362880 - t2 / 39916800))))
        )
        sine = 1 + t2 * (
            -1 / 2 + t2 * (1 / 24 + t2 * (-1 / 720 + t2 * (1 / 40320 + t2 * (-1 / 3628800 + t2 / 479001600))))
        )
        twice = 2 * cosine
        s_old, s_now = jnp.zeros_like(sine), sine
        c_old, c_now = jnp.ones_like(sine), cosine
        for b in range(BASIS):
            geo[RAD + b : RAD + b + 1, here] = s_now * rinv
            geo[DRAD + b : DRAD + b + 1, here] = (c_now * ((b + 1) * PI / CUTOFF) - s_now * rinv) * rinv
            s_old, s_now = s_now, twice * s_now - s_old
            c_old, c_now = c_now, twice * c_now - c_old
        angular = [
            jnp.ones_like(ux),
            ROOT3 * ux,
            ROOT3 * uy,
            ROOT3 * uz,
            ROOT15 * ux * uy,
            ROOT15 * uy * uz,
            0.5 * ROOT5 * (2.0 * uz * uz - ux * ux - uy * uy),
            ROOT15 * ux * uz,
            0.5 * ROOT15 * (ux * ux - uy * uy),
        ]
        for m in range(9):
            geo[ANG + m : ANG + m + 1, here] = angular[m]
        inner = 1.0 - length2 * (1.0 / (CUTOFF * CUTOFF))
        alive = jnp.where(valid, 1.0, 0.0)
        envelope = alive * inner * inner
        geo[ENVL : ENVL + 1, here] = envelope
        geo[DENVL : DENVL + 1, here] = alive * inner * soft * (-4.0 / (CUTOFF * CUTOFF))
        geo[RINV : RINV + 1, here] = rinv
        geo[DIR : DIR + 3, here] = unit
        radial = geo[RAD : RAD + 8, here]
        radial_low = radial - radial.astype(BF16).astype(F32)
        kinds = lax.broadcasted_iota(I32, (8, width), 0)
        hot_c = jnp.where(kinds == held[9:10].astype(I32), 1.0, 0.0)
        hot_p = jnp.where(kinds == part[3:4].astype(I32), 1.0, 0.0)
        inputs = jnp.concatenate(
            [hot_c, hot_p, radial, radial_low, hot_c, hot_p, radial, jnp.zeros((8, width), F32)], axis=0
        ).astype(BF16)
        pre = dot(wx_ref[...], inputs)
        gate = sigmoid(pre)
        act = pre * gate
        slope[:, here] = gate + act * (1.0 - gate)
        after = dot(up_ref[...], stacked(act))
        raw[:, here] = after[0:CH]
        value[:, here] = after[CH : 2 * CH]
        base[:, here] = after[2 * CH :]
        geo[ERAW : ERAW + 1, here] = jnp.sum(act * ab_ref[:, 0:1], axis=0, keepdims=True)
        weights = after[0:CH] * envelope
        for m in range(9):
            term = weights if m == 0 else weights * angular[m]
            rows = slice(m * CH, (m + 1) * CH)
            terms[rows, 0:width], terms[rows, width : 2 * width] = halves(term)
        scatter(terms, hot, env, FIELD)

    def second_pass(store, begin, width):
        hots, _, mixed, mixed_low, value, _, geo, base = store
        here = pl.ds(begin, width)
        hot = hots[:, here]
        gather(fields, hot, around)
        envelope = geo[ENVL : ENVL + 1, here]
        sums = [None, None, None]
        for m in range(9):
            got = around[m * CH : (m + 1) * CH, 0:width]
            term = got if m == 0 else got * geo[ANG + m : ANG + m + 1, here]
            degree = DEGREES[m]
            sums[degree] = term if sums[degree] is None else sums[degree] + term
        held = value[:, here]
        invariant = jnp.concatenate([s * held for s in sums], axis=0)
        pre = base[:, here] + dot(mt_ref[...], stacked(invariant))
        gate = sigmoid(pre)
        act = pre * gate
        back = ab_ref[:, 1:2]
        e_raw = geo[ERAW : ERAW + 1, here] + jnp.sum(act * back, axis=0, keepdims=True)
        geo[ERAW : ERAW + 1, here] = e_raw
        energy = e_raw * envelope
        energy = jnp.concatenate([energy, jnp.zeros((15, width), F32)], axis=0)
        terms[FIELD:, 0:width], terms[FIELD:, width : 2 * width] = halves(energy)
        d_pre = (gate + act * (1.0 - gate)) * back * envelope
        d_high, d_low = halves(d_pre)
        mixed[:, here] = d_high
        mixed_low[:, here] = d_low
        d_inv = dot(mb_ref[...], jnp.concatenate([d_high, d_low, d_high], axis=0))
        d_inv = [d_inv[i * CH : (i + 1) * CH] for i in range(3)]
        value[:, here] = d_inv[0] * sums[0] + d_inv[1] * sums[1] + d_inv[2] * sums[2]
        d_sum = [d * held for d in d_inv]
        for m in range(9):
            share = d_sum[DEGREES[m]]
            term = share if m == 0 else share * geo[ANG + m : ANG + m + 1, here]
            rows = slice(m * CH, (m + 1) * CH)
            terms[rows, 0:width], terms[rows, width : 2 * width] = halves(term)
            if m:
                geo[DANG + m - 1 : DANG + m, here] = jnp.sum(
                    share * around[rows, 0:width], axis=0, keepdims=True
                )
        scatter(terms, hot, g_env, FIELD + 16)

    def rest(step):
        def body(block, carry):
            step(pl.multiple_of(block * EXTRA, EXTRA))
            return carry

        lax.fori_loop(0, extra_blocks, body, 0)

    first_pass(first_store, 0, MAIN, 0)
    rest(lambda begin: first_pass(more_store, begin, EXTRA, MAIN))
    fields[:, 0:ATOM], fields[:, ATOM:] = halves(env[...] * ENV_SCALE)
    second_pass(first_store, 0, MAIN)
    rest(lambda begin: second_pass(more_store, begin, EXTRA))
    energy_ref[...] = g_env[FIELD : FIELD + 1, :]
    fields[:, 0:ATOM], fields[:, ATOM:] = halves(g_env[0:FIELD, :] * ENV_SCALE)

    def third(begin):
        pull = third_pass(
            (more_hots, more_slope, more_mixed, more_low, more_d_value, more_raw, more_geo),
            begin, EXTRA, fields, around, dn_ref, wr_ref, ab_ref,
        )
        to_partners(pull, more_geo, begin, EXTRA, at_partner)
        to_centres(pull, more_hots, begin, EXTRA, at_centre)

    rest(third)


def return_kernel(
    dn_ref, wr_ref, ab_ref,
    fields, more_centre, more_partner, hots, slope, mixed, mixed_low, d_value, raw, geo,
    out_ref, outbox, inbox, around, at_centre, at_partner, send_sem, recv_sem,
):
    barrier, peers = greet()
    at_centre[...] = more_centre[...]
    at_partner[...] = more_partner[...]
    store = (hots, slope, mixed, mixed_low, d_value, raw, geo)
    pull = third_pass(store, 0, MAIN, fields, around, dn_ref, wr_ref, ab_ref)
    to_partners(pull, geo, 0, MAIN, at_partner)
    parts = at_partner[...]
    for k in range(NBR):
        for i in range(3):
            for half in range(2):
                outbox[k, 3 * half + i : 3 * half + i + 1, :] = parts[
                    16 * i + 3 + k : 16 * i + 4 + k, half * 128 : (half + 1) * 128
                ]
        outbox[k, 6:8, :] = jnp.zeros((2, 128), F32)
    pl.semaphore_wait(barrier, NBR)
    copies = swap(peers, outbox, inbox, send_sem, recv_sem)
    to_centres(pull, hots, 0, MAIN, at_centre)
    sums = at_centre[...]
    total = sums[0:3] + sums[8:11]
    total = total - jnp.concatenate([parts[16 * i : 16 * i + 1] for i in range(3)], axis=0)
    for copy in copies:
        copy.wait()
    arrived = inbox[0]
    for k in range(1, NBR):
        arrived = arrived + inbox[k]
    out_ref[...] = total - jnp.concatenate([arrived[0:3], arrived[3:6]], axis=1)


def edge_call(*operands):
    shape = jax.ShapeDtypeStruct
    rest = CAP - MAIN

    def store(lanes, make):
        return [
            make((ATOM, lanes), BF16),
            make((WIDTH, lanes), F32),
            make((WIDTH, lanes), BF16),
            make((WIDTH, lanes), BF16),
            make((CH, lanes), F32),
            make((CH, lanes), F32),
            make((ROWS, lanes), F32),
        ]

    return pl.pallas_call(
        edge_kernel,
        out_shape=(
            shape((1, ATOM), F32),
            shape((FIELD, 2 * ATOM), BF16),
            shape((16, ATOM), F32),
            shape((48, ATOM), F32),
            *store(MAIN, shape),
        ),
        in_specs=[VMEM] * 12,
        out_specs=[VMEM] * 11,
        scratch_shapes=[
            pltpu.VMEM((8, CAP + 512), F32),
            pltpu.VMEM((WIDTH, MAIN), F32),
            *store(rest, pltpu.VMEM),
            pltpu.VMEM((WIDTH, rest), F32),
            pltpu.VMEM((FIELD, ATOM), F32),
            pltpu.VMEM((FIELD + 16, ATOM), F32),
            pltpu.VMEM((FIELD + 16, 2 * MAIN), BF16),
            pltpu.VMEM((FIELD, MAIN), F32),
            pltpu.VMEM((NBR + 1, PAIR // 128, 8, 128), F32),
        ],
        compiler_params=pltpu.CompilerParams(vmem_limit_bytes=46 << 20),
    )(*operands)


def per_device(
    positions, species, send_list, edge_src, edge_dst, edge_count,
    w_in, w_mid, w_pair, w_mix, w_back, w_read,
):
    sends = send_list[0]
    shape = jax.ShapeDtypeStruct
    shared = pl.pallas_call(
        share_kernel,
        out_shape=(
            shape((8, PAIR), F32),
            shape((16, ATOM), BF16),
            shape((NBR, 8, LIST), F32),
            shape((WIDTH, 64), BF16),
            shape((2 * WIDTH, 3 * WIDTH), BF16),
            shape((WIDTH, 6 * WIDTH), BF16),
            shape((WIDTH, 9 * CH), BF16),
            shape((3 * CH, 3 * WIDTH), BF16),
            shape((16, 3 * WIDTH), BF16),
            shape((WIDTH, 2), F32),
            shape((GHOST, NBR), F32),
            shape((8, LIST), F32),
        ),
        in_specs=[SMEM] + [HBM] * 11,
        out_specs=[VMEM] * 12,
        scratch_shapes=[
            pltpu.VMEM((3, ATOM), F32),
            pltpu.VMEM((1, ATOM), I32),
            pltpu.VMEM((NBR, GHOST), I32),
            pltpu.VMEM((1, PAIR), I32),
            pltpu.VMEM((1, PAIR), I32),
            pltpu.VMEM((2 * SPECIES + BASIS, WIDTH), F32),
            pltpu.VMEM((WIDTH, WIDTH), F32),
            pltpu.VMEM((WIDTH, WIDTH), F32),
            pltpu.VMEM((WIDTH + 3 * CH, WIDTH), F32),
            pltpu.VMEM((WIDTH, WIDTH), F32),
            pltpu.VMEM((1, WIDTH), F32),
            pltpu.VMEM((NBR, 8, LIST), F32),
            pltpu.VMEM((8, 384), F32),
            pltpu.SemaphoreType.DMA((11,)),
            pltpu.SemaphoreType.DMA((NBR,)),
            pltpu.SemaphoreType.DMA((NBR,)),
        ],
        compiler_params=pltpu.CompilerParams(
            collective_id=0, has_side_effects=True, vmem_limit_bytes=8 << 20
        ),
    )(
        edge_count,
        *(
            pltpu.with_memory_space_constraint(x, pltpu.HBM)
            for x in (
                positions, species.reshape(1, ATOM), sends, edge_src, edge_dst,
                w_in, w_mid, w_pair, w_mix, w_back, w_read.reshape(1, WIDTH),
            )
        ),
    )
    energy, *kept = edge_call(*shared)
    dn, wr, ab = shared[5], shared[8], shared[9]
    forces = pl.pallas_call(
        return_kernel,
        out_shape=shape((3, ATOM), F32),
        in_specs=[VMEM] * 13,
        out_specs=VMEM,
        scratch_shapes=[
            pltpu.VMEM((NBR, 8, 128), F32),
            pltpu.VMEM((NBR, 8, 128), F32),
            pltpu.VMEM((FIELD, MAIN), F32),
            pltpu.VMEM((16, ATOM), F32),
            pltpu.VMEM((48, ATOM), F32),
            pltpu.SemaphoreType.DMA((NBR,)),
            pltpu.SemaphoreType.DMA((NBR,)),
        ],
        compiler_params=pltpu.CompilerParams(
            collective_id=1, has_side_effects=True, vmem_limit_bytes=20 << 20
        ),
    )(dn, wr, ab, *kept)
    return forces, energy.reshape(ATOM)


def solution(mesh):
    both = ("dom", "face")
    placed = (
        P(None, both), P(both), P(both, None, None), P(both, None), P(both, None), P(both),
        P(), P(), P(), P(), P(), P(),
    )
    return jax.shard_map(
        per_device,
        mesh=mesh,
        in_specs=placed,
        out_specs=(P(None, both), P(both)),
        check_vma=False,
    )
```

```python
import functools

import jax
import jax.numpy as jnp
from jax import lax
from jax.experimental import pallas as pl
from jax.experimental.pallas import tpu as pltpu
from jax.sharding import PartitionSpec as P

CH = 64
WIDTH = 128
BASIS = 8
SPECIES = 7
ENV_SCALE = 0.2
CUTOFF = 6.0
PI = 3.141592653589793
DIRECTIONS = ((-1, -1), (-1, 0), (-1, 1), (0, -1), (0, 1), (1, -1), (1, 0), (1, 1))
NBR = 8
ATOM = 256
GHOST = 64
PAIR = 1024
SLOTS = NBR * GHOST
LIST = 512
CAP = 10 * PAIR
MAIN = 2048
LATE = 768
EXTRA = 512
F32 = jnp.float32
BF16 = jnp.bfloat16
I32 = jnp.int32
MESH = pl.DeviceIdType.MESH
VMEM = pl.BlockSpec(memory_space=pltpu.VMEM)
SMEM = pl.BlockSpec(memory_space=pltpu.SMEM)
HBM = pl.BlockSpec(memory_space=pltpu.HBM)

RAD, DRAD, ANG, ENVL, DENVL, RINV, DIR, ERAW, DANG, CODE, ROWS = 0, 8, 16, 25, 26, 27, 28, 31, 32, 40, 48
FIELD = 9 * CH
ROOT3, ROOT5, ROOT15 = 3.0**0.5, 5.0**0.5, 15.0**0.5
DEGREES = (0, 1, 1, 1, 2, 2, 2, 2, 2)


def dot(a, b):
    return lax.dot_general(a, b, (((1,), (0,)), ((), ())), preferred_element_type=F32)


def dot_nt(a, b):
    return lax.dot_general(a, b, (((1,), (1,)), ((), ())), preferred_element_type=F32)


def exact(a, b):
    return jnp.dot(a, b, precision=lax.Precision.HIGHEST, preferred_element_type=F32)


def halves(x):
    high = x.astype(BF16)
    return high, (x - high.astype(F32)).astype(BF16)


def thirds(x):
    high = x.astype(BF16).astype(F32)
    rest = x - high
    mid = rest.astype(BF16).astype(F32)
    return high, mid, rest - mid


def sigmoid(x):
    return 0.5 * jnp.tanh(0.5 * x) + 0.5


def triple(weight):
    high, low = halves(weight)
    return jnp.concatenate([high, high, low], axis=1)


def stacked(x):
    high, low = halves(x)
    return jnp.concatenate([high, low, high], axis=0)


def one_hot(row, count):
    rows = lax.broadcasted_iota(I32, (count, row.shape[1]), 0).astype(F32).astype(BF16)
    match = rows == row.astype(F32).astype(BF16)
    return jnp.where(match, jnp.ones_like(rows), jnp.zeros_like(rows))


def atom_table(coords, kinds):
    parts = thirds(coords)
    pad = jnp.zeros((6, coords.shape[1]), F32)
    return jnp.concatenate([*parts, kinds, pad], axis=0)


def joined(rows):
    return rows[0:3] + rows[3:6] + rows[6:9]


def greet():
    here = [lax.axis_index("dom"), lax.axis_index("face")]
    sizes = [lax.axis_size("dom"), lax.axis_size("face")]
    peers = []
    for shift in DIRECTIONS:
        peers.append(
            tuple(lax.rem(at + by + size, size) for at, by, size in zip(here, shift, sizes))
        )
    barrier = pltpu.get_barrier_semaphore()
    for peer in peers:
        pl.semaphore_signal(barrier, inc=1, device_id=peer, device_id_type=MESH)
    return barrier, peers


def swap(peers, out_ref, in_ref, send_sem, recv_sem):
    copies = []
    for k, peer in enumerate(peers):
        copies.append(
            pltpu.make_async_remote_copy(
                src_ref=out_ref.at[k],
                dst_ref=in_ref.at[NBR - 1 - k],
                send_sem=send_sem.at[k],
                recv_sem=recv_sem.at[NBR - 1 - k],
                device_id=peer,
                device_id_type=MESH,
            )
        )
    for copy in copies:
        copy.start()
    return copies


def share_kernel(
    count_ref, *refs,
):
    sources, refs = refs[:11], refs[11:]
    (
        own_ref, table_ref, recv_ref, wx_ref, up_ref, dn_ref, mt_ref, mb_ref, wr_ref, ab_ref, cols_ref,
        home_ref, hots_ref, slope_ref, value_ref, raw_ref, geo_ref, base_ref, env_ref,
    ) = refs[:19]
    held, refs = refs[19:30], refs[30:]
    out_buf, order_buf, terms, load_sem, send_sem, recv_sem = refs
    (
        pos_ref, spec_ref, send_ref, src_ref, dst_ref,
        w_in_ref, w_mid_ref, w_pair_ref, w_mix_ref, w_back_ref, w_read_ref,
    ) = held
    loads = [
        pltpu.make_async_copy(source, target, load_sem.at[i])
        for i, (source, target) in enumerate(zip(sources, held))
    ]
    for load in loads:
        load.start()
    barrier, peers = greet()
    for load in loads[:5]:
        load.wait()
    table = atom_table(pos_ref[...], spec_ref[...].astype(F32)).astype(BF16)
    table_ref[...] = table
    sends = jnp.concatenate([send_ref[k : k + 1, :] for k in range(NBR)], axis=1)
    ghosts = dot(table, one_hot(sends, ATOM))
    ghost_rows = jnp.concatenate([joined(ghosts), ghosts[9:10]], axis=0)
    src = src_ref[...]
    dst = dst_ref[...]
    lanes = lax.broadcasted_iota(I32, (1, PAIR), 1)
    live = lanes < count_ref[0]
    ghost = dst >= ATOM
    away = dst - ATOM
    bucket = jnp.where(ghost, (away >> 6) + 1, 0)
    bucket = jnp.where(live, bucket, 15)
    place = jnp.where(ghost, away & 63, dst)
    member = jnp.where(lax.broadcasted_iota(I32, (16, PAIR), 0) == bucket, 1.0, 0.0)
    before = lax.broadcasted_iota(I32, (ATOM, ATOM), 0) < lax.broadcasted_iota(I32, (ATOM, ATOM), 1)
    before = jnp.where(before, 1.0, 0.0).astype(BF16)
    pieces = [member[:, i * ATOM : (i + 1) * ATOM] for i in range(PAIR // ATOM)]
    ranks = dot(jnp.concatenate(pieces, axis=0).astype(BF16), before)
    sums = [jnp.sum(piece, axis=1, keepdims=True) for piece in pieces]
    total = sums[0] + sums[1] + sums[2] + sums[3]
    start = jnp.zeros((16, 1), F32)
    index = lax.broadcasted_iota(I32, (16, 1), 0)
    for b in range(NBR + 1):
        start = start + jnp.where(index > b, total[b : b + 1, :], 0.0)
    offset = start
    spots = []
    for i, piece in enumerate(pieces):
        where = ranks[16 * i : 16 * (i + 1)] + offset
        spots.append(jnp.sum(piece * where, axis=0, keepdims=True))
        offset = offset + sums[i]
    spot = jnp.concatenate(spots, axis=1)
    spot = jnp.where(live, spot, -1.0).astype(I32)
    data = jnp.concatenate(
        [
            place.astype(F32), src.astype(F32), (dst >> 8).astype(F32), (dst & 255).astype(F32),
            jnp.zeros((12, PAIR), F32),
        ],
        axis=0,
    ).astype(BF16)
    for i in range(PAIR // ATOM):
        rows = lax.broadcasted_iota(I32, (ATOM, PAIR), 0) + i * ATOM
        chosen = jnp.where(rows == spot, 1.0, 0.0).astype(BF16)
        ordered = dot_nt(data, chosen)
        span = slice(i * ATOM, (i + 1) * ATOM)
        own_ref[0:1, span] = ordered[1:2]
        own_ref[1:2, span] = ordered[2:3] * ATOM + ordered[3:4]
        for j in range(2):
            for half in range(2):
                order_buf[2 * i + half : 2 * i + half + 1, j * 128 : (j + 1) * 128] = ordered[
                    j : j + 1, half * 128 : (half + 1) * 128
                ]
    atoms = jnp.concatenate([pos_ref[...], spec_ref[...].astype(F32)], axis=0)
    for i in range(4):
        for half in range(2):
            order_buf[2 * i + half : 2 * i + half + 1, 256:384] = atoms[
                i : i + 1, half * 128 : (half + 1) * 128
            ]
    entries = order_buf[...]
    none = jnp.zeros((8, GHOST), F32)
    indices = sends.astype(F32)
    for k in range(NBR):
        out_buf[k, :, 0:384] = entries
        part = slice(k * GHOST, (k + 1) * GHOST)
        mine = jnp.concatenate([ghost_rows[:, part], none[0:2], indices[:, part], none[0:1]], axis=0)
        out_buf[k, :, 384:LIST] = jnp.concatenate([mine, none], axis=1)
        out_buf[k, 4:5, 384:LIST] = jnp.broadcast_to(total[k + 1 : k + 2, :], (1, 128))
        out_buf[k, 5:6, 384:LIST] = jnp.broadcast_to(start[k + 1 : k + 2, :], (1, 128))
    pl.semaphore_wait(barrier, NBR)
    copies = swap(peers, out_buf, recv_ref, send_sem, recv_sem)
    home_ref[:, 0:384] = entries
    home_ref[:, 384:LIST] = jnp.zeros((8, 128), F32)
    home_ref[4:5, 384:LIST] = jnp.broadcast_to(total[0:1, :], (1, 128))
    own_ref[2:3, :] = jnp.full((1, PAIR), count_ref[0], I32).astype(F32)
    cols_ref[...] = send_ref[...].astype(F32).T
    for load in loads[5:]:
        load.wait()
    w_in = w_in_ref[...]
    w_c = w_in[0:SPECIES].T
    w_p = w_in[SPECIES : 2 * SPECIES].T
    w_r = w_in[2 * SPECIES :]
    gap = jnp.zeros((WIDTH, 1), F32)
    first = jnp.concatenate([w_c, gap, w_p, gap, w_r.T], axis=1)
    first_high = first.astype(BF16).astype(F32)
    first_low = first - first_high
    wx_ref[...] = jnp.concatenate(
        [first_high, first_high[:, 16:24], first_low, jnp.zeros((WIDTH, 8), F32)], axis=1
    ).astype(BF16)
    wr_high, wr_low = halves(jnp.concatenate([w_r, jnp.zeros((8, WIDTH), F32)], axis=0))
    wr_ref[...] = jnp.concatenate([wr_high, wr_high, wr_low], axis=1)
    w_mid = w_mid_ref[...]
    w_read = w_read_ref[...]
    down = jnp.concatenate(
        [exact(w_mid, w_pair_ref[...]), exact(w_mid, w_mix_ref[0:WIDTH, :])], axis=1
    )
    a_col = jnp.sum(w_mid * w_read, axis=1, keepdims=True)
    b_col = jnp.sum(w_back_ref[...] * w_read, axis=1, keepdims=True)
    ab_ref[...] = jnp.concatenate([a_col, b_col], axis=1)
    dn_ref[...] = triple(down)
    up_ref[...] = triple(down.T)
    mix = jnp.concatenate(
        [w_mix_ref[pl.ds(WIDTH + degree, CH, stride=3), :] for degree in range(3)], axis=0
    )
    mb_ref[...] = triple(mix)
    mt_ref[...] = triple(mix.T)
    half = LATE // 2
    ends = [own_ref[i : i + 1, 0:half] for i in range(2)]
    centre = jnp.concatenate(ends, axis=1)
    mate = jnp.concatenate(ends[::-1], axis=1)
    found = dot(table, one_hot(mate.astype(I32), ATOM))
    partner = jnp.concatenate([joined(found), found[9:10]], axis=0)
    index = lax.broadcasted_iota(I32, (1, half), 1).astype(F32)
    valid = jnp.concatenate([index, index], axis=1) < total[0:1, :]
    env_ref[...] = jnp.zeros_like(env_ref)
    store = (hots_ref, slope_ref, None, None, value_ref, raw_ref, geo_ref, base_ref)
    first_pass(
        centre.astype(I32), partner, mate, valid, table, store, 0, terms, env_ref, wx_ref, up_ref, ab_ref
    )
    for copy in copies:
        copy.wait()


def gather(fields, hot, around):
    width = hot.shape[1]
    around[:, 0:width] = dot(fields[...], jnp.concatenate([hot, hot], axis=0))


def scatter(terms, hot, total, count):
    width = hot.shape[1]
    for part in (slice(0, width), slice(width, 2 * width)):
        total[0:count, :] += dot_nt(terms[0:count, part], hot)


def first_pass(centre, partner, code, valid, table, store, begin, terms, env, wx_ref, up_ref, ab_ref):
    hots, slope, _, _, value, raw, geo, base = store
    width = centre.shape[1]
    here = pl.ds(begin, width)
    hot = one_hot(centre, ATOM)
    hots[:, here] = hot
    geo[CODE : CODE + 1, here] = code
    held = dot(table, hot)
    delta = partner[0:3] - joined(held)
    length2 = delta[0:1] * delta[0:1] + delta[1:2] * delta[1:2] + delta[2:3] * delta[2:3] + 1.0
    soft = jnp.sqrt(length2)
    rinv = 1.0 / soft
    unit = delta * rinv
    ux, uy, uz = unit[0:1], unit[1:2], unit[2:3]
    turn = soft * (PI / CUTOFF) - PI / 2
    t2 = turn * turn
    cosine = -turn * (
        1 + t2 * (-1 / 6 + t2 * (1 / 120 + t2 * (-1 / 5040 + t2 * (1 / 362880 - t2 / 39916800))))
    )
    sine = 1 + t2 * (
        -1 / 2 + t2 * (1 / 24 + t2 * (-1 / 720 + t2 * (1 / 40320 + t2 * (-1 / 3628800 + t2 / 479001600))))
    )
    twice = 2 * cosine
    s_old, s_now = jnp.zeros_like(sine), sine
    c_old, c_now = jnp.ones_like(sine), cosine
    for b in range(BASIS):
        geo[RAD + b : RAD + b + 1, here] = s_now * rinv
        geo[DRAD + b : DRAD + b + 1, here] = (c_now * ((b + 1) * PI / CUTOFF) - s_now * rinv) * rinv
        s_old, s_now = s_now, twice * s_now - s_old
        c_old, c_now = c_now, twice * c_now - c_old
    angular = [
        jnp.ones_like(ux),
        ROOT3 * ux,
        ROOT3 * uy,
        ROOT3 * uz,
        ROOT15 * ux * uy,
        ROOT15 * uy * uz,
        0.5 * ROOT5 * (2.0 * uz * uz - ux * ux - uy * uy),
        ROOT15 * ux * uz,
        0.5 * ROOT15 * (ux * ux - uy * uy),
    ]
    for m in range(9):
        geo[ANG + m : ANG + m + 1, here] = angular[m]
    inner = 1.0 - length2 * (1.0 / (CUTOFF * CUTOFF))
    alive = jnp.where(valid, 1.0, 0.0)
    envelope = alive * inner * inner
    geo[ENVL : ENVL + 1, here] = envelope
    geo[DENVL : DENVL + 1, here] = alive * inner * soft * (-4.0 / (CUTOFF * CUTOFF))
    geo[RINV : RINV + 1, here] = rinv
    geo[DIR : DIR + 3, here] = unit
    radial = geo[RAD : RAD + 8, here]
    radial_low = radial - radial.astype(BF16).astype(F32)
    kinds = lax.broadcasted_iota(I32, (8, width), 0)
    hot_c = jnp.where(kinds == held[9:10].astype(I32), 1.0, 0.0)
    hot_p = jnp.where(kinds == partner[3:4].astype(I32), 1.0, 0.0)
    inputs = jnp.concatenate(
        [hot_c, hot_p, radial, radial_low, hot_c, hot_p, radial, jnp.zeros((8, width), F32)], axis=0
    ).astype(BF16)
    pre = dot(wx_ref[...], inputs)
    gate = sigmoid(pre)
    act = pre * gate
    slope[:, here] = gate + act * (1.0 - gate)
    after = dot(up_ref[...], stacked(act))
    raw[:, here] = after[0:CH]
    value[:, here] = after[CH : 2 * CH]
    base[:, here] = after[2 * CH :]
    geo[ERAW : ERAW + 1, here] = jnp.sum(act * ab_ref[:, 0:1], axis=0, keepdims=True)
    weights = after[0:CH] * envelope
    for m in range(9):
        term = weights if m == 0 else weights * angular[m]
        rows = slice(m * CH, (m + 1) * CH)
        terms[rows, 0:width], terms[rows, width : 2 * width] = halves(term)
    scatter(terms, hot, env, FIELD)


def third_pass(store, begin, width, fields, around, dn_ref, wr_ref, ab_ref):
    hots, slope, mixed, mixed_low, d_value, raw_ref, geo = store
    here = pl.ds(begin, width)
    gather(fields, hots[:, here], around)
    envelope = geo[ENVL : ENVL + 1, here]
    raw = raw_ref[:, here]
    weights = raw * envelope
    d_weight = None
    d_ang = [None]
    for m in range(9):
        got = around[m * CH : (m + 1) * CH, 0:width]
        term = got if m == 0 else got * geo[ANG + m : ANG + m + 1, here]
        d_weight = term if m == 0 else d_weight + term
        if m:
            d_ang.append(
                geo[DANG + m - 1 : DANG + m, here] + jnp.sum(weights * got, axis=0, keepdims=True)
            )
    d_envelope = geo[ERAW : ERAW + 1, here] + jnp.sum(d_weight * raw, axis=0, keepdims=True)
    pair_high, pair_low = halves(jnp.concatenate([d_weight * envelope, d_value[:, here]], axis=0))
    both_high = jnp.concatenate([pair_high, mixed[:, here]], axis=0)
    both_low = jnp.concatenate([pair_low, mixed_low[:, here]], axis=0)
    d_act = dot(dn_ref[...], jnp.concatenate([both_high, both_low, both_high], axis=0))
    d_act = d_act + ab_ref[:, 0:1] * envelope
    d_radial = dot(wr_ref[...], stacked(d_act * slope[:, here]))
    d_soft = jnp.sum(d_radial[0:8] * geo[DRAD : DRAD + 8, here], axis=0, keepdims=True)
    d_soft = d_soft + d_envelope * geo[DENVL : DENVL + 1, here]
    unit = geo[DIR : DIR + 3, here]
    rinv = geo[RINV : RINV + 1, here]
    ux, uy, uz = unit[0:1], unit[1:2], unit[2:3]
    d_ux = ROOT3 * d_ang[1] + ROOT15 * (uy * d_ang[4] + uz * d_ang[7] + ux * d_ang[8]) - ROOT5 * ux * d_ang[6]
    d_uy = ROOT3 * d_ang[2] + ROOT15 * (ux * d_ang[4] + uz * d_ang[5] - uy * d_ang[8]) - ROOT5 * uy * d_ang[6]
    d_uz = ROOT3 * d_ang[3] + ROOT15 * (uy * d_ang[5] + ux * d_ang[7]) + 2.0 * ROOT5 * uz * d_ang[6]
    along = d_soft - (d_ux * ux + d_uy * uy + d_uz * uz) * rinv
    return [d * rinv + u * along for d, u in ((d_ux, ux), (d_uy, uy), (d_uz, uz))]


def to_partners(pull, geo, begin, width, at_partner):
    code = geo[CODE : CODE + 1, pl.ds(begin, width)].astype(I32)
    seg = lax.broadcasted_iota(I32, (16, width), 0) == (code >> 8)
    high, low = halves(jnp.concatenate([jnp.where(seg, g, 0.0) for g in pull], axis=0))
    hot = one_hot(code & 255, ATOM)
    sums = dot_nt(jnp.concatenate([high, low], axis=0), hot)
    at_partner[...] += sums[0:48] + sums[48:96]


def settled(pull, hot):
    sent = jnp.concatenate([*pull, jnp.zeros((5, hot.shape[1]), F32)], axis=0)
    sent = jnp.concatenate([sent, sent - sent.astype(BF16).astype(F32)], axis=0).astype(BF16)
    return dot_nt(sent, hot)


def edge_kernel(
    own_ref, table_ref, recv_ref,
    wx_ref, up_ref, dn_ref, mt_ref, mb_ref, wr_ref, ab_ref, cols_ref, home_ref,
    late_hots, late_slope, late_value, late_raw, late_geo, late_base, late_env,
    energy_ref, fields, at_centre, at_partner, hots, slope, mixed, mixed_low, d_value, raw, geo,
    edges, base, more_hots, more_slope, more_mixed, more_low, more_d_value, more_raw, more_geo,
    more_base, env, g_env, terms, around, lines, forward,
):
    first_store = (hots, slope, mixed, mixed_low, d_value, raw, geo, base)
    more_store = (
        more_hots, more_slope, more_mixed, more_low, more_d_value, more_raw, more_geo,
        more_base,
    )
    count = own_ref[2:3, 0:128][0, 0].astype(I32)
    src = own_ref[0:1, :]
    dst = own_ref[1:2, :].astype(I32)
    near = jnp.concatenate([recv_ref[k, :, 384 : 384 + GHOST] for k in range(NBR)], axis=1)
    ghosts = jnp.concatenate(
        [*thirds(near[0:3]), near[3:4], near[6:7], jnp.zeros((5, SLOTS), F32)], axis=0
    ).astype(BF16)
    table = table_ref[...]
    segments = jnp.concatenate([table, ghosts[:, 0:ATOM], ghosts[:, ATOM:SLOTS]], axis=0)
    found = dot(segments, one_hot(dst & 255, ATOM))
    part = dst >> 8
    picked = jnp.where(part == 0, found[0:16], jnp.where(part == 1, found[16:32], found[32:48]))
    beyond = (((dst - ATOM) >> 6) + 3).astype(F32) * ATOM + picked[10:11]
    code = jnp.where(part == 0, dst.astype(F32), beyond)
    forward[...] = jnp.concatenate(
        [joined(picked), picked[9:10], src, code, jnp.zeros((2, PAIR), F32)], axis=0
    )
    lane = lax.broadcasted_iota(I32, (8, 128), 1)
    row = lax.broadcasted_iota(I32, (8, 128), 0)

    def kept(ref):
        halves_of = [
            jnp.concatenate([ref[2 * i : 2 * i + 1, 256:384], ref[2 * i + 1 : 2 * i + 2, 256:384]], axis=1)
            for i in range(4)
        ]
        return atom_table(jnp.concatenate(halves_of[0:3], axis=0), halves_of[3]).astype(BF16)

    def place(size, begin, at, k, held, tile):
        base = tile * 128 - at + begin
        first = base >> 7
        turn = base & 127
        low = jnp.clip(first, 0, 7)
        high = jnp.clip(first + 1, 0, 7)
        if k is None:
            left, right = [forward[:, pl.ds(pl.multiple_of(i * 128, 128), 128)] for i in (low, high)]
        else:
            left, right = lines[k, low], lines[k, high]
        back = lax.rem(128 - turn, 128)
        taken = jnp.where(
            lane < 128 - turn, pltpu.roll(left, back, 1), pltpu.roll(right, back, 1)
        )
        if k is not None:
            found = dot(held, one_hot(taken[5:6].astype(I32), ATOM))
            partner = jnp.concatenate([joined(found), found[9:10], jnp.zeros((4, 128), F32)], axis=0)
        if k is not None and k < NBR:
            match = lax.broadcasted_iota(I32, (GHOST, 128), 0) == taken[4:5].astype(I32)
            atom = jnp.sum(jnp.where(match, cols_ref[:, k : k + 1], 0.0), axis=0, keepdims=True)
            taken = jnp.where(row == 4, atom, taken + F32(ATOM * (3 + k)))
        if k is not None:
            taken = jnp.where(row < 4, partner, taken)
        here = pl.ds(pl.multiple_of(tile * 128, 128), 128)
        spot = tile * 128 + lane
        inside = (spot >= at) & (spot < at + size)
        edges[:, here] = jnp.where(inside, taken, edges[:, here])

    def scalar(ref, which):
        return ref[which : which + 1, 384:LIST][0, 0].astype(I32)

    for k, ref in enumerate([recv_ref.at[k] for k in range(NBR)] + [home_ref]):
        for i in range(PAIR // 128):
            lines[k, i] = jnp.where(row == 4, ref[i : i + 1, 0:128], ref[i : i + 1, 128:256])
    inner = scalar(home_ref, 4)
    early = jnp.minimum(inner, LATE // 2)
    jobs = [(count - early, early, jnp.int32(0), None, None, PAIR // 128)]
    at = count - early
    size = inner - early
    jobs.append((size, LATE // 2, at, NBR, kept(home_ref), 0))
    at = at + size
    for k in range(NBR):
        ref = recv_ref.at[k]
        size = scalar(ref, 4)
        jobs.append((size, scalar(ref, 5), at, k, kept(ref), 2))
        at = at + size
    total = at
    for size, begin, at, k, held, usual in jobs:
        for step in range(usual):
            place(size, begin, at, k, held, (at >> 7) + step)
    for size, begin, at, k, held, usual in jobs:
        last = (at + size + 127) >> 7

        def more(tile, carry, size=size, begin=begin, at=at, k=k, held=held):
            place(size, begin, at, k, held, tile)
            return carry

        lax.fori_loop((at >> 7) + usual, last, more, 0)
    extra_blocks = lax.div(jnp.maximum(total - (MAIN - LATE), 0) + EXTRA - 1, EXTRA)

    for target, source in zip(
        (hots, slope, d_value, raw, geo, base),
        (late_hots, late_slope, late_value, late_raw, late_geo, late_base),
    ):
        target[:, 0:LATE] = source[...]
    env[...] = late_env[...]
    g_env[...] = jnp.zeros_like(g_env)
    terms[FIELD:, :] = jnp.zeros((16, 2 * MAIN), BF16)
    at_centre[...] = jnp.zeros_like(at_centre)
    at_partner[...] = jnp.zeros_like(at_partner)

    def second_pass(store, begin, width):
        hots, _, mixed, mixed_low, value, _, geo, base = store
        here = pl.ds(begin, width)
        hot = hots[:, here]
        gather(fields, hot, around)
        envelope = geo[ENVL : ENVL + 1, here]
        sums = [None, None, None]
        for m in range(9):
            got = around[m * CH : (m + 1) * CH, 0:width]
            term = got if m == 0 else got * geo[ANG + m : ANG + m + 1, here]
            degree = DEGREES[m]
            sums[degree] = term if sums[degree] is None else sums[degree] + term
        held = value[:, here]
        invariant = jnp.concatenate([s * held for s in sums], axis=0)
        pre = base[:, here] + dot(mt_ref[...], stacked(invariant))
        gate = sigmoid(pre)
        act = pre * gate
        back = ab_ref[:, 1:2]
        e_raw = geo[ERAW : ERAW + 1, here] + jnp.sum(act * back, axis=0, keepdims=True)
        geo[ERAW : ERAW + 1, here] = e_raw
        energy = e_raw * envelope
        energy = jnp.concatenate([energy, jnp.zeros((15, width), F32)], axis=0)
        terms[FIELD:, 0:width], terms[FIELD:, width : 2 * width] = halves(energy)
        d_pre = (gate + act * (1.0 - gate)) * back * envelope
        d_high, d_low = halves(d_pre)
        mixed[:, here] = d_high
        mixed_low[:, here] = d_low
        d_inv = dot(mb_ref[...], jnp.concatenate([d_high, d_low, d_high], axis=0))
        d_inv = [d_inv[i * CH : (i + 1) * CH] for i in range(3)]
        value[:, here] = d_inv[0] * sums[0] + d_inv[1] * sums[1] + d_inv[2] * sums[2]
        d_sum = [d * held for d in d_inv]
        for m in range(9):
            share = d_sum[DEGREES[m]]
            term = share if m == 0 else share * geo[ANG + m : ANG + m + 1, here]
            rows = slice(m * CH, (m + 1) * CH)
            terms[rows, 0:width], terms[rows, width : 2 * width] = halves(term)
            if m:
                geo[DANG + m - 1 : DANG + m, here] = jnp.sum(
                    share * around[rows, 0:width], axis=0, keepdims=True
                )
        scatter(terms, hot, g_env, FIELD + 16)

    def rest(step):
        def body(block, carry):
            step(pl.multiple_of(block * EXTRA, EXTRA))
            return carry

        lax.fori_loop(0, extra_blocks, body, 0)

    def listed(store, begin, start, width):
        valid = start + lax.broadcasted_iota(I32, (1, width), 1) < total
        part = jnp.where(valid, edges[:, pl.ds(start, width)], 0.0)
        first_pass(
            part[4:5].astype(I32), part[0:4], part[5:6], valid, table, store, begin, terms, env,
            wx_ref, up_ref, ab_ref,
        )

    listed(first_store, LATE, 0, MAIN - LATE)
    rest(lambda begin: listed(more_store, begin, pl.multiple_of(begin + (MAIN - LATE), 256), EXTRA))
    fields[:, 0:ATOM], fields[:, ATOM:] = halves(env[...] * ENV_SCALE)
    second_pass(first_store, 0, MAIN)
    rest(lambda begin: second_pass(more_store, begin, EXTRA))
    energy_ref[...] = g_env[FIELD : FIELD + 1, :]
    fields[:, 0:ATOM], fields[:, ATOM:] = halves(g_env[0:FIELD, :] * ENV_SCALE)

    def third(begin):
        pull = third_pass(
            (more_hots, more_slope, more_mixed, more_low, more_d_value, more_raw, more_geo),
            begin, EXTRA, fields, around, dn_ref, wr_ref, ab_ref,
        )
        to_partners(pull, more_geo, begin, EXTRA, at_partner)
        at_centre[...] += settled(pull, more_hots[:, pl.ds(begin, EXTRA)])

    rest(third)


def return_kernel(
    dn_ref, wr_ref, ab_ref,
    fields, more_centre, more_partner, hots, slope, mixed, mixed_low, d_value, raw, geo,
    out_ref, outbox, inbox, around, at_partner, send_sem, recv_sem,
):
    barrier, peers = greet()
    at_partner[...] = more_partner[...]
    store = (hots, slope, mixed, mixed_low, d_value, raw, geo)
    weights = (fields, around, dn_ref, wr_ref, ab_ref)
    pull = third_pass(store, LATE, MAIN - LATE, *weights)
    to_partners(pull, geo, LATE, MAIN - LATE, at_partner)
    parts = at_partner[...]
    for k in range(NBR):
        for i in range(3):
            for half in range(2):
                outbox[k, 3 * half + i : 3 * half + i + 1, :] = parts[
                    16 * i + 3 + k : 16 * i + 4 + k, half * 128 : (half + 1) * 128
                ]
        outbox[k, 6:8, :] = jnp.zeros((2, 128), F32)
    pl.semaphore_wait(barrier, NBR)
    copies = swap(peers, outbox, inbox, send_sem, recv_sem)
    sums = more_centre[...] + settled(pull, hots[:, LATE:MAIN])
    pull = third_pass(store, 0, LATE, *weights)
    mates = one_hot(geo[CODE : CODE + 1, 0:LATE].astype(I32), ATOM)
    sums = sums + settled(pull, hots[:, 0:LATE]) - settled(pull, mates)
    total = sums[0:3] + sums[8:11]
    total = total - jnp.concatenate([parts[16 * i : 16 * i + 1] for i in range(3)], axis=0)
    for copy in copies:
        copy.wait()
    arrived = inbox[0]
    for k in range(1, NBR):
        arrived = arrived + inbox[k]
    out_ref[...] = total - jnp.concatenate([arrived[0:3], arrived[3:6]], axis=1)


def edge_call(*operands):
    shape = jax.ShapeDtypeStruct
    rest = NBR * PAIR

    def store(lanes, make):
        return [
            make((ATOM, lanes), BF16),
            make((WIDTH, lanes), F32),
            make((WIDTH, lanes), BF16),
            make((WIDTH, lanes), BF16),
            make((CH, lanes), F32),
            make((CH, lanes), F32),
            make((ROWS, lanes), F32),
        ]

    return pl.pallas_call(
        edge_kernel,
        out_shape=(
            shape((1, ATOM), F32),
            shape((FIELD, 2 * ATOM), BF16),
            shape((16, ATOM), F32),
            shape((48, ATOM), F32),
            *store(MAIN, shape),
        ),
        in_specs=[VMEM] * 19,
        out_specs=[VMEM] * 11,
        scratch_shapes=[
            pltpu.VMEM((8, CAP + 512), F32),
            pltpu.VMEM((WIDTH, MAIN), F32),
            *store(rest, pltpu.VMEM),
            pltpu.VMEM((WIDTH, rest), F32),
            pltpu.VMEM((FIELD, ATOM), F32),
            pltpu.VMEM((FIELD + 16, ATOM), F32),
            pltpu.VMEM((FIELD + 16, 2 * MAIN), BF16),
            pltpu.VMEM((FIELD, MAIN), F32),
            pltpu.VMEM((NBR + 1, PAIR // 128, 8, 128), F32),
            pltpu.VMEM((8, PAIR), F32),
        ],
        compiler_params=pltpu.CompilerParams(vmem_limit_bytes=43 << 20),
    )(*operands)


def per_device(
    positions, species, send_list, edge_src, edge_dst, edge_count,
    w_in, w_mid, w_pair, w_mix, w_back, w_read,
):
    sends = send_list[0]
    shape = jax.ShapeDtypeStruct
    shared = pl.pallas_call(
        share_kernel,
        out_shape=(
            shape((8, PAIR), F32),
            shape((16, ATOM), BF16),
            shape((NBR, 8, LIST), F32),
            shape((WIDTH, 64), BF16),
            shape((2 * WIDTH, 3 * WIDTH), BF16),
            shape((WIDTH, 6 * WIDTH), BF16),
            shape((WIDTH, 9 * CH), BF16),
            shape((3 * CH, 3 * WIDTH), BF16),
            shape((16, 3 * WIDTH), BF16),
            shape((WIDTH, 2), F32),
            shape((GHOST, NBR), F32),
            shape((8, LIST), F32),
            shape((ATOM, LATE), BF16),
            shape((WIDTH, LATE), F32),
            shape((CH, LATE), F32),
            shape((CH, LATE), F32),
            shape((ROWS, LATE), F32),
            shape((WIDTH, LATE), F32),
            shape((FIELD, ATOM), F32),
        ),
        in_specs=[SMEM] + [HBM] * 11,
        out_specs=[VMEM] * 19,
        scratch_shapes=[
            pltpu.VMEM((3, ATOM), F32),
            pltpu.VMEM((1, ATOM), I32),
            pltpu.VMEM((NBR, GHOST), I32),
            pltpu.VMEM((1, PAIR), I32),
            pltpu.VMEM((1, PAIR), I32),
            pltpu.VMEM((2 * SPECIES + BASIS, WIDTH), F32),
            pltpu.VMEM((WIDTH, WIDTH), F32),
            pltpu.VMEM((WIDTH, WIDTH), F32),
            pltpu.VMEM((WIDTH + 3 * CH, WIDTH), F32),
            pltpu.VMEM((WIDTH, WIDTH), F32),
            pltpu.VMEM((1, WIDTH), F32),
            pltpu.VMEM((NBR, 8, LIST), F32),
            pltpu.VMEM((8, 384), F32),
            pltpu.VMEM((FIELD, 2 * LATE), BF16),
            pltpu.SemaphoreType.DMA((11,)),
            pltpu.SemaphoreType.DMA((NBR,)),
            pltpu.SemaphoreType.DMA((NBR,)),
        ],
        compiler_params=pltpu.CompilerParams(
            collective_id=0, has_side_effects=True, vmem_limit_bytes=14 << 20
        ),
    )(
        edge_count,
        *(
            pltpu.with_memory_space_constraint(x, pltpu.HBM)
            for x in (
                positions, species.reshape(1, ATOM), sends, edge_src, edge_dst,
                w_in, w_mid, w_pair, w_mix, w_back, w_read.reshape(1, WIDTH),
            )
        ),
    )
    energy, *kept = edge_call(*shared)
    dn, wr, ab = shared[5], shared[8], shared[9]
    forces = pl.pallas_call(
        return_kernel,
        out_shape=shape((3, ATOM), F32),
        in_specs=[VMEM] * 13,
        out_specs=VMEM,
        scratch_shapes=[
            pltpu.VMEM((NBR, 8, 128), F32),
            pltpu.VMEM((NBR, 8, 128), F32),
            pltpu.VMEM((FIELD, MAIN - LATE), F32),
            pltpu.VMEM((48, ATOM), F32),
            pltpu.SemaphoreType.DMA((NBR,)),
            pltpu.SemaphoreType.DMA((NBR,)),
        ],
        compiler_params=pltpu.CompilerParams(
            collective_id=1, has_side_effects=True, vmem_limit_bytes=20 << 20
        ),
    )(dn, wr, ab, *kept)
    return forces, energy.reshape(ATOM)


def solution(mesh):
    both = ("dom", "face")
    placed = (
        P(None, both), P(both), P(both, None, None), P(both, None), P(both, None), P(both),
        P(), P(), P(), P(), P(), P(),
    )
    return jax.shard_map(
        per_device,
        mesh=mesh,
        in_specs=placed,
        out_specs=(P(None, both), P(both)),
        check_vma=False,
    )
```

```python
import functools

import jax
import jax.numpy as jnp
from jax import lax
from jax.experimental import pallas as pl
from jax.experimental.pallas import tpu as pltpu
from jax.sharding import PartitionSpec as P

CH = 64
WIDTH = 128
BASIS = 8
SPECIES = 7
ENV_SCALE = 0.2
CUTOFF = 6.0
PI = 3.141592653589793
DIRECTIONS = ((-1, -1), (-1, 0), (-1, 1), (0, -1), (0, 1), (1, -1), (1, 0), (1, 1))
NBR = 8
FAR_FIRST = (0, 7, 2, 5, 3, 4, 1, 6)
ATOM = 256
GHOST = 64
PAIR = 1024
SLOTS = NBR * GHOST
LIST = 512
CAP = 10 * PAIR
MAIN = 2048
LATE = 768
EXTRA = 512
F32 = jnp.float32
BF16 = jnp.bfloat16
I32 = jnp.int32
MESH = pl.DeviceIdType.MESH
VMEM = pl.BlockSpec(memory_space=pltpu.VMEM)
SMEM = pl.BlockSpec(memory_space=pltpu.SMEM)
HBM = pl.BlockSpec(memory_space=pltpu.HBM)

RAD, DRAD, ANG, ENVL, DENVL, RINV, DIR, ERAW, DANG, CODE, ROWS = 0, 8, 16, 25, 26, 27, 28, 31, 32, 40, 48
FIELD = 9 * CH
ROOT3, ROOT5, ROOT15 = 3.0**0.5, 5.0**0.5, 15.0**0.5
DEGREES = (0, 1, 1, 1, 2, 2, 2, 2, 2)


def dot(a, b):
    return lax.dot_general(a, b, (((1,), (0,)), ((), ())), preferred_element_type=F32)


def dot_nt(a, b):
    return lax.dot_general(a, b, (((1,), (1,)), ((), ())), preferred_element_type=F32)


def exact(a, b):
    return jnp.dot(a, b, precision=lax.Precision.HIGHEST, preferred_element_type=F32)


def halves(x):
    high = x.astype(BF16)
    return high, (x - high.astype(F32)).astype(BF16)


def thirds(x):
    high = x.astype(BF16).astype(F32)
    rest = x - high
    mid = rest.astype(BF16).astype(F32)
    return high, mid, rest - mid


def sigmoid(x):
    return 0.5 * jnp.tanh(0.5 * x) + 0.5


def triple(weight):
    high, low = halves(weight)
    return jnp.concatenate([high, high, low], axis=1)


def stacked(x):
    high, low = halves(x)
    return jnp.concatenate([high, low, high], axis=0)


def one_hot(row, count):
    rows = lax.broadcasted_iota(I32, (count, row.shape[1]), 0).astype(F32).astype(BF16)
    match = rows == row.astype(F32).astype(BF16)
    return jnp.where(match, jnp.ones_like(rows), jnp.zeros_like(rows))


def atom_table(coords, kinds):
    parts = thirds(coords)
    pad = jnp.zeros((6, coords.shape[1]), F32)
    return jnp.concatenate([*parts, kinds, pad], axis=0)


def joined(rows):
    return rows[0:3] + rows[3:6] + rows[6:9]


def greet():
    here = [lax.axis_index("dom"), lax.axis_index("face")]
    sizes = [lax.axis_size("dom"), lax.axis_size("face")]
    peers = []
    for shift in DIRECTIONS:
        peers.append(
            tuple(lax.rem(at + by + size, size) for at, by, size in zip(here, shift, sizes))
        )
    barrier = pltpu.get_barrier_semaphore()
    for k in FAR_FIRST:
        pl.semaphore_signal(barrier, inc=1, device_id=peers[k], device_id_type=MESH)
    return barrier, peers


def swap(peers, out_ref, in_ref, send_sem, recv_sem):
    copies = []
    for k, peer in enumerate(peers):
        copies.append(
            pltpu.make_async_remote_copy(
                src_ref=out_ref.at[k],
                dst_ref=in_ref.at[NBR - 1 - k],
                send_sem=send_sem.at[k],
                recv_sem=recv_sem.at[NBR - 1 - k],
                device_id=peer,
                device_id_type=MESH,
            )
        )
    for k in FAR_FIRST:
        copies[k].start()
    return copies


def share_kernel(
    count_ref, *refs,
):
    sources, refs = refs[:11], refs[11:]
    (
        own_ref, table_ref, recv_ref, wx_ref, up_ref, dn_ref, mt_ref, mb_ref, wr_ref, ab_ref, cols_ref,
        home_ref, hots_ref, slope_ref, value_ref, raw_ref, geo_ref, base_ref, env_ref,
    ) = refs[:19]
    held, refs = refs[19:30], refs[30:]
    out_buf, order_buf, terms, load_sem, send_sem, recv_sem = refs
    (
        pos_ref, spec_ref, send_ref, src_ref, dst_ref,
        w_in_ref, w_mid_ref, w_pair_ref, w_mix_ref, w_back_ref, w_read_ref,
    ) = held
    loads = [
        pltpu.make_async_copy(source, target, load_sem.at[i])
        for i, (source, target) in enumerate(zip(sources, held))
    ]
    barrier, peers = greet()
    for load in loads:
        load.start()
    for load in loads[:5]:
        load.wait()
    table = atom_table(pos_ref[...], spec_ref[...].astype(F32)).astype(BF16)
    table_ref[...] = table
    sends = jnp.concatenate([send_ref[k : k + 1, :] for k in range(NBR)], axis=1)
    ghosts = dot(table, one_hot(sends, ATOM))
    ghost_rows = jnp.concatenate([joined(ghosts), ghosts[9:10]], axis=0)
    src = src_ref[...]
    dst = dst_ref[...]
    lanes = lax.broadcasted_iota(I32, (1, PAIR), 1)
    live = lanes < count_ref[0]
    ghost = dst >= ATOM
    away = dst - ATOM
    bucket = jnp.where(ghost, (away >> 6) + 1, 0)
    bucket = jnp.where(live, bucket, 15)
    place = jnp.where(ghost, away & 63, dst)
    member = jnp.where(lax.broadcasted_iota(I32, (16, PAIR), 0) == bucket, 1.0, 0.0)
    before = lax.broadcasted_iota(I32, (ATOM, ATOM), 0) < lax.broadcasted_iota(I32, (ATOM, ATOM), 1)
    before = jnp.where(before, 1.0, 0.0).astype(BF16)
    pieces = [member[:, i * ATOM : (i + 1) * ATOM] for i in range(PAIR // ATOM)]
    ranks = dot(jnp.concatenate(pieces, axis=0).astype(BF16), before)
    sums = [jnp.sum(piece, axis=1, keepdims=True) for piece in pieces]
    total = sums[0] + sums[1] + sums[2] + sums[3]
    start = jnp.zeros((16, 1), F32)
    index = lax.broadcasted_iota(I32, (16, 1), 0)
    for b in range(NBR + 1):
        start = start + jnp.where(index > b, total[b : b + 1, :], 0.0)
    offset = start
    spots = []
    for i, piece in enumerate(pieces):
        where = ranks[16 * i : 16 * (i + 1)] + offset
        spots.append(jnp.sum(piece * where, axis=0, keepdims=True))
        offset = offset + sums[i]
    spot = jnp.concatenate(spots, axis=1)
    spot = jnp.where(live, spot, -1.0).astype(I32)
    data = jnp.concatenate(
        [
            place.astype(F32), src.astype(F32), (dst >> 8).astype(F32), (dst & 255).astype(F32),
            jnp.zeros((12, PAIR), F32),
        ],
        axis=0,
    ).astype(BF16)
    for i in range(PAIR // ATOM):
        rows = lax.broadcasted_iota(I32, (ATOM, PAIR), 0) + i * ATOM
        chosen = jnp.where(rows == spot, 1.0, 0.0).astype(BF16)
        ordered = dot_nt(data, chosen)
        span = slice(i * ATOM, (i + 1) * ATOM)
        own_ref[0:1, span] = ordered[1:2]
        own_ref[1:2, span] = ordered[2:3] * ATOM + ordered[3:4]
        for j in range(2):
            for half in range(2):
                order_buf[2 * i + half : 2 * i + half + 1, j * 128 : (j + 1) * 128] = ordered[
                    j : j + 1, half * 128 : (half + 1) * 128
                ]
    atoms = jnp.concatenate([pos_ref[...], spec_ref[...].astype(F32)], axis=0)
    for i in range(4):
        for half in range(2):
            order_buf[2 * i + half : 2 * i + half + 1, 256:384] = atoms[
                i : i + 1, half * 128 : (half + 1) * 128
            ]
    entries = order_buf[...]
    none = jnp.zeros((8, GHOST), F32)
    indices = sends.astype(F32)
    for k in range(NBR):
        out_buf[k, :, 0:384] = entries
        part = slice(k * GHOST, (k + 1) * GHOST)
        mine = jnp.concatenate([ghost_rows[:, part], none[0:2], indices[:, part], none[0:1]], axis=0)
        out_buf[k, :, 384:LIST] = jnp.concatenate([mine, none], axis=1)
        out_buf[k, 4:5, 384:LIST] = jnp.broadcast_to(total[k + 1 : k + 2, :], (1, 128))
        out_buf[k, 5:6, 384:LIST] = jnp.broadcast_to(start[k + 1 : k + 2, :], (1, 128))
    pl.semaphore_wait(barrier, NBR)
    copies = swap(peers, out_buf, recv_ref, send_sem, recv_sem)
    home_ref[:, 0:384] = entries
    home_ref[:, 384:LIST] = jnp.zeros((8, 128), F32)
    home_ref[4:5, 384:LIST] = jnp.broadcast_to(total[0:1, :], (1, 128))
    own_ref[2:3, :] = jnp.full((1, PAIR), count_ref[0], I32).astype(F32)
    cols_ref[...] = send_ref[...].astype(F32).T
    for load in loads[5:]:
        load.wait()
    w_in = w_in_ref[...]
    w_c = w_in[0:SPECIES].T
    w_p = w_in[SPECIES : 2 * SPECIES].T
    w_r = w_in[2 * SPECIES :]
    gap = jnp.zeros((WIDTH, 1), F32)
    first = jnp.concatenate([w_c, gap, w_p, gap, w_r.T], axis=1)
    first_high = first.astype(BF16).astype(F32)
    first_low = first - first_high
    wx_ref[...] = jnp.concatenate(
        [first_high, first_high[:, 16:24], first_low, jnp.zeros((WIDTH, 8), F32)], axis=1
    ).astype(BF16)
    wr_high, wr_low = halves(jnp.concatenate([w_r, jnp.zeros((8, WIDTH), F32)], axis=0))
    wr_ref[...] = jnp.concatenate([wr_high, wr_high, wr_low], axis=1)
    w_mid = w_mid_ref[...]
    w_read = w_read_ref[...]
    down = jnp.concatenate(
        [exact(w_mid, w_pair_ref[...]), exact(w_mid, w_mix_ref[0:WIDTH, :])], axis=1
    )
    a_col = jnp.sum(w_mid * w_read, axis=1, keepdims=True)
    b_col = jnp.sum(w_back_ref[...] * w_read, axis=1, keepdims=True)
    ab_ref[...] = jnp.concatenate([a_col, b_col], axis=1)
    dn_ref[...] = triple(down)
    up_ref[...] = triple(down.T)
    mix = jnp.concatenate(
        [w_mix_ref[pl.ds(WIDTH + degree, CH, stride=3), :] for degree in range(3)], axis=0
    )
    mb_ref[...] = triple(mix)
    mt_ref[...] = triple(mix.T)
    half = LATE // 2
    ends = [own_ref[i : i + 1, 0:half] for i in range(2)]
    centre = jnp.concatenate(ends, axis=1)
    mate = jnp.concatenate(ends[::-1], axis=1)
    found = dot(table, one_hot(mate.astype(I32), ATOM))
    partner = jnp.concatenate([joined(found), found[9:10]], axis=0)
    index = lax.broadcasted_iota(I32, (1, half), 1).astype(F32)
    valid = jnp.concatenate([index, index], axis=1) < total[0:1, :]
    env_ref[...] = jnp.zeros_like(env_ref)
    store = (hots_ref, slope_ref, None, None, value_ref, raw_ref, geo_ref, base_ref)
    first_pass(
        centre.astype(I32), partner, mate, valid, table, store, 0, terms, env_ref, wx_ref, up_ref, ab_ref
    )
    for copy in copies:
        copy.wait()


def gather(fields, hot, around):
    width = hot.shape[1]
    around[:, 0:width] = dot(fields[...], jnp.concatenate([hot, hot], axis=0))


def scatter(terms, hot, total, count):
    width = hot.shape[1]
    for part in (slice(0, width), slice(width, 2 * width)):
        total[0:count, :] += dot_nt(terms[0:count, part], hot)


def first_pass(centre, partner, code, valid, table, store, begin, terms, env, wx_ref, up_ref, ab_ref):
    hots, slope, _, _, value, raw, geo, base = store
    width = centre.shape[1]
    here = pl.ds(begin, width)
    hot = one_hot(centre, ATOM)
    hots[:, here] = hot
    geo[CODE : CODE + 1, here] = code
    held = dot(table, hot)
    delta = partner[0:3] - joined(held)
    length2 = delta[0:1] * delta[0:1] + delta[1:2] * delta[1:2] + delta[2:3] * delta[2:3] + 1.0
    soft = jnp.sqrt(length2)
    rinv = 1.0 / soft
    unit = delta * rinv
    ux, uy, uz = unit[0:1], unit[1:2], unit[2:3]
    turn = soft * (PI / CUTOFF) - PI / 2
    t2 = turn * turn
    cosine = -turn * (
        1 + t2 * (-1 / 6 + t2 * (1 / 120 + t2 * (-1 / 5040 + t2 * (1 / 362880 - t2 / 39916800))))
    )
    sine = 1 + t2 * (
        -1 / 2 + t2 * (1 / 24 + t2 * (-1 / 720 + t2 * (1 / 40320 + t2 * (-1 / 3628800 + t2 / 479001600))))
    )
    twice = 2 * cosine
    s_old, s_now = jnp.zeros_like(sine), sine
    c_old, c_now = jnp.ones_like(sine), cosine
    for b in range(BASIS):
        geo[RAD + b : RAD + b + 1, here] = s_now * rinv
        geo[DRAD + b : DRAD + b + 1, here] = (c_now * ((b + 1) * PI / CUTOFF) - s_now * rinv) * rinv
        s_old, s_now = s_now, twice * s_now - s_old
        c_old, c_now = c_now, twice * c_now - c_old
    angular = [
        jnp.ones_like(ux),
        ROOT3 * ux,
        ROOT3 * uy,
        ROOT3 * uz,
        ROOT15 * ux * uy,
        ROOT15 * uy * uz,
        0.5 * ROOT5 * (2.0 * uz * uz - ux * ux - uy * uy),
        ROOT15 * ux * uz,
        0.5 * ROOT15 * (ux * ux - uy * uy),
    ]
    for m in range(9):
        geo[ANG + m : ANG + m + 1, here] = angular[m]
    inner = 1.0 - length2 * (1.0 / (CUTOFF * CUTOFF))
    alive = jnp.where(valid, 1.0, 0.0)
    envelope = alive * inner * inner
    geo[ENVL : ENVL + 1, here] = envelope
    geo[DENVL : DENVL + 1, here] = alive * inner * soft * (-4.0 / (CUTOFF * CUTOFF))
    geo[RINV : RINV + 1, here] = rinv
    geo[DIR : DIR + 3, here] = unit
    radial = geo[RAD : RAD + 8, here]
    radial_low = radial - radial.astype(BF16).astype(F32)
    kinds = lax.broadcasted_iota(I32, (8, width), 0)
    hot_c = jnp.where(kinds == held[9:10].astype(I32), 1.0, 0.0)
    hot_p = jnp.where(kinds == partner[3:4].astype(I32), 1.0, 0.0)
    inputs = jnp.concatenate(
        [hot_c, hot_p, radial, radial_low, hot_c, hot_p, radial, jnp.zeros((8, width), F32)], axis=0
    ).astype(BF16)
    pre = dot(wx_ref[...], inputs)
    gate = sigmoid(pre)
    act = pre * gate
    slope[:, here] = gate + act * (1.0 - gate)
    after = dot(up_ref[...], stacked(act))
    raw[:, here] = after[0:CH]
    value[:, here] = after[CH : 2 * CH]
    base[:, here] = after[2 * CH :]
    geo[ERAW : ERAW + 1, here] = jnp.sum(act * ab_ref[:, 0:1], axis=0, keepdims=True)
    weights = after[0:CH] * envelope
    for m in range(9):
        term = weights if m == 0 else weights * angular[m]
        rows = slice(m * CH, (m + 1) * CH)
        terms[rows, 0:width], terms[rows, width : 2 * width] = halves(term)
    scatter(terms, hot, env, FIELD)


def third_pass(store, begin, width, fields, around, dn_ref, wr_ref, ab_ref):
    hots, slope, mixed, mixed_low, d_value, raw_ref, geo = store
    here = pl.ds(begin, width)
    gather(fields, hots[:, here], around)
    envelope = geo[ENVL : ENVL + 1, here]
    raw = raw_ref[:, here]
    weights = raw * envelope
    d_weight = None
    d_ang = [None]
    for m in range(9):
        got = around[m * CH : (m + 1) * CH, 0:width]
        term = got if m == 0 else got * geo[ANG + m : ANG + m + 1, here]
        d_weight = term if m == 0 else d_weight + term
        if m:
            d_ang.append(
                geo[DANG + m - 1 : DANG + m, here] + jnp.sum(weights * got, axis=0, keepdims=True)
            )
    d_envelope = geo[ERAW : ERAW + 1, here] + jnp.sum(d_weight * raw, axis=0, keepdims=True)
    pair_high, pair_low = halves(jnp.concatenate([d_weight * envelope, d_value[:, here]], axis=0))
    both_high = jnp.concatenate([pair_high, mixed[:, here]], axis=0)
    both_low = jnp.concatenate([pair_low, mixed_low[:, here]], axis=0)
    d_act = dot(dn_ref[...], jnp.concatenate([both_high, both_low, both_high], axis=0))
    d_act = d_act + ab_ref[:, 0:1] * envelope
    d_radial = dot(wr_ref[...], stacked(d_act * slope[:, here]))
    d_soft = jnp.sum(d_radial[0:8] * geo[DRAD : DRAD + 8, here], axis=0, keepdims=True)
    d_soft = d_soft + d_envelope * geo[DENVL : DENVL + 1, here]
    unit = geo[DIR : DIR + 3, here]
    rinv = geo[RINV : RINV + 1, here]
    ux, uy, uz = unit[0:1], unit[1:2], unit[2:3]
    d_ux = ROOT3 * d_ang[1] + ROOT15 * (uy * d_ang[4] + uz * d_ang[7] + ux * d_ang[8]) - ROOT5 * ux * d_ang[6]
    d_uy = ROOT3 * d_ang[2] + ROOT15 * (ux * d_ang[4] + uz * d_ang[5] - uy * d_ang[8]) - ROOT5 * uy * d_ang[6]
    d_uz = ROOT3 * d_ang[3] + ROOT15 * (uy * d_ang[5] + ux * d_ang[7]) + 2.0 * ROOT5 * uz * d_ang[6]
    along = d_soft - (d_ux * ux + d_uy * uy + d_uz * uz) * rinv
    return [d * rinv + u * along for d, u in ((d_ux, ux), (d_uy, uy), (d_uz, uz))]


def to_partners(pull, geo, begin, width, at_partner):
    code = geo[CODE : CODE + 1, pl.ds(begin, width)].astype(I32)
    seg = lax.broadcasted_iota(I32, (16, width), 0) == (code >> 8)
    high, low = halves(jnp.concatenate([jnp.where(seg, g, 0.0) for g in pull], axis=0))
    hot = one_hot(code & 255, ATOM)
    sums = dot_nt(jnp.concatenate([high, low], axis=0), hot)
    at_partner[...] += sums[0:48] + sums[48:96]


def settled(pull, hot):
    sent = jnp.concatenate([*pull, jnp.zeros((5, hot.shape[1]), F32)], axis=0)
    sent = jnp.concatenate([sent, sent - sent.astype(BF16).astype(F32)], axis=0).astype(BF16)
    return dot_nt(sent, hot)


def edge_kernel(
    own_ref, table_ref, recv_ref,
    wx_ref, up_ref, dn_ref, mt_ref, mb_ref, wr_ref, ab_ref, cols_ref, home_ref,
    late_hots, late_slope, late_value, late_raw, late_geo, late_base, late_env,
    energy_ref, fields, at_centre, at_partner, hots, slope, mixed, mixed_low, d_value, raw, geo,
    edges, base, more_hots, more_slope, more_mixed, more_low, more_d_value, more_raw, more_geo,
    more_base, env, g_env, terms, around, lines, forward,
):
    first_store = (hots, slope, mixed, mixed_low, d_value, raw, geo, base)
    more_store = (
        more_hots, more_slope, more_mixed, more_low, more_d_value, more_raw, more_geo,
        more_base,
    )
    count = own_ref[2:3, 0:128][0, 0].astype(I32)
    src = own_ref[0:1, :]
    dst = own_ref[1:2, :].astype(I32)
    near = jnp.concatenate([recv_ref[k, :, 384 : 384 + GHOST] for k in range(NBR)], axis=1)
    ghosts = jnp.concatenate(
        [*thirds(near[0:3]), near[3:4], near[6:7], jnp.zeros((5, SLOTS), F32)], axis=0
    ).astype(BF16)
    table = table_ref[...]
    segments = jnp.concatenate([table, ghosts[:, 0:ATOM], ghosts[:, ATOM:SLOTS]], axis=0)
    found = dot(segments, one_hot(dst & 255, ATOM))
    part = dst >> 8
    picked = jnp.where(part == 0, found[0:16], jnp.where(part == 1, found[16:32], found[32:48]))
    beyond = (((dst - ATOM) >> 6) + 3).astype(F32) * ATOM + picked[10:11]
    code = jnp.where(part == 0, dst.astype(F32), beyond)
    forward[...] = jnp.concatenate(
        [joined(picked), picked[9:10], src, code, jnp.zeros((2, PAIR), F32)], axis=0
    )
    lane = lax.broadcasted_iota(I32, (8, 128), 1)
    row = lax.broadcasted_iota(I32, (8, 128), 0)

    def kept(ref):
        halves_of = [
            jnp.concatenate([ref[2 * i : 2 * i + 1, 256:384], ref[2 * i + 1 : 2 * i + 2, 256:384]], axis=1)
            for i in range(4)
        ]
        return atom_table(jnp.concatenate(halves_of[0:3], axis=0), halves_of[3]).astype(BF16)

    def place(size, begin, at, k, held, tile, whole=False):
        base = tile * 128 - at + begin
        first = base >> 7
        turn = base & 127
        low = jnp.clip(first, 0, 7)
        high = jnp.clip(first + 1, 0, 7)
        if k is None:
            left, right = [forward[:, pl.ds(pl.multiple_of(i * 128, 128), 128)] for i in (low, high)]
        else:
            left, right = lines[k, low], lines[k, high]
        back = lax.rem(128 - turn, 128)
        taken = jnp.where(
            lane < 128 - turn, pltpu.roll(left, back, 1), pltpu.roll(right, back, 1)
        )
        if k is not None:
            found = dot(held, one_hot(taken[5:6].astype(I32), ATOM))
            partner = jnp.concatenate([joined(found), found[9:10], jnp.zeros((4, 128), F32)], axis=0)
        if k is not None and k < NBR:
            match = lax.broadcasted_iota(I32, (GHOST, 128), 0) == taken[4:5].astype(I32)
            atom = jnp.sum(jnp.where(match, cols_ref[:, k : k + 1], 0.0), axis=0, keepdims=True)
            taken = jnp.where(row == 4, atom, taken + F32(ATOM * (3 + k)))
        if k is not None:
            taken = jnp.where(row < 4, partner, taken)
        here = pl.ds(pl.multiple_of(tile * 128, 128), 128)
        if whole:
            edges[:, here] = taken
            return
        spot = tile * 128 + lane
        inside = (spot >= at) & (spot < at + size)
        edges[:, here] = jnp.where(inside, taken, edges[:, here])

    def scalar(ref, which):
        return ref[which : which + 1, 384:LIST][0, 0].astype(I32)

    for k, ref in enumerate([recv_ref.at[k] for k in range(NBR)] + [home_ref]):
        for i in range(PAIR // 128):
            lines[k, i] = jnp.where(row == 4, ref[i : i + 1, 0:128], ref[i : i + 1, 128:256])
    inner = scalar(home_ref, 4)
    early = jnp.minimum(inner, LATE // 2)
    jobs = [(count - early, early, jnp.int32(0), None, None, PAIR // 128)]
    at = count - early
    size = inner - early
    jobs.append((size, LATE // 2, at, NBR, kept(home_ref), 0))
    at = at + size
    for k in range(NBR):
        ref = recv_ref.at[k]
        size = scalar(ref, 4)
        jobs.append((size, scalar(ref, 5), at, k, kept(ref), 2))
        at = at + size
    total = at
    for size, begin, at, k, held, usual in jobs:
        for step in range(usual):
            place(size, begin, at, k, held, (at >> 7) + step, k is None or step > 0)
    left_over = jnp.int32(0)
    for size, begin, at, k, held, usual in jobs:
        left_over = left_over + jnp.maximum(((at + size + 127) >> 7) - (at >> 7) - usual, 0)

    @pl.when(left_over > 0)
    def _():
        for size, begin, at, k, held, usual in jobs:

            def more(tile, carry, size=size, begin=begin, at=at, k=k, held=held):
                place(size, begin, at, k, held, tile)
                return carry

            lax.fori_loop((at >> 7) + usual, (at + size + 127) >> 7, more, 0)

    extra_blocks = lax.div(jnp.maximum(total - (MAIN - LATE), 0) + EXTRA - 1, EXTRA)

    env[...] = late_env[...]
    g_env[...] = jnp.zeros_like(g_env)
    terms[FIELD:, :] = jnp.zeros((16, 2 * MAIN), BF16)
    at_centre[...] = jnp.zeros_like(at_centre)
    at_partner[...] = jnp.zeros_like(at_partner)

    def second_pass(store, begin, width):
        hots, _, mixed, mixed_low, value, _, geo, base = store
        here = pl.ds(begin, width)
        hot = hots[:, here]
        gather(fields, hot, around)
        envelope = geo[ENVL : ENVL + 1, here]
        sums = [None, None, None]
        for m in range(9):
            got = around[m * CH : (m + 1) * CH, 0:width]
            term = got if m == 0 else got * geo[ANG + m : ANG + m + 1, here]
            degree = DEGREES[m]
            sums[degree] = term if sums[degree] is None else sums[degree] + term
        held = value[:, here]
        invariant = jnp.concatenate([s * held for s in sums], axis=0)
        pre = base[:, here] + dot(mt_ref[...], stacked(invariant))
        gate = sigmoid(pre)
        act = pre * gate
        back = ab_ref[:, 1:2]
        e_raw = geo[ERAW : ERAW + 1, here] + jnp.sum(act * back, axis=0, keepdims=True)
        geo[ERAW : ERAW + 1, here] = e_raw
        energy = e_raw * envelope
        energy = jnp.concatenate([energy, jnp.zeros((15, width), F32)], axis=0)
        terms[FIELD:, 0:width], terms[FIELD:, width : 2 * width] = halves(energy)
        d_pre = (gate + act * (1.0 - gate)) * back * envelope
        d_high, d_low = halves(d_pre)
        mixed[:, here] = d_high
        mixed_low[:, here] = d_low
        d_inv = dot(mb_ref[...], jnp.concatenate([d_high, d_low, d_high], axis=0))
        d_inv = [d_inv[i * CH : (i + 1) * CH] for i in range(3)]
        value[:, here] = d_inv[0] * sums[0] + d_inv[1] * sums[1] + d_inv[2] * sums[2]
        d_sum = [d * held for d in d_inv]
        for m in range(9):
            share = d_sum[DEGREES[m]]
            term = share if m == 0 else share * geo[ANG + m : ANG + m + 1, here]
            rows = slice(m * CH, (m + 1) * CH)
            terms[rows, 0:width], terms[rows, width : 2 * width] = halves(term)
            if m:
                geo[DANG + m - 1 : DANG + m, here] = jnp.sum(
                    share * around[rows, 0:width], axis=0, keepdims=True
                )
        scatter(terms, hot, g_env, FIELD + 16)

    def rest(step):
        def body(block, carry):
            step(pl.multiple_of(block * EXTRA, EXTRA))
            return carry

        lax.fori_loop(0, extra_blocks, body, 0)

    def listed(store, begin, start, width):
        valid = start + lax.broadcasted_iota(I32, (1, width), 1) < total
        part = jnp.where(valid, edges[:, pl.ds(start, width)], 0.0)
        first_pass(
            part[4:5].astype(I32), part[0:4], part[5:6], valid, table, store, begin, terms, env,
            wx_ref, up_ref, ab_ref,
        )

    listed(first_store, LATE, 0, MAIN - LATE)
    for target, source in zip(
        (hots, slope, d_value, raw, geo, base),
        (late_hots, late_slope, late_value, late_raw, late_geo, late_base),
    ):
        target[:, 0:LATE] = source[...]
    rest(lambda begin: listed(more_store, begin, pl.multiple_of(begin + (MAIN - LATE), 256), EXTRA))
    fields[:, 0:ATOM], fields[:, ATOM:] = halves(env[...] * ENV_SCALE)
    second_pass(first_store, 0, MAIN)
    rest(lambda begin: second_pass(more_store, begin, EXTRA))
    energy_ref[...] = g_env[FIELD : FIELD + 1, :]
    fields[:, 0:ATOM], fields[:, ATOM:] = halves(g_env[0:FIELD, :] * ENV_SCALE)

    def third(begin):
        pull = third_pass(
            (more_hots, more_slope, more_mixed, more_low, more_d_value, more_raw, more_geo),
            begin, EXTRA, fields, around, dn_ref, wr_ref, ab_ref,
        )
        to_partners(pull, more_geo, begin, EXTRA, at_partner)
        at_centre[...] += settled(pull, more_hots[:, pl.ds(begin, EXTRA)])

    rest(third)


def return_kernel(
    dn_ref, wr_ref, ab_ref,
    fields, more_centre, more_partner, hots, slope, mixed, mixed_low, d_value, raw, geo,
    out_ref, outbox, inbox, around, at_partner, send_sem, recv_sem,
):
    barrier, peers = greet()
    at_partner[...] = more_partner[...]
    store = (hots, slope, mixed, mixed_low, d_value, raw, geo)
    weights = (fields, around, dn_ref, wr_ref, ab_ref)
    pull = third_pass(store, LATE, MAIN - LATE, *weights)
    to_partners(pull, geo, LATE, MAIN - LATE, at_partner)
    parts = at_partner[...]
    for k in range(NBR):
        for i in range(3):
            for half in range(2):
                outbox[k, 3 * half + i : 3 * half + i + 1, :] = parts[
                    16 * i + 3 + k : 16 * i + 4 + k, half * 128 : (half + 1) * 128
                ]
        outbox[k, 6:8, :] = jnp.zeros((2, 128), F32)
    pl.semaphore_wait(barrier, NBR)
    copies = swap(peers, outbox, inbox, send_sem, recv_sem)
    sums = more_centre[...] + settled(pull, hots[:, LATE:MAIN])
    pull = third_pass(store, 0, LATE, *weights)
    mates = one_hot(geo[CODE : CODE + 1, 0:LATE].astype(I32), ATOM)
    sums = sums + settled(pull, hots[:, 0:LATE]) - settled(pull, mates)
    total = sums[0:3] + sums[8:11]
    total = total - jnp.concatenate([parts[16 * i : 16 * i + 1] for i in range(3)], axis=0)
    for copy in copies:
        copy.wait()
    arrived = inbox[0]
    for k in range(1, NBR):
        arrived = arrived + inbox[k]
    out_ref[...] = total - jnp.concatenate([arrived[0:3], arrived[3:6]], axis=1)


def edge_call(*operands):
    shape = jax.ShapeDtypeStruct
    rest = NBR * PAIR

    def store(lanes, make):
        return [
            make((ATOM, lanes), BF16),
            make((WIDTH, lanes), F32),
            make((WIDTH, lanes), BF16),
            make((WIDTH, lanes), BF16),
            make((CH, lanes), F32),
            make((CH, lanes), F32),
            make((ROWS, lanes), F32),
        ]

    return pl.pallas_call(
        edge_kernel,
        out_shape=(
            shape((1, ATOM), F32),
            shape((FIELD, 2 * ATOM), BF16),
            shape((16, ATOM), F32),
            shape((48, ATOM), F32),
            *store(MAIN, shape),
        ),
        in_specs=[VMEM] * 19,
        out_specs=[VMEM] * 11,
        scratch_shapes=[
            pltpu.VMEM((8, CAP + 512), F32),
            pltpu.VMEM((WIDTH, MAIN), F32),
            *store(rest, pltpu.VMEM),
            pltpu.VMEM((WIDTH, rest), F32),
            pltpu.VMEM((FIELD, ATOM), F32),
            pltpu.VMEM((FIELD + 16, ATOM), F32),
            pltpu.VMEM((FIELD + 16, 2 * MAIN), BF16),
            pltpu.VMEM((FIELD, MAIN), F32),
            pltpu.VMEM((NBR + 1, PAIR // 128, 8, 128), F32),
            pltpu.VMEM((8, PAIR), F32),
        ],
        compiler_params=pltpu.CompilerParams(vmem_limit_bytes=43 << 20),
    )(*operands)


def per_device(
    positions, species, send_list, edge_src, edge_dst, edge_count,
    w_in, w_mid, w_pair, w_mix, w_back, w_read,
):
    sends = send_list[0]
    shape = jax.ShapeDtypeStruct
    shared = pl.pallas_call(
        share_kernel,
        out_shape=(
            shape((8, PAIR), F32),
            shape((16, ATOM), BF16),
            shape((NBR, 8, LIST), F32),
            shape((WIDTH, 64), BF16),
            shape((2 * WIDTH, 3 * WIDTH), BF16),
            shape((WIDTH, 6 * WIDTH), BF16),
            shape((WIDTH, 9 * CH), BF16),
            shape((3 * CH, 3 * WIDTH), BF16),
            shape((16, 3 * WIDTH), BF16),
            shape((WIDTH, 2), F32),
            shape((GHOST, NBR), F32),
            shape((8, LIST), F32),
            shape((ATOM, LATE), BF16),
            shape((WIDTH, LATE), F32),
            shape((CH, LATE), F32),
            shape((CH, LATE), F32),
            shape((ROWS, LATE), F32),
            shape((WIDTH, LATE), F32),
            shape((FIELD, ATOM), F32),
        ),
        in_specs=[SMEM] + [HBM] * 11,
        out_specs=[VMEM] * 19,
        scratch_shapes=[
            pltpu.VMEM((3, ATOM), F32),
            pltpu.VMEM((1, ATOM), I32),
            pltpu.VMEM((NBR, GHOST), I32),
            pltpu.VMEM((1, PAIR), I32),
            pltpu.VMEM((1, PAIR), I32),
            pltpu.VMEM((2 * SPECIES + BASIS, WIDTH), F32),
            pltpu.VMEM((WIDTH, WIDTH), F32),
            pltpu.VMEM((WIDTH, WIDTH), F32),
            pltpu.VMEM((WIDTH + 3 * CH, WIDTH), F32),
            pltpu.VMEM((WIDTH, WIDTH), F32),
            pltpu.VMEM((1, WIDTH), F32),
            pltpu.VMEM((NBR, 8, LIST), F32),
            pltpu.VMEM((8, 384), F32),
            pltpu.VMEM((FIELD, 2 * LATE), BF16),
            pltpu.SemaphoreType.DMA((11,)),
            pltpu.SemaphoreType.DMA((NBR,)),
            pltpu.SemaphoreType.DMA((NBR,)),
        ],
        compiler_params=pltpu.CompilerParams(
            collective_id=0, has_side_effects=True, vmem_limit_bytes=14 << 20
        ),
    )(
        edge_count,
        *(
            pltpu.with_memory_space_constraint(x, pltpu.HBM)
            for x in (
                positions, species.reshape(1, ATOM), sends, edge_src, edge_dst,
                w_in, w_mid, w_pair, w_mix, w_back, w_read.reshape(1, WIDTH),
            )
        ),
    )
    energy, *kept = edge_call(*shared)
    dn, wr, ab = shared[5], shared[8], shared[9]
    forces = pl.pallas_call(
        return_kernel,
        out_shape=shape((3, ATOM), F32),
        in_specs=[VMEM] * 13,
        out_specs=VMEM,
        scratch_shapes=[
            pltpu.VMEM((NBR, 8, 128), F32),
            pltpu.VMEM((NBR, 8, 128), F32),
            pltpu.VMEM((FIELD, MAIN - LATE), F32),
            pltpu.VMEM((48, ATOM), F32),
            pltpu.SemaphoreType.DMA((NBR,)),
            pltpu.SemaphoreType.DMA((NBR,)),
        ],
        compiler_params=pltpu.CompilerParams(
            collective_id=1, has_side_effects=True, vmem_limit_bytes=20 << 20
        ),
    )(dn, wr, ab, *kept)
    return forces, energy.reshape(ATOM)


def solution(mesh):
    both = ("dom", "face")
    placed = (
        P(None, both), P(both), P(both, None, None), P(both, None), P(both, None), P(both),
        P(), P(), P(), P(), P(), P(),
    )
    return jax.shard_map(
        per_device,
        mesh=mesh,
        in_specs=placed,
        out_specs=(P(None, both), P(both)),
        check_vma=False,
    )
```

```python
import functools

import jax
import jax.numpy as jnp
from jax import lax
from jax.experimental import pallas as pl
from jax.experimental.pallas import tpu as pltpu
from jax.sharding import PartitionSpec as P

CH = 64
WIDTH = 128
BASIS = 8
SPECIES = 7
ENV_SCALE = 0.2
CUTOFF = 6.0
PI = 3.141592653589793
DIRECTIONS = ((-1, -1), (-1, 0), (-1, 1), (0, -1), (0, 1), (1, -1), (1, 0), (1, 1))
NBR = 8
FAR_FIRST = (0, 7, 2, 5, 3, 4, 1, 6)
ATOM = 256
GHOST = 64
PAIR = 1024
SLOTS = NBR * GHOST
LIST = 512
CAP = 10 * PAIR
MAIN = 2048
LATE = 768
EXTRA = 512
F32 = jnp.float32
BF16 = jnp.bfloat16
I32 = jnp.int32
MESH = pl.DeviceIdType.MESH
VMEM = pl.BlockSpec(memory_space=pltpu.VMEM)
SMEM = pl.BlockSpec(memory_space=pltpu.SMEM)
HBM = pl.BlockSpec(memory_space=pltpu.HBM)

RAD, DRAD, ANG, ENVL, DENVL, RINV, DIR, ERAW, DANG, CODE, ROWS = 0, 8, 16, 25, 26, 27, 28, 31, 32, 40, 48
FIELD = 9 * CH
ROOT3, ROOT5, ROOT15 = 3.0**0.5, 5.0**0.5, 15.0**0.5
DEGREES = (0, 1, 1, 1, 2, 2, 2, 2, 2)


def dot(a, b):
    return lax.dot_general(a, b, (((1,), (0,)), ((), ())), preferred_element_type=F32)


def dot_nt(a, b):
    return lax.dot_general(a, b, (((1,), (1,)), ((), ())), preferred_element_type=F32)


def exact(a, b):
    return jnp.dot(a, b, precision=lax.Precision.HIGHEST, preferred_element_type=F32)


def halves(x):
    high = x.astype(BF16)
    return high, (x - high.astype(F32)).astype(BF16)


def thirds(x):
    high = x.astype(BF16).astype(F32)
    rest = x - high
    mid = rest.astype(BF16).astype(F32)
    return high, mid, rest - mid


def sigmoid(x):
    return 0.5 * jnp.tanh(0.5 * x) + 0.5


def triple(weight):
    high, low = halves(weight)
    return jnp.concatenate([high, high, low], axis=1)


def stacked(x):
    high, low = halves(x)
    return jnp.concatenate([high, low, high], axis=0)


def one_hot(row, count):
    rows = lax.broadcasted_iota(I32, (count, row.shape[1]), 0).astype(F32).astype(BF16)
    match = rows == row.astype(F32).astype(BF16)
    return jnp.where(match, jnp.ones_like(rows), jnp.zeros_like(rows))


def atom_table(coords, kinds):
    parts = thirds(coords)
    pad = jnp.zeros((6, coords.shape[1]), F32)
    return jnp.concatenate([*parts, kinds, pad], axis=0)


def joined(rows):
    return rows[0:3] + rows[3:6] + rows[6:9]


def greet():
    here = [lax.axis_index("dom"), lax.axis_index("face")]
    sizes = [lax.axis_size("dom"), lax.axis_size("face")]
    peers = []
    for shift in DIRECTIONS:
        peers.append(
            tuple(lax.rem(at + by + size, size) for at, by, size in zip(here, shift, sizes))
        )
    barrier = pltpu.get_barrier_semaphore()
    for k in FAR_FIRST:
        pl.semaphore_signal(barrier, inc=1, device_id=peers[k], device_id_type=MESH)
    return barrier, peers


def swap(peers, out_ref, in_ref, send_sem, recv_sem):
    copies = []
    for k, peer in enumerate(peers):
        copies.append(
            pltpu.make_async_remote_copy(
                src_ref=out_ref.at[k],
                dst_ref=in_ref.at[NBR - 1 - k],
                send_sem=send_sem.at[k],
                recv_sem=recv_sem.at[NBR - 1 - k],
                device_id=peer,
                device_id_type=MESH,
            )
        )
    for k in FAR_FIRST:
        copies[k].start()
    return copies


def share_kernel(
    count_ref, *refs,
):
    sources, refs = refs[:11], refs[11:]
    (
        own_ref, table_ref, recv_ref, wx_ref, up_ref, dn_ref, mt_ref, mb_ref, wr_ref, ab_ref, cols_ref,
        home_ref, hots_ref, slope_ref, value_ref, raw_ref, geo_ref, base_ref, env_ref,
    ) = refs[:19]
    held, refs = refs[19:30], refs[30:]
    out_buf, order_buf, terms, load_sem, send_sem, recv_sem = refs
    (
        pos_ref, spec_ref, send_ref, src_ref, dst_ref,
        w_in_ref, w_mid_ref, w_pair_ref, w_mix_ref, w_back_ref, w_read_ref,
    ) = held
    loads = [
        pltpu.make_async_copy(source, target, load_sem.at[i])
        for i, (source, target) in enumerate(zip(sources, held))
    ]
    for load in loads[:5]:
        load.start()
    barrier, peers = greet()
    for load in loads[5:]:
        load.start()
    for load in loads[:5]:
        load.wait()
    table = atom_table(pos_ref[...], spec_ref[...].astype(F32)).astype(BF16)
    table_ref[...] = table
    sends = jnp.concatenate([send_ref[k : k + 1, :] for k in range(NBR)], axis=1)
    ghosts = dot(table, one_hot(sends, ATOM))
    ghost_rows = jnp.concatenate([joined(ghosts), ghosts[9:10]], axis=0)
    src = src_ref[...]
    dst = dst_ref[...]
    lanes = lax.broadcasted_iota(I32, (1, PAIR), 1)
    live = lanes < count_ref[0]
    ghost = dst >= ATOM
    away = dst - ATOM
    bucket = jnp.where(ghost, (away >> 6) + 1, 0)
    bucket = jnp.where(live, bucket, 15)
    place = jnp.where(ghost, away & 63, dst)
    member = jnp.where(lax.broadcasted_iota(I32, (16, PAIR), 0) == bucket, 1.0, 0.0)
    before = lax.broadcasted_iota(I32, (ATOM, ATOM), 0) < lax.broadcasted_iota(I32, (ATOM, ATOM), 1)
    before = jnp.where(before, 1.0, 0.0).astype(BF16)
    pieces = [member[:, i * ATOM : (i + 1) * ATOM] for i in range(PAIR // ATOM)]
    ranks = dot(jnp.concatenate(pieces, axis=0).astype(BF16), before)
    sums = [jnp.sum(piece, axis=1, keepdims=True) for piece in pieces]
    total = sums[0] + sums[1] + sums[2] + sums[3]
    start = jnp.zeros((16, 1), F32)
    index = lax.broadcasted_iota(I32, (16, 1), 0)
    for b in range(NBR + 1):
        start = start + jnp.where(index > b, total[b : b + 1, :], 0.0)
    offset = start
    spots = []
    for i, piece in enumerate(pieces):
        where = ranks[16 * i : 16 * (i + 1)] + offset
        spots.append(jnp.sum(piece * where, axis=0, keepdims=True))
        offset = offset + sums[i]
    spot = jnp.concatenate(spots, axis=1)
    spot = jnp.where(live, spot, -1.0).astype(I32)
    data = jnp.concatenate(
        [
            place.astype(F32), src.astype(F32), (dst >> 8).astype(F32), (dst & 255).astype(F32),
            jnp.zeros((12, PAIR), F32),
        ],
        axis=0,
    ).astype(BF16)
    for i in range(PAIR // ATOM):
        ordered = dot_nt(data, one_hot(spot - i * ATOM, ATOM))
        span = slice(i * ATOM, (i + 1) * ATOM)
        own_ref[0:1, span] = ordered[1:2]
        own_ref[1:2, span] = ordered[2:3] * ATOM + ordered[3:4]
        for j in range(2):
            for half in range(2):
                order_buf[2 * i + half : 2 * i + half + 1, j * 128 : (j + 1) * 128] = ordered[
                    j : j + 1, half * 128 : (half + 1) * 128
                ]
    atoms = jnp.concatenate([pos_ref[...], spec_ref[...].astype(F32)], axis=0)
    for i in range(4):
        for half in range(2):
            order_buf[2 * i + half : 2 * i + half + 1, 256:384] = atoms[
                i : i + 1, half * 128 : (half + 1) * 128
            ]
    entries = order_buf[...]
    none = jnp.zeros((8, GHOST), F32)
    indices = sends.astype(F32)
    for k in range(NBR):
        out_buf[k, :, 0:384] = entries
        part = slice(k * GHOST, (k + 1) * GHOST)
        mine = jnp.concatenate([ghost_rows[:, part], none[0:2], indices[:, part], none[0:1]], axis=0)
        out_buf[k, :, 384:LIST] = jnp.concatenate([mine, none], axis=1)
        out_buf[k, 4:5, 384:LIST] = jnp.broadcast_to(total[k + 1 : k + 2, :], (1, 128))
        out_buf[k, 5:6, 384:LIST] = jnp.broadcast_to(start[k + 1 : k + 2, :], (1, 128))
    pl.semaphore_wait(barrier, NBR)
    copies = swap(peers, out_buf, recv_ref, send_sem, recv_sem)
    home_ref[:, 0:384] = entries
    home_ref[:, 384:LIST] = jnp.zeros((8, 128), F32)
    home_ref[4:5, 384:LIST] = jnp.broadcast_to(total[0:1, :], (1, 128))
    own_ref[2:3, :] = jnp.full((1, PAIR), count_ref[0], I32).astype(F32)
    cols_ref[...] = send_ref[...].astype(F32).T
    for load in loads[5:]:
        load.wait()
    w_in = w_in_ref[...]
    w_c = w_in[0:SPECIES].T
    w_p = w_in[SPECIES : 2 * SPECIES].T
    w_r = w_in[2 * SPECIES :]
    gap = jnp.zeros((WIDTH, 1), F32)
    first = jnp.concatenate([w_c, gap, w_p, gap, w_r.T], axis=1)
    first_high = first.astype(BF16).astype(F32)
    first_low = first - first_high
    wx_ref[...] = jnp.concatenate(
        [first_high, first_high[:, 16:24], first_low, jnp.zeros((WIDTH, 8), F32)], axis=1
    ).astype(BF16)
    wr_high, wr_low = halves(jnp.concatenate([w_r, jnp.zeros((8, WIDTH), F32)], axis=0))
    wr_ref[...] = jnp.concatenate([wr_high, wr_high, wr_low], axis=1)
    w_mid = w_mid_ref[...]
    w_read = w_read_ref[...]
    down = jnp.concatenate(
        [exact(w_mid, w_pair_ref[...]), exact(w_mid, w_mix_ref[0:WIDTH, :])], axis=1
    )
    a_col = jnp.sum(w_mid * w_read, axis=1, keepdims=True)
    b_col = jnp.sum(w_back_ref[...] * w_read, axis=1, keepdims=True)
    ab_ref[...] = jnp.concatenate([a_col, b_col], axis=1)
    dn_ref[...] = triple(down)
    up_ref[...] = triple(down.T)
    mix = jnp.concatenate(
        [w_mix_ref[pl.ds(WIDTH + degree, CH, stride=3), :] for degree in range(3)], axis=0
    )
    mb_ref[...] = triple(mix)
    mt_ref[...] = triple(mix.T)
    half = LATE // 2
    ends = [own_ref[i : i + 1, 0:half] for i in range(2)]
    centre = jnp.concatenate(ends, axis=1)
    mate = jnp.concatenate(ends[::-1], axis=1)
    found = dot(table, one_hot(mate.astype(I32), ATOM))
    partner = jnp.concatenate([joined(found), found[9:10]], axis=0)
    index = lax.broadcasted_iota(I32, (1, half), 1).astype(F32)
    valid = jnp.concatenate([index, index], axis=1) < total[0:1, :]
    env_ref[...] = jnp.zeros_like(env_ref)
    store = (hots_ref, slope_ref, None, None, value_ref, raw_ref, geo_ref, base_ref)
    first_pass(
        centre.astype(I32), partner, mate, valid, table, store, 0, terms, env_ref, wx_ref, up_ref, ab_ref
    )
    for copy in copies:
        copy.wait()


def gather(fields, hot, around):
    width = hot.shape[1]
    around[:, 0:width] = dot(fields[...], jnp.concatenate([hot, hot], axis=0))


def scatter(terms, hot, total, count):
    width = hot.shape[1]
    for part in (slice(0, width), slice(width, 2 * width)):
        total[0:count, :] += dot_nt(terms[0:count, part], hot)


def first_pass(centre, partner, code, valid, table, store, begin, terms, env, wx_ref, up_ref, ab_ref):
    hots, slope, _, _, value, raw, geo, base = store
    width = centre.shape[1]
    here = pl.ds(begin, width)
    hot = one_hot(centre, ATOM)
    hots[:, here] = hot
    geo[CODE : CODE + 1, here] = code
    held = dot(table, hot)
    delta = partner[0:3] - joined(held)
    length2 = delta[0:1] * delta[0:1] + delta[1:2] * delta[1:2] + delta[2:3] * delta[2:3] + 1.0
    soft = jnp.sqrt(length2)
    rinv = 1.0 / soft
    unit = delta * rinv
    ux, uy, uz = unit[0:1], unit[1:2], unit[2:3]
    turn = soft * (PI / CUTOFF) - PI / 2
    t2 = turn * turn
    cosine = -turn * (
        1 + t2 * (-1 / 6 + t2 * (1 / 120 + t2 * (-1 / 5040 + t2 * (1 / 362880 - t2 / 39916800))))
    )
    sine = 1 + t2 * (
        -1 / 2 + t2 * (1 / 24 + t2 * (-1 / 720 + t2 * (1 / 40320 + t2 * (-1 / 3628800 + t2 / 479001600))))
    )
    twice = 2 * cosine
    s_old, s_now = jnp.zeros_like(sine), sine
    c_old, c_now = jnp.ones_like(sine), cosine
    for b in range(BASIS):
        geo[RAD + b : RAD + b + 1, here] = s_now * rinv
        geo[DRAD + b : DRAD + b + 1, here] = (c_now * ((b + 1) * PI / CUTOFF) - s_now * rinv) * rinv
        s_old, s_now = s_now, twice * s_now - s_old
        c_old, c_now = c_now, twice * c_now - c_old
    angular = [
        jnp.ones_like(ux),
        ROOT3 * ux,
        ROOT3 * uy,
        ROOT3 * uz,
        ROOT15 * ux * uy,
        ROOT15 * uy * uz,
        0.5 * ROOT5 * (2.0 * uz * uz - ux * ux - uy * uy),
        ROOT15 * ux * uz,
        0.5 * ROOT15 * (ux * ux - uy * uy),
    ]
    for m in range(9):
        geo[ANG + m : ANG + m + 1, here] = angular[m]
    inner = 1.0 - length2 * (1.0 / (CUTOFF * CUTOFF))
    alive = jnp.where(valid, 1.0, 0.0)
    envelope = alive * inner * inner
    geo[ENVL : ENVL + 1, here] = envelope
    geo[DENVL : DENVL + 1, here] = alive * inner * soft * (-4.0 / (CUTOFF * CUTOFF))
    geo[RINV : RINV + 1, here] = rinv
    geo[DIR : DIR + 3, here] = unit
    radial = geo[RAD : RAD + 8, here]
    radial_low = radial - radial.astype(BF16).astype(F32)
    kinds = lax.broadcasted_iota(I32, (8, width), 0)
    hot_c = jnp.where(kinds == held[9:10].astype(I32), 1.0, 0.0)
    hot_p = jnp.where(kinds == partner[3:4].astype(I32), 1.0, 0.0)
    inputs = jnp.concatenate(
        [hot_c, hot_p, radial, radial_low, hot_c, hot_p, radial, jnp.zeros((8, width), F32)], axis=0
    ).astype(BF16)
    pre = dot(wx_ref[...], inputs)
    gate = sigmoid(pre)
    act = pre * gate
    slope[:, here] = gate + act * (1.0 - gate)
    after = dot(up_ref[...], stacked(act))
    raw[:, here] = after[0:CH]
    value[:, here] = after[CH : 2 * CH]
    base[:, here] = after[2 * CH :]
    geo[ERAW : ERAW + 1, here] = jnp.sum(act * ab_ref[:, 0:1], axis=0, keepdims=True)
    weights = after[0:CH] * envelope
    for m in range(9):
        term = weights if m == 0 else weights * angular[m]
        rows = slice(m * CH, (m + 1) * CH)
        terms[rows, 0:width], terms[rows, width : 2 * width] = halves(term)
    scatter(terms, hot, env, FIELD)


def third_pass(store, begin, width, fields, around, dn_ref, wr_ref, ab_ref):
    hots, slope, mixed, mixed_low, d_value, raw_ref, geo = store
    here = pl.ds(begin, width)
    gather(fields, hots[:, here], around)
    envelope = geo[ENVL : ENVL + 1, here]
    raw = raw_ref[:, here]
    weights = raw * envelope
    d_weight = None
    d_ang = [None]
    for m in range(9):
        got = around[m * CH : (m + 1) * CH, 0:width]
        term = got if m == 0 else got * geo[ANG + m : ANG + m + 1, here]
        d_weight = term if m == 0 else d_weight + term
        if m:
            d_ang.append(
                geo[DANG + m - 1 : DANG + m, here] + jnp.sum(weights * got, axis=0, keepdims=True)
            )
    d_envelope = geo[ERAW : ERAW + 1, here] + jnp.sum(d_weight * raw, axis=0, keepdims=True)
    pair_high, pair_low = halves(jnp.concatenate([d_weight * envelope, d_value[:, here]], axis=0))
    both_high = jnp.concatenate([pair_high, mixed[:, here]], axis=0)
    both_low = jnp.concatenate([pair_low, mixed_low[:, here]], axis=0)
    d_act = dot(dn_ref[...], jnp.concatenate([both_high, both_low, both_high], axis=0))
    d_act = d_act + ab_ref[:, 0:1] * envelope
    d_radial = dot(wr_ref[...], stacked(d_act * slope[:, here]))
    d_soft = jnp.sum(d_radial[0:8] * geo[DRAD : DRAD + 8, here], axis=0, keepdims=True)
    d_soft = d_soft + d_envelope * geo[DENVL : DENVL + 1, here]
    unit = geo[DIR : DIR + 3, here]
    rinv = geo[RINV : RINV + 1, here]
    ux, uy, uz = unit[0:1], unit[1:2], unit[2:3]
    d_ux = ROOT3 * d_ang[1] + ROOT15 * (uy * d_ang[4] + uz * d_ang[7] + ux * d_ang[8]) - ROOT5 * ux * d_ang[6]
    d_uy = ROOT3 * d_ang[2] + ROOT15 * (ux * d_ang[4] + uz * d_ang[5] - uy * d_ang[8]) - ROOT5 * uy * d_ang[6]
    d_uz = ROOT3 * d_ang[3] + ROOT15 * (uy * d_ang[5] + ux * d_ang[7]) + 2.0 * ROOT5 * uz * d_ang[6]
    along = d_soft - (d_ux * ux + d_uy * uy + d_uz * uz) * rinv
    return [d * rinv + u * along for d, u in ((d_ux, ux), (d_uy, uy), (d_uz, uz))]


def to_partners(pull, geo, begin, width, at_partner):
    code = geo[CODE : CODE + 1, pl.ds(begin, width)].astype(I32)
    seg = lax.broadcasted_iota(I32, (16, width), 0) == (code >> 8)
    high, low = halves(jnp.concatenate([jnp.where(seg, g, 0.0) for g in pull], axis=0))
    hot = one_hot(code & 255, ATOM)
    sums = dot_nt(jnp.concatenate([high, low], axis=0), hot)
    at_partner[...] += sums[0:48] + sums[48:96]


def settled(pull, hot):
    sent = jnp.concatenate([*pull, jnp.zeros((5, hot.shape[1]), F32)], axis=0)
    sent = jnp.concatenate([sent, sent - sent.astype(BF16).astype(F32)], axis=0).astype(BF16)
    return dot_nt(sent, hot)


def edge_kernel(
    own_ref, table_ref, recv_ref,
    wx_ref, up_ref, dn_ref, mt_ref, mb_ref, wr_ref, ab_ref, cols_ref, home_ref,
    late_hots, late_slope, late_value, late_raw, late_geo, late_base, late_env,
    energy_ref, fields, at_centre, at_partner, hots, slope, mixed, mixed_low, d_value, raw, geo,
    edges, base, more_hots, more_slope, more_mixed, more_low, more_d_value, more_raw, more_geo,
    more_base, env, g_env, terms, around, lines, forward,
):
    first_store = (hots, slope, mixed, mixed_low, d_value, raw, geo, base)
    more_store = (
        more_hots, more_slope, more_mixed, more_low, more_d_value, more_raw, more_geo,
        more_base,
    )
    count = own_ref[2:3, 0:128][0, 0].astype(I32)
    src = own_ref[0:1, :]
    dst = own_ref[1:2, :].astype(I32)
    near = jnp.concatenate([recv_ref[k, :, 384 : 384 + GHOST] for k in range(NBR)], axis=1)
    ghosts = jnp.concatenate(
        [*thirds(near[0:3]), near[3:4], near[6:7], jnp.zeros((5, SLOTS), F32)], axis=0
    ).astype(BF16)
    table = table_ref[...]
    segments = jnp.concatenate([table, ghosts[:, 0:ATOM], ghosts[:, ATOM:SLOTS]], axis=0)
    found = dot(segments, one_hot(dst & 255, ATOM))
    part = dst >> 8
    picked = jnp.where(part == 0, found[0:16], jnp.where(part == 1, found[16:32], found[32:48]))
    beyond = (((dst - ATOM) >> 6) + 3).astype(F32) * ATOM + picked[10:11]
    code = jnp.where(part == 0, dst.astype(F32), beyond)
    forward[...] = jnp.concatenate(
        [joined(picked), picked[9:10], src, code, jnp.zeros((2, PAIR), F32)], axis=0
    )
    lane = lax.broadcasted_iota(I32, (8, 128), 1)
    row = lax.broadcasted_iota(I32, (8, 128), 0)

    def kept(ref):
        halves_of = [
            jnp.concatenate([ref[2 * i : 2 * i + 1, 256:384], ref[2 * i + 1 : 2 * i + 2, 256:384]], axis=1)
            for i in range(4)
        ]
        return atom_table(jnp.concatenate(halves_of[0:3], axis=0), halves_of[3]).astype(BF16)

    def place(size, begin, at, k, held, tile, whole=False):
        base = tile * 128 - at + begin
        first = base >> 7
        turn = base & 127
        low = jnp.clip(first, 0, 7)
        high = jnp.clip(first + 1, 0, 7)
        if k is None:
            left, right = [forward[:, pl.ds(pl.multiple_of(i * 128, 128), 128)] for i in (low, high)]
        else:
            left, right = lines[k, low], lines[k, high]
        back = lax.rem(128 - turn, 128)
        taken = jnp.where(
            lane < 128 - turn, pltpu.roll(left, back, 1), pltpu.roll(right, back, 1)
        )
        if k is not None:
            found = dot(held, one_hot(taken[5:6].astype(I32), ATOM))
            partner = jnp.concatenate([joined(found), found[9:10], jnp.zeros((4, 128), F32)], axis=0)
        if k is not None and k < NBR:
            match = lax.broadcasted_iota(I32, (GHOST, 128), 0) == taken[4:5].astype(I32)
            atom = jnp.sum(jnp.where(match, cols_ref[:, k : k + 1], 0.0), axis=0, keepdims=True)
            taken = jnp.where(row == 4, atom, taken + F32(ATOM * (3 + k)))
        if k is not None:
            taken = jnp.where(row < 4, partner, taken)
        here = pl.ds(pl.multiple_of(tile * 128, 128), 128)
        if whole:
            edges[:, here] = taken
            return
        spot = tile * 128 + lane
        inside = (spot >= at) & (spot < at + size)
        edges[:, here] = jnp.where(inside, taken, edges[:, here])

    def scalar(ref, which):
        return ref[which : which + 1, 384:LIST][0, 0].astype(I32)

    for k, ref in enumerate([recv_ref.at[k] for k in range(NBR)] + [home_ref]):
        for i in range(PAIR // 128):
            lines[k, i] = jnp.where(row == 4, ref[i : i + 1, 0:128], ref[i : i + 1, 128:256])
    inner = scalar(home_ref, 4)
    early = jnp.minimum(inner, LATE // 2)
    jobs = [(count - early, early, jnp.int32(0), None, None, PAIR // 128)]
    at = count - early
    size = inner - early
    jobs.append((size, LATE // 2, at, NBR, kept(home_ref), 0))
    at = at + size
    for k in range(NBR):
        ref = recv_ref.at[k]
        size = scalar(ref, 4)
        jobs.append((size, scalar(ref, 5), at, k, kept(ref), 2))
        at = at + size
    total = at
    for size, begin, at, k, held, usual in jobs:
        for step in range(usual):
            place(size, begin, at, k, held, (at >> 7) + step, k is None or step > 0)
    left_over = jnp.int32(0)
    for size, begin, at, k, held, usual in jobs:
        left_over = left_over + jnp.maximum(((at + size + 127) >> 7) - (at >> 7) - usual, 0)

    @pl.when(left_over > 0)
    def _():
        for size, begin, at, k, held, usual in jobs:

            def more(tile, carry, size=size, begin=begin, at=at, k=k, held=held):
                place(size, begin, at, k, held, tile)
                return carry

            lax.fori_loop((at >> 7) + usual, (at + size + 127) >> 7, more, 0)

    extra_blocks = lax.div(jnp.maximum(total - (MAIN - LATE), 0) + EXTRA - 1, EXTRA)

    env[...] = late_env[...]
    g_env[...] = jnp.zeros_like(g_env)
    terms[FIELD:, :] = jnp.zeros((16, 2 * MAIN), BF16)
    at_centre[...] = jnp.zeros_like(at_centre)
    at_partner[...] = jnp.zeros_like(at_partner)

    def second_pass(store, begin, width):
        hots, _, mixed, mixed_low, value, _, geo, base = store
        here = pl.ds(begin, width)
        hot = hots[:, here]
        gather(fields, hot, around)
        envelope = geo[ENVL : ENVL + 1, here]
        sums = [None, None, None]
        for m in range(9):
            got = around[m * CH : (m + 1) * CH, 0:width]
            term = got if m == 0 else got * geo[ANG + m : ANG + m + 1, here]
            degree = DEGREES[m]
            sums[degree] = term if sums[degree] is None else sums[degree] + term
        held = value[:, here]
        invariant = jnp.concatenate([s * held for s in sums], axis=0)
        pre = base[:, here] + dot(mt_ref[...], stacked(invariant))
        gate = sigmoid(pre)
        act = pre * gate
        back = ab_ref[:, 1:2]
        e_raw = geo[ERAW : ERAW + 1, here] + jnp.sum(act * back, axis=0, keepdims=True)
        geo[ERAW : ERAW + 1, here] = e_raw
        energy = e_raw * envelope
        energy = jnp.concatenate([energy, jnp.zeros((15, width), F32)], axis=0)
        terms[FIELD:, 0:width], terms[FIELD:, width : 2 * width] = halves(energy)
        d_pre = (gate + act * (1.0 - gate)) * back * envelope
        d_high, d_low = halves(d_pre)
        mixed[:, here] = d_high
        mixed_low[:, here] = d_low
        d_inv = dot(mb_ref[...], jnp.concatenate([d_high, d_low, d_high], axis=0))
        d_inv = [d_inv[i * CH : (i + 1) * CH] for i in range(3)]
        value[:, here] = d_inv[0] * sums[0] + d_inv[1] * sums[1] + d_inv[2] * sums[2]
        d_sum = [d * held for d in d_inv]
        for m in range(9):
            share = d_sum[DEGREES[m]]
            term = share if m == 0 else share * geo[ANG + m : ANG + m + 1, here]
            rows = slice(m * CH, (m + 1) * CH)
            terms[rows, 0:width], terms[rows, width : 2 * width] = halves(term)
            if m:
                geo[DANG + m - 1 : DANG + m, here] = jnp.sum(
                    share * around[rows, 0:width], axis=0, keepdims=True
                )
        scatter(terms, hot, g_env, FIELD + 16)

    def rest(step):
        def body(block, carry):
            step(pl.multiple_of(block * EXTRA, EXTRA))
            return carry

        lax.fori_loop(0, extra_blocks, body, 0)

    def listed(store, begin, start, width):
        valid = start + lax.broadcasted_iota(I32, (1, width), 1) < total
        part = jnp.where(valid, edges[:, pl.ds(start, width)], 0.0)
        first_pass(
            part[4:5].astype(I32), part[0:4], part[5:6], valid, table, store, begin, terms, env,
            wx_ref, up_ref, ab_ref,
        )

    listed(first_store, LATE, 0, MAIN - LATE)
    for target, source in zip(
        (hots, slope, d_value, raw, geo, base),
        (late_hots, late_slope, late_value, late_raw, late_geo, late_base),
    ):
        target[:, 0:LATE] = source[...]
    rest(lambda begin: listed(more_store, begin, pl.multiple_of(begin + (MAIN - LATE), 256), EXTRA))
    fields[:, 0:ATOM], fields[:, ATOM:] = halves(env[...] * ENV_SCALE)
    second_pass(first_store, 0, MAIN)
    rest(lambda begin: second_pass(more_store, begin, EXTRA))
    energy_ref[...] = g_env[FIELD : FIELD + 1, :]
    fields[:, 0:ATOM], fields[:, ATOM:] = halves(g_env[0:FIELD, :] * ENV_SCALE)

    def third(begin):
        pull = third_pass(
            (more_hots, more_slope, more_mixed, more_low, more_d_value, more_raw, more_geo),
            begin, EXTRA, fields, around, dn_ref, wr_ref, ab_ref,
        )
        to_partners(pull, more_geo, begin, EXTRA, at_partner)
        at_centre[...] += settled(pull, more_hots[:, pl.ds(begin, EXTRA)])

    rest(third)


def return_kernel(
    dn_ref, wr_ref, ab_ref,
    fields, more_centre, more_partner, hots, slope, mixed, mixed_low, d_value, raw, geo,
    out_ref, outbox, inbox, around, at_partner, send_sem, recv_sem,
):
    barrier, peers = greet()
    at_partner[...] = more_partner[...]
    store = (hots, slope, mixed, mixed_low, d_value, raw, geo)
    weights = (fields, around, dn_ref, wr_ref, ab_ref)
    pull = third_pass(store, LATE, MAIN - LATE, *weights)
    to_partners(pull, geo, LATE, MAIN - LATE, at_partner)
    parts = at_partner[...]
    for k in range(NBR):
        for i in range(3):
            for half in range(2):
                outbox[k, 3 * half + i : 3 * half + i + 1, :] = parts[
                    16 * i + 3 + k : 16 * i + 4 + k, half * 128 : (half + 1) * 128
                ]
        outbox[k, 6:8, :] = jnp.zeros((2, 128), F32)
    pl.semaphore_wait(barrier, NBR)
    copies = swap(peers, outbox, inbox, send_sem, recv_sem)
    sums = more_centre[...] + settled(pull, hots[:, LATE:MAIN])
    pull = third_pass(store, 0, LATE, *weights)
    mates = one_hot(geo[CODE : CODE + 1, 0:LATE].astype(I32), ATOM)
    sums = sums + settled(pull, hots[:, 0:LATE]) - settled(pull, mates)
    total = sums[0:3] + sums[8:11]
    total = total - jnp.concatenate([parts[16 * i : 16 * i + 1] for i in range(3)], axis=0)
    for copy in copies:
        copy.wait()
    arrived = inbox[0]
    for k in range(1, NBR):
        arrived = arrived + inbox[k]
    out_ref[...] = total - jnp.concatenate([arrived[0:3], arrived[3:6]], axis=1)


def edge_call(*operands):
    shape = jax.ShapeDtypeStruct
    rest = NBR * PAIR

    def store(lanes, make):
        return [
            make((ATOM, lanes), BF16),
            make((WIDTH, lanes), F32),
            make((WIDTH, lanes), BF16),
            make((WIDTH, lanes), BF16),
            make((CH, lanes), F32),
            make((CH, lanes), F32),
            make((ROWS, lanes), F32),
        ]

    return pl.pallas_call(
        edge_kernel,
        out_shape=(
            shape((1, ATOM), F32),
            shape((FIELD, 2 * ATOM), BF16),
            shape((16, ATOM), F32),
            shape((48, ATOM), F32),
            *store(MAIN, shape),
        ),
        in_specs=[VMEM] * 19,
        out_specs=[VMEM] * 11,
        scratch_shapes=[
            pltpu.VMEM((8, CAP + 512), F32),
            pltpu.VMEM((WIDTH, MAIN), F32),
            *store(rest, pltpu.VMEM),
            pltpu.VMEM((WIDTH, rest), F32),
            pltpu.VMEM((FIELD, ATOM), F32),
            pltpu.VMEM((FIELD + 16, ATOM), F32),
            pltpu.VMEM((FIELD + 16, 2 * MAIN), BF16),
            pltpu.VMEM((FIELD, MAIN), F32),
            pltpu.VMEM((NBR + 1, PAIR // 128, 8, 128), F32),
            pltpu.VMEM((8, PAIR), F32),
        ],
        compiler_params=pltpu.CompilerParams(vmem_limit_bytes=43 << 20),
    )(*operands)


def per_device(
    positions, species, send_list, edge_src, edge_dst, edge_count,
    w_in, w_mid, w_pair, w_mix, w_back, w_read,
):
    sends = send_list[0]
    shape = jax.ShapeDtypeStruct
    shared = pl.pallas_call(
        share_kernel,
        out_shape=(
            shape((8, PAIR), F32),
            shape((16, ATOM), BF16),
            shape((NBR, 8, LIST), F32),
            shape((WIDTH, 64), BF16),
            shape((2 * WIDTH, 3 * WIDTH), BF16),
            shape((WIDTH, 6 * WIDTH), BF16),
            shape((WIDTH, 9 * CH), BF16),
            shape((3 * CH, 3 * WIDTH), BF16),
            shape((16, 3 * WIDTH), BF16),
            shape((WIDTH, 2), F32),
            shape((GHOST, NBR), F32),
            shape((8, LIST), F32),
            shape((ATOM, LATE), BF16),
            shape((WIDTH, LATE), F32),
            shape((CH, LATE), F32),
            shape((CH, LATE), F32),
            shape((ROWS, LATE), F32),
            shape((WIDTH, LATE), F32),
            shape((FIELD, ATOM), F32),
        ),
        in_specs=[SMEM] + [HBM] * 11,
        out_specs=[VMEM] * 19,
        scratch_shapes=[
            pltpu.VMEM((3, ATOM), F32),
            pltpu.VMEM((1, ATOM), I32),
            pltpu.VMEM((NBR, GHOST), I32),
            pltpu.VMEM((1, PAIR), I32),
            pltpu.VMEM((1, PAIR), I32),
            pltpu.VMEM((2 * SPECIES + BASIS, WIDTH), F32),
            pltpu.VMEM((WIDTH, WIDTH), F32),
            pltpu.VMEM((WIDTH, WIDTH), F32),
            pltpu.VMEM((WIDTH + 3 * CH, WIDTH), F32),
            pltpu.VMEM((WIDTH, WIDTH), F32),
            pltpu.VMEM((1, WIDTH), F32),
            pltpu.VMEM((NBR, 8, LIST), F32),
            pltpu.VMEM((8, 384), F32),
            pltpu.VMEM((FIELD, 2 * LATE), BF16),
            pltpu.SemaphoreType.DMA((11,)),
            pltpu.SemaphoreType.DMA((NBR,)),
            pltpu.SemaphoreType.DMA((NBR,)),
        ],
        compiler_params=pltpu.CompilerParams(
            collective_id=0, has_side_effects=True, vmem_limit_bytes=14 << 20
        ),
    )(
        edge_count,
        *(
            pltpu.with_memory_space_constraint(x, pltpu.HBM)
            for x in (
                positions, species.reshape(1, ATOM), sends, edge_src, edge_dst,
                w_in, w_mid, w_pair, w_mix, w_back, w_read.reshape(1, WIDTH),
            )
        ),
    )
    energy, *kept = edge_call(*shared)
    dn, wr, ab = shared[5], shared[8], shared[9]
    forces = pl.pallas_call(
        return_kernel,
        out_shape=shape((3, ATOM), F32),
        in_specs=[VMEM] * 13,
        out_specs=VMEM,
        scratch_shapes=[
            pltpu.VMEM((NBR, 8, 128), F32),
            pltpu.VMEM((NBR, 8, 128), F32),
            pltpu.VMEM((FIELD, MAIN - LATE), F32),
            pltpu.VMEM((48, ATOM), F32),
            pltpu.SemaphoreType.DMA((NBR,)),
            pltpu.SemaphoreType.DMA((NBR,)),
        ],
        compiler_params=pltpu.CompilerParams(
            collective_id=1, has_side_effects=True, vmem_limit_bytes=20 << 20
        ),
    )(dn, wr, ab, *kept)
    return forces, energy.reshape(ATOM)


def solution(mesh):
    both = ("dom", "face")
    placed = (
        P(None, both), P(both), P(both, None, None), P(both, None), P(both, None), P(both),
        P(), P(), P(), P(), P(), P(),
    )
    return jax.shard_map(
        per_device,
        mesh=mesh,
        in_specs=placed,
        out_specs=(P(None, both), P(both)),
        check_vma=False,
    )
```

```python
import functools

import jax
import jax.numpy as jnp
from jax import lax
from jax.experimental import pallas as pl
from jax.experimental.pallas import tpu as pltpu
from jax.sharding import PartitionSpec as P

CH = 64
WIDTH = 128
BASIS = 8
SPECIES = 7
ENV_SCALE = 0.2
CUTOFF = 6.0
PI = 3.141592653589793
DIRECTIONS = ((-1, -1), (-1, 0), (-1, 1), (0, -1), (0, 1), (1, -1), (1, 0), (1, 1))
NBR = 8
ORDER = tuple(range(NBR))
ATOM = 256
GHOST = 64
PAIR = 1024
SLOTS = NBR * GHOST
LIST = 512
CAP = 10 * PAIR
MAIN = 2048
LATE = 768
EXTRA = 512
F32 = jnp.float32
BF16 = jnp.bfloat16
I32 = jnp.int32
MESH = pl.DeviceIdType.MESH
VMEM = pl.BlockSpec(memory_space=pltpu.VMEM)
SMEM = pl.BlockSpec(memory_space=pltpu.SMEM)
HBM = pl.BlockSpec(memory_space=pltpu.HBM)

RAD, DRAD, ANG, ENVL, DENVL, RINV, DIR, ERAW, DANG, CODE, ROWS = 0, 8, 16, 25, 26, 27, 28, 31, 32, 40, 48
FIELD = 9 * CH
ROOT3, ROOT5, ROOT15 = 3.0**0.5, 5.0**0.5, 15.0**0.5
DEGREES = (0, 1, 1, 1, 2, 2, 2, 2, 2)


def dot(a, b):
    return lax.dot_general(a, b, (((1,), (0,)), ((), ())), preferred_element_type=F32)


def dot_nt(a, b):
    return lax.dot_general(a, b, (((1,), (1,)), ((), ())), preferred_element_type=F32)


def exact(a, b):
    return jnp.dot(a, b, precision=lax.Precision.HIGHEST, preferred_element_type=F32)


def halves(x):
    high = x.astype(BF16)
    return high, (x - high.astype(F32)).astype(BF16)


def thirds(x):
    high = x.astype(BF16).astype(F32)
    rest = x - high
    mid = rest.astype(BF16).astype(F32)
    return high, mid, rest - mid


def sigmoid(x):
    return 0.5 * jnp.tanh(0.5 * x) + 0.5


def triple(weight):
    high, low = halves(weight)
    return jnp.concatenate([high, high, low], axis=1)


def stacked(x):
    high, low = halves(x)
    return jnp.concatenate([high, low, high], axis=0)


def one_hot(row, count):
    rows = lax.broadcasted_iota(I32, (count, row.shape[1]), 0).astype(F32).astype(BF16)
    match = rows == row.astype(F32).astype(BF16)
    return jnp.where(match, jnp.ones_like(rows), jnp.zeros_like(rows))


def atom_table(coords, kinds):
    parts = thirds(coords)
    pad = jnp.zeros((6, coords.shape[1]), F32)
    return jnp.concatenate([*parts, kinds, pad], axis=0)


def joined(rows):
    return rows[0:3] + rows[3:6] + rows[6:9]


def greet():
    here = [lax.axis_index("dom"), lax.axis_index("face")]
    sizes = [lax.axis_size("dom"), lax.axis_size("face")]
    peers = []
    for shift in DIRECTIONS:
        peers.append(
            tuple(lax.rem(at + by + size, size) for at, by, size in zip(here, shift, sizes))
        )
    barrier = pltpu.get_barrier_semaphore()
    for k in ORDER:
        pl.semaphore_signal(barrier, inc=1, device_id=peers[k], device_id_type=MESH)
    return barrier, peers


def swap(peers, out_ref, in_ref, send_sem, recv_sem):
    copies = []
    for k, peer in enumerate(peers):
        copies.append(
            pltpu.make_async_remote_copy(
                src_ref=out_ref.at[k],
                dst_ref=in_ref.at[NBR - 1 - k],
                send_sem=send_sem.at[k],
                recv_sem=recv_sem.at[NBR - 1 - k],
                device_id=peer,
                device_id_type=MESH,
            )
        )
    for k in ORDER:
        copies[k].start()
    return copies


def share_kernel(
    count_ref, *refs,
):
    sources, refs = refs[:11], refs[11:]
    (
        own_ref, table_ref, recv_ref, wx_ref, up_ref, dn_ref, mt_ref, mb_ref, wr_ref, ab_ref, cols_ref,
        home_ref, hots_ref, slope_ref, value_ref, raw_ref, geo_ref, base_ref, env_ref,
    ) = refs[:19]
    held, refs = refs[19:30], refs[30:]
    out_buf, order_buf, terms, load_sem, send_sem, recv_sem = refs
    (
        pos_ref, spec_ref, send_ref, src_ref, dst_ref,
        w_in_ref, w_mid_ref, w_pair_ref, w_mix_ref, w_back_ref, w_read_ref,
    ) = held
    loads = [
        pltpu.make_async_copy(source, target, load_sem.at[i])
        for i, (source, target) in enumerate(zip(sources, held))
    ]
    for load in loads[:5]:
        load.start()
    barrier, peers = greet()
    for load in loads[5:]:
        load.start()
    for load in loads[:5]:
        load.wait()
    table = atom_table(pos_ref[...], spec_ref[...].astype(F32)).astype(BF16)
    table_ref[...] = table
    sends = jnp.concatenate([send_ref[k : k + 1, :] for k in range(NBR)], axis=1)
    ghosts = dot(table, one_hot(sends, ATOM))
    ghost_rows = jnp.concatenate([joined(ghosts), ghosts[9:10]], axis=0)
    src = src_ref[...]
    dst = dst_ref[...]
    lanes = lax.broadcasted_iota(I32, (1, PAIR), 1)
    live = lanes < count_ref[0]
    ghost = dst >= ATOM
    away = dst - ATOM
    bucket = jnp.where(ghost, (away >> 6) + 1, 0)
    bucket = jnp.where(live, bucket, 15)
    place = jnp.where(ghost, away & 63, dst)
    member = jnp.where(lax.broadcasted_iota(I32, (16, PAIR), 0) == bucket, 1.0, 0.0)
    before = lax.broadcasted_iota(I32, (ATOM, ATOM), 0) < lax.broadcasted_iota(I32, (ATOM, ATOM), 1)
    before = jnp.where(before, 1.0, 0.0).astype(BF16)
    pieces = [member[:, i * ATOM : (i + 1) * ATOM] for i in range(PAIR // ATOM)]
    ranks = dot(jnp.concatenate(pieces, axis=0).astype(BF16), before)
    sums = [jnp.sum(piece, axis=1, keepdims=True) for piece in pieces]
    total = sums[0] + sums[1] + sums[2] + sums[3]
    start = jnp.zeros((16, 1), F32)
    index = lax.broadcasted_iota(I32, (16, 1), 0)
    for b in range(NBR + 1):
        start = start + jnp.where(index > b, total[b : b + 1, :], 0.0)
    offset = start
    spots = []
    for i, piece in enumerate(pieces):
        where = ranks[16 * i : 16 * (i + 1)] + offset
        spots.append(jnp.sum(piece * where, axis=0, keepdims=True))
        offset = offset + sums[i]
    spot = jnp.concatenate(spots, axis=1)
    spot = jnp.where(live, spot, -1.0).astype(I32)
    data = jnp.concatenate(
        [
            place.astype(F32), src.astype(F32), (dst >> 8).astype(F32), (dst & 255).astype(F32),
            jnp.zeros((12, PAIR), F32),
        ],
        axis=0,
    ).astype(BF16)
    for i in range(PAIR // ATOM):
        ordered = dot_nt(data, one_hot(spot - i * ATOM, ATOM))
        span = slice(i * ATOM, (i + 1) * ATOM)
        own_ref[0:1, span] = ordered[1:2]
        own_ref[1:2, span] = ordered[2:3] * ATOM + ordered[3:4]
        for j in range(2):
            for half in range(2):
                order_buf[2 * i + half : 2 * i + half + 1, j * 128 : (j + 1) * 128] = ordered[
                    j : j + 1, half * 128 : (half + 1) * 128
                ]
    atoms = jnp.concatenate([pos_ref[...], spec_ref[...].astype(F32)], axis=0)
    for i in range(4):
        for half in range(2):
            order_buf[2 * i + half : 2 * i + half + 1, 256:384] = atoms[
                i : i + 1, half * 128 : (half + 1) * 128
            ]
    entries = order_buf[...]
    none = jnp.zeros((8, GHOST), F32)
    indices = sends.astype(F32)
    for k in range(NBR):
        out_buf[k, :, 0:384] = entries
        part = slice(k * GHOST, (k + 1) * GHOST)
        mine = jnp.concatenate([ghost_rows[:, part], none[0:2], indices[:, part], none[0:1]], axis=0)
        out_buf[k, :, 384:LIST] = jnp.concatenate([mine, none], axis=1)
        out_buf[k, 4:5, 384:LIST] = jnp.broadcast_to(total[k + 1 : k + 2, :], (1, 128))
        out_buf[k, 5:6, 384:LIST] = jnp.broadcast_to(start[k + 1 : k + 2, :], (1, 128))
    pl.semaphore_wait(barrier, NBR)
    copies = swap(peers, out_buf, recv_ref, send_sem, recv_sem)
    home_ref[:, 0:384] = entries
    home_ref[:, 384:LIST] = jnp.zeros((8, 128), F32)
    home_ref[4:5, 384:LIST] = jnp.broadcast_to(total[0:1, :], (1, 128))
    own_ref[2:3, :] = jnp.full((1, PAIR), count_ref[0], I32).astype(F32)
    cols_ref[...] = send_ref[...].astype(F32).T
    for load in loads[5:]:
        load.wait()
    w_in = w_in_ref[...]
    w_c = w_in[0:SPECIES].T
    w_p = w_in[SPECIES : 2 * SPECIES].T
    w_r = w_in[2 * SPECIES :]
    gap = jnp.zeros((WIDTH, 1), F32)
    first = jnp.concatenate([w_c, gap, w_p, gap, w_r.T], axis=1)
    first_high = first.astype(BF16).astype(F32)
    first_low = first - first_high
    wx_ref[...] = jnp.concatenate(
        [first_high, first_high[:, 16:24], first_low, jnp.zeros((WIDTH, 8), F32)], axis=1
    ).astype(BF16)
    wr_high, wr_low = halves(jnp.concatenate([w_r, jnp.zeros((8, WIDTH), F32)], axis=0))
    wr_ref[...] = jnp.concatenate([wr_high, wr_high, wr_low], axis=1)
    w_mid = w_mid_ref[...]
    w_read = w_read_ref[...]
    down = jnp.concatenate(
        [exact(w_mid, w_pair_ref[...]), exact(w_mid, w_mix_ref[0:WIDTH, :])], axis=1
    )
    a_col = jnp.sum(w_mid * w_read, axis=1, keepdims=True)
    b_col = jnp.sum(w_back_ref[...] * w_read, axis=1, keepdims=True)
    ab_ref[...] = jnp.concatenate([a_col, b_col], axis=1)
    dn_ref[...] = triple(down)
    up_ref[...] = triple(down.T)
    mix = jnp.concatenate(
        [w_mix_ref[pl.ds(WIDTH + degree, CH, stride=3), :] for degree in range(3)], axis=0
    )
    mb_ref[...] = triple(mix)
    mt_ref[...] = triple(mix.T)
    half = LATE // 2
    ends = [own_ref[i : i + 1, 0:half] for i in range(2)]
    centre = jnp.concatenate(ends, axis=1)
    mate = jnp.concatenate(ends[::-1], axis=1)
    found = dot(table, one_hot(mate.astype(I32), ATOM))
    partner = jnp.concatenate([joined(found), found[9:10]], axis=0)
    index = lax.broadcasted_iota(I32, (1, half), 1).astype(F32)
    valid = jnp.concatenate([index, index], axis=1) < total[0:1, :]
    env_ref[...] = jnp.zeros_like(env_ref)
    store = (hots_ref, slope_ref, None, None, value_ref, raw_ref, geo_ref, base_ref)
    first_pass(
        centre.astype(I32), partner, mate, valid, table, store, 0, terms, env_ref, wx_ref, up_ref, ab_ref
    )
    for copy in copies:
        copy.wait()


def gather(fields, hot, around):
    width = hot.shape[1]
    around[:, 0:width] = dot(fields[...], jnp.concatenate([hot, hot], axis=0))


def scatter(terms, hot, total, count):
    width = hot.shape[1]
    high = dot_nt(terms[0:count, 0:width], hot)
    total[0:count, :] += high + dot_nt(terms[0:count, width : 2 * width], hot)


def first_pass(centre, partner, code, valid, table, store, begin, terms, env, wx_ref, up_ref, ab_ref):
    hots, slope, _, _, value, raw, geo, base = store
    width = centre.shape[1]
    here = pl.ds(begin, width)
    hot = one_hot(centre, ATOM)
    hots[:, here] = hot
    geo[CODE : CODE + 1, here] = code
    held = dot(table, hot)
    delta = partner[0:3] - joined(held)
    length2 = delta[0:1] * delta[0:1] + delta[1:2] * delta[1:2] + delta[2:3] * delta[2:3] + 1.0
    soft = jnp.sqrt(length2)
    rinv = 1.0 / soft
    unit = delta * rinv
    ux, uy, uz = unit[0:1], unit[1:2], unit[2:3]
    turn = soft * (PI / CUTOFF) - PI / 2
    t2 = turn * turn
    cosine = -turn * (
        1 + t2 * (-1 / 6 + t2 * (1 / 120 + t2 * (-1 / 5040 + t2 * (1 / 362880 - t2 / 39916800))))
    )
    sine = 1 + t2 * (
        -1 / 2 + t2 * (1 / 24 + t2 * (-1 / 720 + t2 * (1 / 40320 + t2 * (-1 / 3628800 + t2 / 479001600))))
    )
    twice = 2 * cosine
    s_old, s_now = jnp.zeros_like(sine), sine
    c_old, c_now = jnp.ones_like(sine), cosine
    for b in range(BASIS):
        geo[RAD + b : RAD + b + 1, here] = s_now * rinv
        geo[DRAD + b : DRAD + b + 1, here] = (c_now * ((b + 1) * PI / CUTOFF) - s_now * rinv) * rinv
        s_old, s_now = s_now, twice * s_now - s_old
        c_old, c_now = c_now, twice * c_now - c_old
    angular = [
        jnp.ones_like(ux),
        ROOT3 * ux,
        ROOT3 * uy,
        ROOT3 * uz,
        ROOT15 * ux * uy,
        ROOT15 * uy * uz,
        0.5 * ROOT5 * (2.0 * uz * uz - ux * ux - uy * uy),
        ROOT15 * ux * uz,
        0.5 * ROOT15 * (ux * ux - uy * uy),
    ]
    for m in range(9):
        geo[ANG + m : ANG + m + 1, here] = angular[m]
    inner = 1.0 - length2 * (1.0 / (CUTOFF * CUTOFF))
    alive = jnp.where(valid, 1.0, 0.0)
    envelope = alive * inner * inner
    geo[ENVL : ENVL + 1, here] = envelope
    geo[DENVL : DENVL + 1, here] = alive * inner * soft * (-4.0 / (CUTOFF * CUTOFF))
    geo[RINV : RINV + 1, here] = rinv
    geo[DIR : DIR + 3, here] = unit
    radial = geo[RAD : RAD + 8, here]
    radial_low = radial - radial.astype(BF16).astype(F32)
    kinds = lax.broadcasted_iota(I32, (8, width), 0)
    hot_c = jnp.where(kinds == held[9:10].astype(I32), 1.0, 0.0)
    hot_p = jnp.where(kinds == partner[3:4].astype(I32), 1.0, 0.0)
    inputs = jnp.concatenate(
        [hot_c, hot_p, radial, radial_low, hot_c, hot_p, radial, jnp.zeros((8, width), F32)], axis=0
    ).astype(BF16)
    pre = dot(wx_ref[...], inputs)
    gate = sigmoid(pre)
    act = pre * gate
    slope[:, here] = gate + act * (1.0 - gate)
    after = dot(up_ref[...], stacked(act))
    raw[:, here] = after[0:CH]
    value[:, here] = after[CH : 2 * CH]
    base[:, here] = after[2 * CH :]
    geo[ERAW : ERAW + 1, here] = jnp.sum(act * ab_ref[:, 0:1], axis=0, keepdims=True)
    weights = after[0:CH] * envelope
    for m in range(9):
        term = weights if m == 0 else weights * angular[m]
        rows = slice(m * CH, (m + 1) * CH)
        terms[rows, 0:width], terms[rows, width : 2 * width] = halves(term)
    scatter(terms, hot, env, FIELD)


def third_pass(store, begin, width, fields, around, dn_ref, wr_ref, ab_ref):
    hots, slope, mixed, mixed_low, d_value, raw_ref, geo = store
    here = pl.ds(begin, width)
    gather(fields, hots[:, here], around)
    envelope = geo[ENVL : ENVL + 1, here]
    raw = raw_ref[:, here]
    weights = raw * envelope
    d_weight = None
    d_ang = [None]
    for m in range(9):
        got = around[m * CH : (m + 1) * CH, 0:width]
        term = got if m == 0 else got * geo[ANG + m : ANG + m + 1, here]
        d_weight = term if m == 0 else d_weight + term
        if m:
            d_ang.append(
                geo[DANG + m - 1 : DANG + m, here] + jnp.sum(weights * got, axis=0, keepdims=True)
            )
    d_envelope = geo[ERAW : ERAW + 1, here] + jnp.sum(d_weight * raw, axis=0, keepdims=True)
    pair_high, pair_low = halves(jnp.concatenate([d_weight * envelope, d_value[:, here]], axis=0))
    both_high = jnp.concatenate([pair_high, mixed[:, here]], axis=0)
    both_low = jnp.concatenate([pair_low, mixed_low[:, here]], axis=0)
    d_act = dot(dn_ref[...], jnp.concatenate([both_high, both_low, both_high], axis=0))
    d_act = d_act + ab_ref[:, 0:1] * envelope
    d_radial = dot(wr_ref[...], stacked(d_act * slope[:, here]))
    d_soft = jnp.sum(d_radial[0:8] * geo[DRAD : DRAD + 8, here], axis=0, keepdims=True)
    d_soft = d_soft + d_envelope * geo[DENVL : DENVL + 1, here]
    unit = geo[DIR : DIR + 3, here]
    rinv = geo[RINV : RINV + 1, here]
    ux, uy, uz = unit[0:1], unit[1:2], unit[2:3]
    d_ux = ROOT3 * d_ang[1] + ROOT15 * (uy * d_ang[4] + uz * d_ang[7] + ux * d_ang[8]) - ROOT5 * ux * d_ang[6]
    d_uy = ROOT3 * d_ang[2] + ROOT15 * (ux * d_ang[4] + uz * d_ang[5] - uy * d_ang[8]) - ROOT5 * uy * d_ang[6]
    d_uz = ROOT3 * d_ang[3] + ROOT15 * (uy * d_ang[5] + ux * d_ang[7]) + 2.0 * ROOT5 * uz * d_ang[6]
    along = d_soft - (d_ux * ux + d_uy * uy + d_uz * uz) * rinv
    return [d * rinv + u * along for d, u in ((d_ux, ux), (d_uy, uy), (d_uz, uz))]


def to_partners(pull, geo, begin, width, at_partner):
    code = geo[CODE : CODE + 1, pl.ds(begin, width)].astype(I32)
    seg = lax.broadcasted_iota(I32, (16, width), 0) == (code >> 8)
    high, low = halves(jnp.concatenate([jnp.where(seg, g, 0.0) for g in pull], axis=0))
    hot = one_hot(code & 255, ATOM)
    sums = dot_nt(jnp.concatenate([high, low], axis=0), hot)
    at_partner[...] += sums[0:48] + sums[48:96]


def settled(pull, hot):
    sent = jnp.concatenate([*pull, jnp.zeros((5, hot.shape[1]), F32)], axis=0)
    sent = jnp.concatenate([sent, sent - sent.astype(BF16).astype(F32)], axis=0).astype(BF16)
    return dot_nt(sent, hot)


def edge_kernel(
    own_ref, table_ref, recv_ref,
    wx_ref, up_ref, dn_ref, mt_ref, mb_ref, wr_ref, ab_ref, cols_ref, home_ref,
    late_hots, late_slope, late_value, late_raw, late_geo, late_base, late_env,
    energy_ref, fields, at_centre, at_partner, hots, slope, mixed, mixed_low, d_value, raw, geo,
    edges, base, more_hots, more_slope, more_mixed, more_low, more_d_value, more_raw, more_geo,
    more_base, env, g_env, terms, around, lines, forward,
):
    first_store = (hots, slope, mixed, mixed_low, d_value, raw, geo, base)
    more_store = (
        more_hots, more_slope, more_mixed, more_low, more_d_value, more_raw, more_geo,
        more_base,
    )
    count = own_ref[2:3, 0:128][0, 0].astype(I32)
    src = own_ref[0:1, :]
    dst = own_ref[1:2, :].astype(I32)
    near = jnp.concatenate([recv_ref[k, :, 384 : 384 + GHOST] for k in range(NBR)], axis=1)
    ghosts = jnp.concatenate(
        [*thirds(near[0:3]), near[3:4], near[6:7], jnp.zeros((5, SLOTS), F32)], axis=0
    ).astype(BF16)
    table = table_ref[...]
    segments = jnp.concatenate([table, ghosts[:, 0:ATOM], ghosts[:, ATOM:SLOTS]], axis=0)
    found = dot(segments, one_hot(dst & 255, ATOM))
    part = dst >> 8
    picked = jnp.where(part == 0, found[0:16], jnp.where(part == 1, found[16:32], found[32:48]))
    beyond = (((dst - ATOM) >> 6) + 3).astype(F32) * ATOM + picked[10:11]
    code = jnp.where(part == 0, dst.astype(F32), beyond)
    forward[...] = jnp.concatenate(
        [joined(picked), picked[9:10], src, code, jnp.zeros((2, PAIR), F32)], axis=0
    )
    lane = lax.broadcasted_iota(I32, (8, 128), 1)
    row = lax.broadcasted_iota(I32, (8, 128), 0)

    def kept(ref):
        halves_of = [
            jnp.concatenate([ref[2 * i : 2 * i + 1, 256:384], ref[2 * i + 1 : 2 * i + 2, 256:384]], axis=1)
            for i in range(4)
        ]
        return atom_table(jnp.concatenate(halves_of[0:3], axis=0), halves_of[3]).astype(BF16)

    def place(size, begin, at, k, held, tile, whole=False):
        base = tile * 128 - at + begin
        first = base >> 7
        turn = base & 127
        low = jnp.clip(first, 0, 7)
        high = jnp.clip(first + 1, 0, 7)
        if k is None:
            left, right = [forward[:, pl.ds(pl.multiple_of(i * 128, 128), 128)] for i in (low, high)]
        else:
            left, right = lines[k, low], lines[k, high]
        back = lax.rem(128 - turn, 128)
        taken = jnp.where(
            lane < 128 - turn, pltpu.roll(left, back, 1), pltpu.roll(right, back, 1)
        )
        if k is not None:
            found = dot(held, one_hot(taken[5:6].astype(I32), ATOM))
            partner = jnp.concatenate([joined(found), found[9:10], jnp.zeros((4, 128), F32)], axis=0)
        if k is not None and k < NBR:
            match = lax.broadcasted_iota(I32, (GHOST, 128), 0) == taken[4:5].astype(I32)
            atom = jnp.sum(jnp.where(match, cols_ref[:, k : k + 1], 0.0), axis=0, keepdims=True)
            taken = jnp.where(row == 4, atom, taken + F32(ATOM * (3 + k)))
        if k is not None:
            taken = jnp.where(row < 4, partner, taken)
        here = pl.ds(pl.multiple_of(tile * 128, 128), 128)
        if whole:
            edges[:, here] = taken
            return
        spot = tile * 128 + lane
        inside = (spot >= at) & (spot < at + size)
        edges[:, here] = jnp.where(inside, taken, edges[:, here])

    def scalar(ref, which):
        return ref[which : which + 1, 384:LIST][0, 0].astype(I32)

    for k, ref in enumerate([recv_ref.at[k] for k in range(NBR)] + [home_ref]):
        for i in range(PAIR // 128):
            lines[k, i] = jnp.where(row == 4, ref[i : i + 1, 0:128], ref[i : i + 1, 128:256])
    inner = scalar(home_ref, 4)
    early = jnp.minimum(inner, LATE // 2)
    jobs = [(count - early, early, jnp.int32(0), None, None, PAIR // 128)]
    at = count - early
    size = inner - early
    jobs.append((size, LATE // 2, at, NBR, kept(home_ref), 0))
    at = at + size
    for k in range(NBR):
        ref = recv_ref.at[k]
        size = scalar(ref, 4)
        jobs.append((size, scalar(ref, 5), at, k, kept(ref), 2))
        at = at + size
    total = at
    for size, begin, at, k, held, usual in jobs:
        for step in range(usual):
            place(size, begin, at, k, held, (at >> 7) + step, k is None or step > 0)
    left_over = jnp.int32(0)
    for size, begin, at, k, held, usual in jobs:
        left_over = left_over + jnp.maximum(((at + size + 127) >> 7) - (at >> 7) - usual, 0)

    @pl.when(left_over > 0)
    def _():
        for size, begin, at, k, held, usual in jobs:

            def more(tile, carry, size=size, begin=begin, at=at, k=k, held=held):
                place(size, begin, at, k, held, tile)
                return carry

            lax.fori_loop((at >> 7) + usual, (at + size + 127) >> 7, more, 0)

    extra_blocks = lax.div(jnp.maximum(total - (MAIN - LATE), 0) + EXTRA - 1, EXTRA)

    env[...] = late_env[...]
    g_env[...] = jnp.zeros_like(g_env)
    terms[FIELD:, :] = jnp.zeros((16, 2 * MAIN), BF16)
    at_centre[...] = jnp.zeros_like(at_centre)
    at_partner[...] = jnp.zeros_like(at_partner)

    def second_pass(store, begin, width):
        hots, _, mixed, mixed_low, value, _, geo, base = store
        here = pl.ds(begin, width)
        hot = hots[:, here]
        gather(fields, hot, around)
        envelope = geo[ENVL : ENVL + 1, here]
        sums = [None, None, None]
        for m in range(9):
            got = around[m * CH : (m + 1) * CH, 0:width]
            term = got if m == 0 else got * geo[ANG + m : ANG + m + 1, here]
            degree = DEGREES[m]
            sums[degree] = term if sums[degree] is None else sums[degree] + term
        held = value[:, here]
        invariant = jnp.concatenate([s * held for s in sums], axis=0)
        pre = base[:, here] + dot(mt_ref[...], stacked(invariant))
        gate = sigmoid(pre)
        act = pre * gate
        back = ab_ref[:, 1:2]
        e_raw = geo[ERAW : ERAW + 1, here] + jnp.sum(act * back, axis=0, keepdims=True)
        geo[ERAW : ERAW + 1, here] = e_raw
        energy = e_raw * envelope
        energy = jnp.concatenate([energy, jnp.zeros((15, width), F32)], axis=0)
        terms[FIELD:, 0:width], terms[FIELD:, width : 2 * width] = halves(energy)
        d_pre = (gate + act * (1.0 - gate)) * back * envelope
        d_high, d_low = halves(d_pre)
        mixed[:, here] = d_high
        mixed_low[:, here] = d_low
        d_inv = dot(mb_ref[...], jnp.concatenate([d_high, d_low, d_high], axis=0))
        d_inv = [d_inv[i * CH : (i + 1) * CH] for i in range(3)]
        value[:, here] = d_inv[0] * sums[0] + d_inv[1] * sums[1] + d_inv[2] * sums[2]
        d_sum = [d * held for d in d_inv]
        for m in range(9):
            share = d_sum[DEGREES[m]]
            term = share if m == 0 else share * geo[ANG + m : ANG + m + 1, here]
            rows = slice(m * CH, (m + 1) * CH)
            terms[rows, 0:width], terms[rows, width : 2 * width] = halves(term)
            if m:
                geo[DANG + m - 1 : DANG + m, here] = jnp.sum(
                    share * around[rows, 0:width], axis=0, keepdims=True
                )
        scatter(terms, hot, g_env, FIELD + 16)

    def rest(step):
        def body(block, carry):
            step(pl.multiple_of(block * EXTRA, EXTRA))
            return carry

        lax.fori_loop(0, extra_blocks, body, 0)

    def listed(store, begin, start, width):
        valid = start + lax.broadcasted_iota(I32, (1, width), 1) < total
        part = jnp.where(valid, edges[:, pl.ds(start, width)], 0.0)
        first_pass(
            part[4:5].astype(I32), part[0:4], part[5:6], valid, table, store, begin, terms, env,
            wx_ref, up_ref, ab_ref,
        )

    listed(first_store, LATE, 0, MAIN - LATE)
    for target, source in zip(
        (hots, slope, d_value, raw, geo, base),
        (late_hots, late_slope, late_value, late_raw, late_geo, late_base),
    ):
        target[:, 0:LATE] = source[...]
    rest(lambda begin: listed(more_store, begin, pl.multiple_of(begin + (MAIN - LATE), 256), EXTRA))
    fields[:, 0:ATOM], fields[:, ATOM:] = halves(env[...] * ENV_SCALE)
    second_pass(first_store, 0, MAIN)
    rest(lambda begin: second_pass(more_store, begin, EXTRA))
    energy_ref[...] = g_env[FIELD : FIELD + 1, :]
    fields[:, 0:ATOM], fields[:, ATOM:] = halves(g_env[0:FIELD, :] * ENV_SCALE)

    def third(begin):
        pull = third_pass(
            (more_hots, more_slope, more_mixed, more_low, more_d_value, more_raw, more_geo),
            begin, EXTRA, fields, around, dn_ref, wr_ref, ab_ref,
        )
        to_partners(pull, more_geo, begin, EXTRA, at_partner)
        at_centre[...] += settled(pull, more_hots[:, pl.ds(begin, EXTRA)])

    rest(third)


def return_kernel(
    dn_ref, wr_ref, ab_ref,
    fields, more_centre, more_partner, hots, slope, mixed, mixed_low, d_value, raw, geo,
    out_ref, outbox, inbox, around, at_partner, send_sem, recv_sem,
):
    barrier, peers = greet()
    at_partner[...] = more_partner[...]
    store = (hots, slope, mixed, mixed_low, d_value, raw, geo)
    weights = (fields, around, dn_ref, wr_ref, ab_ref)
    pull = third_pass(store, LATE, MAIN - LATE, *weights)
    to_partners(pull, geo, LATE, MAIN - LATE, at_partner)
    parts = at_partner[...]
    for k in range(NBR):
        for i in range(3):
            for half in range(2):
                outbox[k, 3 * half + i : 3 * half + i + 1, :] = parts[
                    16 * i + 3 + k : 16 * i + 4 + k, half * 128 : (half + 1) * 128
                ]
        outbox[k, 6:8, :] = jnp.zeros((2, 128), F32)
    pl.semaphore_wait(barrier, NBR)
    copies = swap(peers, outbox, inbox, send_sem, recv_sem)
    sums = more_centre[...] + settled(pull, hots[:, LATE:MAIN])
    pull = third_pass(store, 0, LATE, *weights)
    mates = one_hot(geo[CODE : CODE + 1, 0:LATE].astype(I32), ATOM)
    sums = sums + settled(pull, hots[:, 0:LATE]) - settled(pull, mates)
    total = sums[0:3] + sums[8:11]
    total = total - jnp.concatenate([parts[16 * i : 16 * i + 1] for i in range(3)], axis=0)
    for copy in copies:
        copy.wait()
    arrived = inbox[0]
    for k in range(1, NBR):
        arrived = arrived + inbox[k]
    out_ref[...] = total - jnp.concatenate([arrived[0:3], arrived[3:6]], axis=1)


def edge_call(*operands):
    shape = jax.ShapeDtypeStruct
    rest = NBR * PAIR

    def store(lanes, make):
        return [
            make((ATOM, lanes), BF16),
            make((WIDTH, lanes), F32),
            make((WIDTH, lanes), BF16),
            make((WIDTH, lanes), BF16),
            make((CH, lanes), F32),
            make((CH, lanes), F32),
            make((ROWS, lanes), F32),
        ]

    return pl.pallas_call(
        edge_kernel,
        out_shape=(
            shape((1, ATOM), F32),
            shape((FIELD, 2 * ATOM), BF16),
            shape((16, ATOM), F32),
            shape((48, ATOM), F32),
            *store(MAIN, shape),
        ),
        in_specs=[VMEM] * 19,
        out_specs=[VMEM] * 11,
        scratch_shapes=[
            pltpu.VMEM((8, CAP + 512), F32),
            pltpu.VMEM((WIDTH, MAIN), F32),
            *store(rest, pltpu.VMEM),
            pltpu.VMEM((WIDTH, rest), F32),
            pltpu.VMEM((FIELD, ATOM), F32),
            pltpu.VMEM((FIELD + 16, ATOM), F32),
            pltpu.VMEM((FIELD + 16, 2 * MAIN), BF16),
            pltpu.VMEM((FIELD, MAIN), F32),
            pltpu.VMEM((NBR + 1, PAIR // 128, 8, 128), F32),
            pltpu.VMEM((8, PAIR), F32),
        ],
        compiler_params=pltpu.CompilerParams(vmem_limit_bytes=43 << 20),
    )(*operands)


def per_device(
    positions, species, send_list, edge_src, edge_dst, edge_count,
    w_in, w_mid, w_pair, w_mix, w_back, w_read,
):
    sends = send_list[0]
    shape = jax.ShapeDtypeStruct
    shared = pl.pallas_call(
        share_kernel,
        out_shape=(
            shape((8, PAIR), F32),
            shape((16, ATOM), BF16),
            shape((NBR, 8, LIST), F32),
            shape((WIDTH, 64), BF16),
            shape((2 * WIDTH, 3 * WIDTH), BF16),
            shape((WIDTH, 6 * WIDTH), BF16),
            shape((WIDTH, 9 * CH), BF16),
            shape((3 * CH, 3 * WIDTH), BF16),
            shape((16, 3 * WIDTH), BF16),
            shape((WIDTH, 2), F32),
            shape((GHOST, NBR), F32),
            shape((8, LIST), F32),
            shape((ATOM, LATE), BF16),
            shape((WIDTH, LATE), F32),
            shape((CH, LATE), F32),
            shape((CH, LATE), F32),
            shape((ROWS, LATE), F32),
            shape((WIDTH, LATE), F32),
            shape((FIELD, ATOM), F32),
        ),
        in_specs=[SMEM] + [HBM] * 11,
        out_specs=[VMEM] * 19,
        scratch_shapes=[
            pltpu.VMEM((3, ATOM), F32),
            pltpu.VMEM((1, ATOM), I32),
            pltpu.VMEM((NBR, GHOST), I32),
            pltpu.VMEM((1, PAIR), I32),
            pltpu.VMEM((1, PAIR), I32),
            pltpu.VMEM((2 * SPECIES + BASIS, WIDTH), F32),
            pltpu.VMEM((WIDTH, WIDTH), F32),
            pltpu.VMEM((WIDTH, WIDTH), F32),
            pltpu.VMEM((WIDTH + 3 * CH, WIDTH), F32),
            pltpu.VMEM((WIDTH, WIDTH), F32),
            pltpu.VMEM((1, WIDTH), F32),
            pltpu.VMEM((NBR, 8, LIST), F32),
            pltpu.VMEM((8, 384), F32),
            pltpu.VMEM((FIELD, 2 * LATE), BF16),
            pltpu.SemaphoreType.DMA((11,)),
            pltpu.SemaphoreType.DMA((NBR,)),
            pltpu.SemaphoreType.DMA((NBR,)),
        ],
        compiler_params=pltpu.CompilerParams(
            collective_id=0, has_side_effects=True, vmem_limit_bytes=14 << 20
        ),
    )(
        edge_count,
        *(
            pltpu.with_memory_space_constraint(x, pltpu.HBM)
            for x in (
                positions, species.reshape(1, ATOM), sends, edge_src, edge_dst,
                w_in, w_mid, w_pair, w_mix, w_back, w_read.reshape(1, WIDTH),
            )
        ),
    )
    energy, *kept = edge_call(*shared)
    dn, wr, ab = shared[5], shared[8], shared[9]
    forces = pl.pallas_call(
        return_kernel,
        out_shape=shape((3, ATOM), F32),
        in_specs=[VMEM] * 13,
        out_specs=VMEM,
        scratch_shapes=[
            pltpu.VMEM((NBR, 8, 128), F32),
            pltpu.VMEM((NBR, 8, 128), F32),
            pltpu.VMEM((FIELD, MAIN - LATE), F32),
            pltpu.VMEM((48, ATOM), F32),
            pltpu.SemaphoreType.DMA((NBR,)),
            pltpu.SemaphoreType.DMA((NBR,)),
        ],
        compiler_params=pltpu.CompilerParams(
            collective_id=1, has_side_effects=True, vmem_limit_bytes=20 << 20
        ),
    )(dn, wr, ab, *kept)
    return forces, energy.reshape(ATOM)


def solution(mesh):
    both = ("dom", "face")
    placed = (
        P(None, both), P(both), P(both, None, None), P(both, None), P(both, None), P(both),
        P(), P(), P(), P(), P(), P(),
    )
    return jax.shard_map(
        per_device,
        mesh=mesh,
        in_specs=placed,
        out_specs=(P(None, both), P(both)),
        check_vma=False,
    )
```
